256 devices in a mesh: blk: 16 (over x_hi, z), rows: 16 (over y, x_lo, core).
Axes of the slice: x: 4 (x_hi: 2, x_lo: 2; x = x_hi * 2 + x_lo), y: 4, z: 8, core: 2. Of those that a mesh axis runs over, the one named last changes fastest.
Arguments:
- queries: bfloat16 [32768, 512], P(('blk', 'rows')), may hold values from -200 to 200, as said below
- keys: bfloat16 [32768, 128], P(('blk', 'rows')), may hold values from -8 to 8, as said below
- values: bfloat16 [32768, 128], P(('blk', 'rows')), may hold values from -6 to 6
- forward_out: bfloat16 [32768, 512], P(('blk', 'rows')), may hold values from -3 to 3
- grad_out: bfloat16 [32768, 512], P(('blk', 'rows')), may hold values from -192 to 192
- block_mask: int32 [2, 128, 128], replicated, may hold values from 0 to 2, as said below
Outputs:
- grad_queries: float32 [32768, 512], P(('blk', 'rows'))
- grad_keys: float32 [32768, 128], P(('blk', 'rows'))
- grad_values: float32 [32768, 128], P(('blk', 'rows'))
The draws below stay inside these ranges and needn't reach their ends.
Inputs may be any that keep to these rules, and one draw needn't show every extreme that they name: `block_mask`: for each context, entry 2 marks a pair of blocks at the same step of the series' time axis, 1 a key block attended in full, 0 none; every diagonal entry is 2. `queries`: real values. `keys`: real values.
All inputs are finite; a program needn't handle non-finite values.
Results may differ from the reference program's by a relative error of at most 0.0095.
Values may be sent and summed in bfloat16 or wider, within the bound.
No kernel may reach another device: no remote copies, remote signals or barrier semaphores. Data moves between devices by JAX's collectives and lax.ppermute only.
A program may use at most 128 MiB of HBM per device.

```python
import math
import jax
import jax.numpy as jnp
from jax import lax

HD = 128
GROUP_HEADS = 4
BLK = 128
VARS = 4
SPAN = 2048
SEQ = 16384
TOKENS = 32768
N_BLK = 16


def draw_keys(key, part):
    key_rows = jax.random.normal(jax.random.fold_in(key, 11), (TOKENS, HD), jnp.float32)
    return key_rows.astype(jnp.bfloat16)


def draw_queries(key, part):
    own_key = jax.random.fold_in(key, 29)
    query_rows = jax.random.normal(own_key, (TOKENS, GROUP_HEADS * HD), jnp.float32)
    return query_rows.astype(jnp.bfloat16)


def context_mask(key):
    block_total = SEQ // BLK
    series_len = block_total // VARS
    group_of = jax.random.randint(key, (VARS,), 0, 3)
    block_ids = jnp.arange(block_total)
    series_group = group_of[block_ids // series_len]
    time_step = block_ids % series_len
    same_group = series_group[:, None] == series_group[None, :]
    earlier = time_step[None, :] < time_step[:, None]
    same_step = time_step[None, :] == time_step[:, None]
    return jnp.where(same_group & earlier, 1, jnp.where(same_group & same_step, 2, 0)).astype(jnp.int32)


def draw_block_mask(key, part):
    key = jax.random.fold_in(key, 5)
    first = context_mask(jax.random.fold_in(key, 1))
    second = context_mask(jax.random.fold_in(key, 2))
    return jnp.stack([first, second]).astype(jnp.int32)


def shard_levels(stream_key, dims, shards, smallest, top_value):
    loudness, own = 1.0, jax.random.fold_in(stream_key, 6)
    for dim, blocks in shards:
        heights = jnp.exp(jax.random.uniform(jax.random.fold_in(own, dim), (blocks,), jnp.float32, smallest / len(shards), top_value / len(shards)))
        loudness = loudness * jnp.repeat(heights, dims[dim] // blocks).reshape([-1 if axis == dim else 1 for axis in range(len(dims))])
    return loudness


def centred(key, extent, deviation, limit, cuts=(), kind=jnp.bfloat16):
    factor_of = shard_levels(key, extent, cuts, -0.22, 0.18) if cuts else 1.0
    drawn = jax.random.normal(key, extent, jnp.float32) * deviation * factor_of
    return jnp.minimum(jnp.maximum(drawn, -limit), limit).astype(kind)


def setup_inputs(seed: int = 0) -> dict:
    arg_keys = jax.random.split(jax.random.key(seed), 7)
    queries = draw_queries(jax.random.fold_in(arg_keys[6], 71), 0)
    keys = draw_keys(jax.random.fold_in(arg_keys[6], 71), 0)
    values = centred(arg_keys[2], (TOKENS, HD), 1.0, 6.0, ((0, 256),))
    forward_out = centred(arg_keys[3], (TOKENS, GROUP_HEADS * HD), 0.5, 3.0, ((0, 256),))
    grad_out = centred(arg_keys[4], (TOKENS, GROUP_HEADS * HD), 32.0, 192.0, ((0, 256),))
    block_mask = draw_block_mask(jax.random.fold_in(arg_keys[6], 71), 0)
    return {"queries": queries, "keys": keys, "values": values, "forward_out": forward_out, "grad_out": grad_out, "block_mask": block_mask}


def one_context(queries, keys, values, forward_out, grad_out, block_mask):
    scaling = 1.0 / math.sqrt(HD)
    block_total = SEQ // BLK
    key_place = jnp.arange(SEQ) % BLK
    query_place = jnp.arange(BLK)
    key_float = keys.astype(jnp.float32)
    value_float = values.astype(jnp.float32)

    def split_rows(array):
        return array.reshape(block_total, BLK, GROUP_HEADS, HD)

    def block_step(loop_state, inputs):
        key_acc, value_acc = loop_state
        query_block, out_block, grad_block, mask_row = inputs
        query_heads = query_block.astype(jnp.float32)
        grad_heads = grad_block.astype(jnp.float32)
        out_heads = out_block.astype(jnp.float32)
        key_level = jnp.repeat(mask_row, BLK, total_repeat_length=SEQ)
        allowed = (key_level == 1)[None, :] | (key_level == 2)[None, :] & (key_place[None, :] <= query_place[:, None])
        allowed = allowed[None]
        scores = jnp.einsum('phd,jd->hpj', query_heads, key_float) * scaling
        row_top = lax.optimization_barrier(jnp.max(jnp.where(allowed, scores, -jnp.inf), axis=-1))
        row_total = lax.optimization_barrier(jnp.sum(jnp.where(allowed, jnp.exp(scores - row_top[..., None]), 0.0), axis=-1))
        log_total = row_top + jnp.log(row_total)
        attention = jnp.where(allowed, jnp.exp(scores - log_total[..., None]), 0.0)
        attention_low = lax.optimization_barrier(attention.astype(jnp.bfloat16)).astype(jnp.float32)
        row_delta = jnp.einsum('phd,phd->hp', grad_heads, out_heads)
        value_acc = value_acc + jnp.einsum('hpj,phd->jd', attention_low, grad_heads)
        grad_attention = jnp.einsum('phd,jd->hpj', grad_heads, value_float)
        grad_scores = attention * (grad_attention - row_delta[..., None])
        grad_scores = lax.optimization_barrier(grad_scores.astype(jnp.bfloat16)).astype(jnp.float32)
        grad_block_q = jnp.einsum('hpj,jd->phd', grad_scores, key_float) * scaling
        key_acc = key_acc + jnp.einsum('hpj,phd->jd', grad_scores, query_heads) * scaling
        return ((key_acc, value_acc), grad_block_q.reshape(BLK, GROUP_HEADS * HD))
    start_state = (jnp.zeros((SEQ, HD), jnp.float32), jnp.zeros((SEQ, HD), jnp.float32))
    inputs = (split_rows(queries), split_rows(forward_out), split_rows(grad_out), block_mask)
    (grad_keys, grad_values), grad_blocks = lax.scan(block_step, start_state, inputs)
    return (grad_blocks.reshape(SEQ, GROUP_HEADS * HD), grad_keys, grad_values)

def to_context(array):
    width = array.shape[-1]
    split = array.reshape(N_BLK // 2, 2, SPAN, width)
    return jnp.transpose(split, (1, 0, 2, 3)).reshape(2, SEQ, width)

def from_context(array):
    width = array.shape[-1]
    split = array.reshape(2, N_BLK // 2, SPAN, width)
    return jnp.transpose(split, (1, 0, 2, 3)).reshape(2 * SEQ, width)

def reference(queries, keys, values, forward_out, grad_out, block_mask):
    query_ctx = to_context(queries)
    key_ctx = to_context(keys)
    value_ctx = to_context(values)
    out_ctx = to_context(forward_out)
    grad_ctx = to_context(grad_out)
    query_parts = []
    key_parts = []
    value_parts = []
    for context in range(2):
        grad_q, grad_k, grad_v = one_context(query_ctx[context], key_ctx[context], value_ctx[context], out_ctx[context], grad_ctx[context], block_mask[context])
        query_parts.append(grad_q)
        key_parts.append(grad_k)
        value_parts.append(grad_v)
    return (from_context(jnp.stack(query_parts)), from_context(jnp.stack(key_parts)), from_context(jnp.stack(value_parts)))
```

```python
import functools
import math

import jax
import jax.numpy as jnp
from jax import lax
from jax.experimental import pallas as pl
from jax.experimental.pallas import tpu as pltpu
from jax.sharding import PartitionSpec as P

BLK = 128
HEADS = 4
HD = 128
COLS = HEADS * HD
N_Q = 8
N_K = 16
N_QUAD = N_K // 4
QUAD = 4 * BLK
WIDE = 2 * BLK
EXTRA = 16
D_ROWS = BLK + EXTRA
ROWS = BLK + D_ROWS
NEGATIVE = -1e30
FLOOR = -1e6
SCALING = 1.0 / math.sqrt(HD)
EXP_SCALE = SCALING * math.log2(math.e)
MIB = 1024 * 1024
F32 = jnp.float32
BF16 = jnp.bfloat16
ANY = pl.BlockSpec(memory_space=pl.ANY)
HBM = pl.BlockSpec(memory_space=pltpu.HBM)
VM = pl.BlockSpec(memory_space=pltpu.VMEM)
SM = pl.BlockSpec(memory_space=pltpu.SMEM)

NT = (((1,), (1,)), ((), ()))
NN = (((1,), (0,)), ((), ()))


def dot(a, b, dims):
    return lax.dot_general(a, b, dims, preferred_element_type=F32)


def struct(shape, dtype):
    return jax.ShapeDtypeStruct(shape, dtype)


def copy_all(pairs, sem):
    return [pltpu.make_async_copy(a, b, sem.at[n]) for n, (a, b) in enumerate(pairs)]


def pack_keys_kernel(k_ref, v_ref, kv_ref, sem):
    copies = copy_all(
        [(k_ref, kv_ref.at[:, pl.ds(0, HD)]), (v_ref, kv_ref.at[:, pl.ds(HD, HD)])], sem
    )
    for c in copies:
        c.start()
    for c in copies:
        c.wait()


def pack_queries_kernel(q_ref, do_ref, o_ref, qdo_ref, o_buf, sem):
    copies = copy_all(
        [
            (do_ref, qdo_ref.at[pl.ds(BLK, BLK)]),
            (o_ref, o_buf),
            (q_ref, qdo_ref.at[pl.ds(0, BLK)]),
        ],
        sem,
    )
    for c in copies:
        c.start()
    for c in copies[:2]:
        c.wait()
    prod = qdo_ref[BLK : 2 * BLK, :].astype(F32) * o_buf[...].astype(F32)
    delta = jnp.concatenate(
        [
            jnp.sum(prod[:, h * HD : (h + 1) * HD].T, axis=0, keepdims=True)
            for h in range(HEADS)
        ],
        axis=1,
    )
    high = delta.astype(BF16).astype(F32)
    rest = delta - high
    mid = rest.astype(BF16).astype(F32)
    low = rest - mid
    row = lax.broadcasted_iota(jnp.int32, (EXTRA, COLS), 0)
    extra = jnp.where(row == 0, high, jnp.where(row == 1, mid, jnp.where(row == 2, low, 0.0)))
    qdo_ref[2 * BLK :, :] = extra.astype(BF16)
    copies[2].wait()


def pack_keys(keys, values):
    return pl.pallas_call(
        pack_keys_kernel,
        out_shape=struct((BLK, 2 * HD), BF16),
        in_specs=[HBM] * 2,
        out_specs=VM,
        scratch_shapes=[pltpu.SemaphoreType.DMA((2,))],
        compiler_params=pltpu.CompilerParams(vmem_limit_bytes=4 * MIB),
    )(*[pltpu.with_memory_space_constraint(a, pltpu.HBM) for a in (keys, values)])


def pack_queries(queries, grad_out, forward_out):
    return pl.pallas_call(
        pack_queries_kernel,
        out_shape=struct((ROWS, COLS), BF16),
        in_specs=[HBM] * 3,
        out_specs=VM,
        scratch_shapes=[pltpu.VMEM((BLK, COLS), BF16), pltpu.SemaphoreType.DMA((3,))],
        compiler_params=pltpu.CompilerParams(vmem_limit_bytes=6 * MIB),
    )(*[pltpu.with_memory_space_constraint(a, pltpu.HBM) for a in (queries, grad_out, forward_out)])


AT_Q, AT_K, AT_G, AT_Z = 1, 1 + N_Q, 1 + N_Q + N_K, 1 + 2 * N_Q + N_K
LIMITS, TABLE, ALL, FAR, NEAR, PLAN = 0, 128, 192, 256, 288, 320
T_ROW, T_COUNT = 8, 4


def plan_kernel(place, mask_hbm, plan, mask_s, found, sem):
    copy = pltpu.make_async_copy(mask_hbm.at[place[0]], mask_s, sem)
    copy.start()
    copy.wait()

    def row(i, carry):
        at = place[AT_Q + i]
        active = jnp.int32(0)
        for quad in range(N_QUAD):
            seen = jnp.int32(0)
            for a in range(4):
                level = mask_s[at, place[AT_K + 4 * quad + a]]
                plan[LIMITS + i * N_K + 4 * quad + a] = jnp.where(
                    level == 1, -BLK, jnp.where(level == 2, 0, BLK)
                )
                seen = seen | level
            plan[TABLE + i * T_ROW + active] = quad
            active += jnp.where(seen != 0, 1, 0)
        plan[TABLE + i * T_ROW + T_COUNT] = active
        return carry

    lax.fori_loop(0, N_Q, row, 0)

    n = jnp.int32(0)
    for i in range(N_Q):
        count = plan[TABLE + i * T_ROW + T_COUNT]
        for j in range(2):
            plan[ALL + 2 + n] = plan[TABLE + i * T_ROW + 2 * j] * N_Q + i
            plan[ALL + 3 + n] = plan[TABLE + i * T_ROW + 2 * j + 1] * N_Q + i
            n += jnp.where(count >= 2 * j + 2, 2, 0)
    plan[ALL] = n // 2
    for i in range(N_Q):
        count = plan[TABLE + i * T_ROW + T_COUNT]
        plan[ALL + 2 + n] = plan[TABLE + i * T_ROW + jnp.maximum(count - 1, 0)] * N_Q + i
        n += count % 2
    plan[ALL + 1] = n

    for base, quads in ((NEAR, (0, 1)), (FAR, (2, 3))):
        counts = []
        for k, quad in enumerate(quads):
            c = jnp.int32(0)
            for i in range(N_Q):
                found[k * 16 + c] = quad * N_Q + i
                has = jnp.int32(0)
                for s in range(N_QUAD):
                    here = (plan[TABLE + i * T_ROW + s] == quad) & (
                        s < plan[TABLE + i * T_ROW + T_COUNT]
                    )
                    has = has | jnp.where(here, 1, 0)
                c += has
            counts.append(c)
        n = jnp.int32(0)
        for k in range(2):
            for j in range(N_Q // 2):
                plan[base + 2 + n] = found[k * 16 + 2 * j]
                plan[base + 3 + n] = found[k * 16 + 2 * j + 1]
                n += jnp.where(counts[k] >= 2 * j + 2, 2, 0)
        plan[base] = n // 2
        for k in range(2):
            plan[base + 2 + n] = found[k * 16 + jnp.maximum(counts[k] - 1, 0)]
            n += counts[k] % 2
        plan[base + 1] = n


def run_plan(place, mask):
    return pl.pallas_call(
        plan_kernel,
        out_shape=struct((PLAN,), jnp.int32),
        in_specs=[SM, ANY],
        out_specs=SM,
        scratch_shapes=[
            pltpu.SMEM((BLK, BLK), jnp.int32),
            pltpu.SMEM((32,), jnp.int32),
            pltpu.SemaphoreType.DMA(()),
        ],
        compiler_params=pltpu.CompilerParams(vmem_limit_bytes=4 * MIB),
    )(place, mask)


def queries_of(near, far, i):
    at = (i % 4) * ROWS
    return (near, far)[i // 4][at : at + BLK]


def grads_of(near, far, i):
    at = (i % 4) * ROWS + BLK
    return (near, far)[i // 4][at : at + D_ROWS]


def fill_quads(kvs, cols, buf):
    for quad in range(N_QUAD):
        for odd in range(2):
            at = slice((quad % 2) * WIDE, (quad % 2 + 1) * WIDE)
            buf[quad, odd * WIDE : (odd + 1) * WIDE] = kvs[2 * (quad // 2) + odd][at, cols]


def heads(ref, i, hp):
    c = hp * WIDE
    return jnp.concatenate([ref[i, :BLK, c : c + HD], ref[i, :BLK, c + HD : c + 2 * HD]], axis=0)


def scores_kernel(
    place, plan, near, far, kv0, kv1, kv2, kv3,
    e_hbm, stats_hbm,
    qs, ks, sc, ebuf, mx, lacc, st, count, e_sem, st_sem,
):
    count[0] = 0
    fill_quads((kv0, kv1, kv2, kv3), slice(0, HD), ks)
    for i in range(N_Q):
        qs[i] = queries_of(near, far, i)
    diff = (
        lax.broadcasted_iota(jnp.int32, (BLK, WIDE), 1) % BLK
        - lax.broadcasted_iota(jnp.int32, (BLK, WIDE), 0)
    )

    def out_copy(slot, unit):
        return pltpu.make_async_copy(ebuf.at[slot], e_hbm.at[unit], e_sem.at[slot])

    def query_block(i, carry):
        base = TABLE + i * T_ROW
        active = plan[base + T_COUNT]
        mx[...] = jnp.full(mx.shape, NEGATIVE, F32)
        lacc[...] = jnp.zeros(lacc.shape, F32)

        def score_quads(quads):
            for hp in range(2):
                cols = slice(hp * WIDE, (hp + 1) * WIDE)
                rhs = heads(qs, i, hp)
                best = mx[:, cols]
                for quad in quads:
                    s = dot(ks[quad], rhs, NT)
                    for a in range(4):
                        at = slice(a * BLK, (a + 1) * BLK)
                        limit = plan[LIMITS + i * N_K + 4 * quad + a]
                        part = jnp.where(diff >= limit, s[at], NEGATIVE)
                        sc[quad, at, cols] = part
                        best = jnp.maximum(
                            best, jnp.max(part.reshape(BLK // 8, 8, WIDE), axis=0)
                        )
                mx[:, cols] = best

        def score_pair(n, carry):
            score_quads([plan[base + 2 * n], plan[base + 2 * n + 1]])
            return carry

        lax.fori_loop(0, active // 2, score_pair, 0)

        @pl.when(active % 2 == 1)
        def _():
            score_quads([plan[base + active - 1]])

        m = jnp.maximum(jnp.max(mx[...], axis=0, keepdims=True), FLOOR)

        def exp_quad(k, carry):
            quad = plan[base + k]
            n = count[0]
            slot = n % 2

            @pl.when(n >= 2)
            def _():
                out_copy(slot, 0).wait()

            for hp in range(2):
                cols = slice(hp * WIDE, (hp + 1) * WIDE)
                e = jnp.exp2((sc[quad, :, cols] - m[:, cols]) * EXP_SCALE)
                lacc[:, cols] += jnp.sum(e.reshape(QUAD // 8, 8, WIDE), axis=0)
                ebuf[slot, :, cols] = e.astype(BF16)
            out_copy(slot, quad * N_Q + i).start()
            count[0] = n + 1
            return carry

        lax.fori_loop(0, active, exp_quad, 0)
        g = place[AT_G + i]
        st[pl.ds(g, 1), :] = m
        st[pl.ds(N_Q + g, 1), :] = jnp.sum(lacc[...], axis=0, keepdims=True)
        return carry

    lax.fori_loop(0, N_Q, query_block, 0)

    st_copies = copy_all([(st, stats_hbm.at[g]) for g in range(N_Q)], st_sem)
    for c in st_copies:
        c.start()
    for c in st_copies:
        c.wait()
    for slot_no in range(2):

        @pl.when(count[0] > slot_no)
        def _():
            out_copy(slot_no, 0).wait()


def run_scores(place, plan, near, far, kvs):
    return pl.pallas_call(
        scores_kernel,
        out_shape=[
            pltpu.HBM((N_QUAD * N_Q, QUAD, COLS), BF16),
            pltpu.HBM((N_Q, 2 * N_Q, COLS), F32),
        ],
        in_specs=[SM, SM] + [VM] * 6,
        out_specs=[HBM, HBM],
        scratch_shapes=[
            pltpu.VMEM((N_Q, BLK, COLS), BF16),
            pltpu.VMEM((N_QUAD, QUAD, HD), BF16),
            pltpu.VMEM((N_QUAD, QUAD, COLS), F32),
            pltpu.VMEM((2, QUAD, COLS), BF16),
            pltpu.VMEM((8, COLS), F32),
            pltpu.VMEM((8, COLS), F32),
            pltpu.VMEM((2 * N_Q, COLS), F32),
            pltpu.SMEM((1,), jnp.int32),
            pltpu.SemaphoreType.DMA((2,)),
            pltpu.SemaphoreType.DMA((N_Q,)),
        ],
        compiler_params=pltpu.CompilerParams(vmem_limit_bytes=14 * MIB),
    )(place, plan, near, far, *kvs)


DEPTH = 4


def loop_units(plan, base, visit):
    pairs, total = plan[base], plan[base + 1]

    def pair(n, carry):
        visit(2 * n, 2)
        return carry

    def single(n, carry):
        visit(n, 1)
        return carry

    lax.fori_loop(0, pairs, pair, 0)
    lax.fori_loop(2 * pairs, total, single, 0)


def prefetch(plan, base, copies, first, number):
    total = plan[base + 1]
    for k in range(number):

        @pl.when(first + k + 2 < total)
        def _():
            for c in copies(first + k + 2):
                c.start()

    for k in range(number):
        for c in copies(first + k):
            c.wait()


def start_first(plan, base, copies):
    for n in range(2):

        @pl.when(n < plan[base + 1])
        def _():
            for c in copies(n):
                c.start()


def parts_kernel(
    place, plan, near, far, kv0, kv1, kv2, kv3, e_hbm,
    u_hbm, dq_hbm,
    ds, ks, vs, kts, ebuf, ubuf, dqs, dq_low, e_sem, u_sem, dq_sem,
):
    def in_copies(n):
        unit, at = plan[ALL + 2 + n], n % DEPTH
        return (pltpu.make_async_copy(e_hbm.at[unit], ebuf.at[at], e_sem.at[at]),)

    def out_copy(n, unit):
        at = n % DEPTH
        return pltpu.make_async_copy(ubuf.at[at], u_hbm.at[unit], u_sem.at[at])

    start_first(plan, ALL, in_copies)
    kvs = (kv0, kv1, kv2, kv3)
    fill_quads(kvs, slice(0, HD), ks)
    fill_quads(kvs, slice(HD, 2 * HD), vs)
    for i in range(N_Q):
        ds[i] = grads_of(near, far, i)
    dqs[...] = jnp.zeros(dqs.shape, F32)
    for quad in range(N_QUAD):
        kts[quad] = ks[quad].T

    def visit(first, number):
        units = [plan[ALL + 2 + first + k] for k in range(number)]
        i = units[0] % N_Q
        for k in range(number):

            @pl.when(first + k >= DEPTH)
            def _():
                out_copy(first + k, 0).wait()

        prefetch(plan, ALL, in_copies, first, number)
        extra = ds[i, BLK:, :].astype(F32)
        delta = extra[0:1] + extra[1:2] + extra[2:3]
        for hp in range(2):
            cols = slice(hp * WIDE, (hp + 1) * WIDE)
            rhs = heads(ds, i, hp)
            dq = dqs[i, :, cols]
            for k in range(number):
                quad, at = units[k] // N_Q, (first + k) % DEPTH
                da = dot(vs[quad], rhs, NT)
                e = ebuf[at, :, cols].astype(F32)
                u = (e * (da - delta[:, cols])).astype(BF16)
                ubuf[at, :, cols] = u
                dq += dot(kts[quad], u, NN)
            dqs[i, :, cols] = dq
        for k in range(number):
            out_copy(first + k, units[k]).start()

    loop_units(plan, ALL, visit)
    dq_copies = copy_all([(dq_low.at[i], dq_hbm.at[place[AT_G + i]]) for i in range(N_Q)], dq_sem)
    for i in range(N_Q):
        dq_low[i] = dqs[i].astype(BF16)
        dq_copies[i].start()
    for c in dq_copies:
        c.wait()
    for n in range(DEPTH):

        @pl.when(n < plan[ALL + 1])
        def _():
            out_copy(n, 0).wait()


def run_parts(place, plan, near, far, kvs, e):
    dma = pltpu.SemaphoreType.DMA
    return pl.pallas_call(
        parts_kernel,
        out_shape=[
            pltpu.HBM((N_QUAD * N_Q, QUAD, COLS), BF16),
            pltpu.HBM((N_Q, HD, COLS), BF16),
        ],
        in_specs=[SM, SM] + [VM] * 6 + [HBM],
        out_specs=[HBM, HBM],
        scratch_shapes=[
            pltpu.VMEM((N_Q, D_ROWS, COLS), BF16),
            pltpu.VMEM((N_QUAD, QUAD, HD), BF16),
            pltpu.VMEM((N_QUAD, QUAD, HD), BF16),
            pltpu.VMEM((N_QUAD, HD, QUAD), BF16),
            pltpu.VMEM((DEPTH, QUAD, COLS), BF16),
            pltpu.VMEM((DEPTH, QUAD, COLS), BF16),
            pltpu.VMEM((N_Q, HD, COLS), F32),
            pltpu.VMEM((N_Q, HD, COLS), BF16),
            dma((DEPTH,)),
            dma((DEPTH,)),
            dma((N_Q,)),
        ],
        compiler_params=pltpu.CompilerParams(vmem_limit_bytes=18 * MIB),
    )(place, plan, near, far, *kvs, e)


def row_weights(place, stats, near, far, ws, wq, wdo):
    ms = [stats[j, :N_Q, :] for j in range(N_Q)]
    top = functools.reduce(jnp.maximum, ms)
    tot = sum(stats[j, N_Q:, :] * jnp.exp2((ms[j] - top) * EXP_SCALE) for j in range(N_Q))
    ws[...] = jnp.exp2((stats[place[AT_G], :N_Q, :] - top) * EXP_SCALE) / tot
    rows = []
    for i in range(N_Q):
        w = ws[pl.ds(place[AT_G + i], 1), :]
        rows += [w[:, h * BLK : (h + 1) * BLK] for h in range(HEADS)]
    rows.append(jnp.zeros((BLK - len(rows), BLK), F32))
    cols = jnp.concatenate(rows, axis=0).T
    for i in range(N_Q):
        q = queries_of(near, far, i)
        do = grads_of(near, far, i)
        for h in range(HEADS):
            w = cols[:, i * HEADS + h : i * HEADS + h + 1]
            at = slice(h * BLK, (h + 1) * BLK)
            c = slice(h * HD, (h + 1) * HD)
            wq[i, at, :] = (q[:, c].astype(F32) * w).astype(BF16)
            wdo[i, at, :] = (do[:BLK, c].astype(F32) * w).astype(BF16)


def sum_keys(plan, base, first_quad, rows, wq, wdo, e_hbm, u_hbm, acc, bufs, between=None):
    ebuf, ubuf, e_sem, u_sem = bufs
    size = acc.shape[1]

    def in_copies(n):
        unit, at = plan[base + 2 + n], n % DEPTH
        return [
            pltpu.make_async_copy(
                hbm.at[unit, pl.ds(rows, size)], buf.at[at, pl.ds(0, size)], sem.at[at]
            )
            for hbm, buf, sem in ((e_hbm, ebuf, e_sem), (u_hbm, ubuf, u_sem))
        ]

    start_first(plan, base, in_copies)
    acc[...] = jnp.zeros(acc.shape, F32)
    if between is not None:
        between()

    def visit(first, number):
        units = [plan[base + 2 + first + k] for k in range(number)]
        quad = units[0] // N_Q - first_quad
        prefetch(plan, base, in_copies, first, number)
        for buf, w, cols in ((ubuf, wq, slice(0, HD)), (ebuf, wdo, slice(HD, 2 * HD))):
            total = acc[quad, :, cols]
            for k in range(number):
                total += dot(buf[(first + k) % DEPTH, :size], w[units[k] % N_Q], NN)
            acc[quad, :, cols] = total

    loop_units(plan, base, visit)


def far_kernel(
    place, plan, stats, near, far, e_hbm, u_hbm,
    out1, out2, out3, wq_hbm, wdo_hbm,
    ws, wq, wdo, acc, acc_odd, w_sem, *bufs,
):
    w_copies = copy_all([(wq, wq_hbm), (wdo, wdo_hbm)], w_sem)

    def weigh():
        row_weights(place, stats, near, far, ws, wq, wdo)
        for c in w_copies:
            c.start()

    sum_keys(plan, FAR, 2, 0, wq, wdo, e_hbm, u_hbm, acc, bufs, weigh)
    sum_keys(plan, NEAR, 0, WIDE, wq, wdo, e_hbm, u_hbm, acc_odd, bufs)
    for quad in range(2):
        at = slice(quad * WIDE, (quad + 1) * WIDE)
        out1[at, :] = acc_odd[quad].astype(BF16)
        out2[at, :] = acc[quad, :WIDE].astype(BF16)
        out3[at, :] = acc[quad, WIDE:].astype(BF16)
    for c in w_copies:
        c.wait()


def own_kernel(plan, wq_hbm, wdo_hbm, e_hbm, u_hbm, out, wq, wdo, acc, w_sem, *bufs):
    w_copies = copy_all([(wq_hbm, wq), (wdo_hbm, wdo)], w_sem)
    for c in w_copies:
        c.start()

    def wait():
        for c in w_copies:
            c.wait()

    sum_keys(plan, NEAR, 0, 0, wq, wdo, e_hbm, u_hbm, acc, bufs, wait)
    for quad in range(2):
        out[quad * WIDE : (quad + 1) * WIDE, :] = acc[quad]


def keys_bufs(rows):
    return [
        pltpu.VMEM((DEPTH, rows, COLS), BF16),
        pltpu.VMEM((DEPTH, rows, COLS), BF16),
        pltpu.SemaphoreType.DMA((DEPTH,)),
        pltpu.SemaphoreType.DMA((DEPTH,)),
    ]


def run_far(place, plan, stats, near, far, e, u):
    return pl.pallas_call(
        far_kernel,
        out_shape=[struct((QUAD, 2 * HD), BF16)] * 3 + [pltpu.HBM((N_Q, COLS, HD), BF16)] * 2,
        in_specs=[SM, SM] + [VM] * 3 + [HBM, HBM],
        out_specs=[VM] * 3 + [HBM] * 2,
        scratch_shapes=[
            pltpu.VMEM((N_Q, COLS), F32),
            pltpu.VMEM((N_Q, COLS, HD), BF16),
            pltpu.VMEM((N_Q, COLS, HD), BF16),
            pltpu.VMEM((2, QUAD, 2 * HD), F32),
            pltpu.VMEM((2, WIDE, 2 * HD), F32),
            pltpu.SemaphoreType.DMA((2,)),
        ]
        + keys_bufs(QUAD),
        compiler_params=pltpu.CompilerParams(vmem_limit_bytes=18 * MIB),
    )(place, plan, stats, near, far, e, u)


def run_own(plan, wq, wdo, e, u):
    return pl.pallas_call(
        own_kernel,
        out_shape=struct((QUAD, 2 * HD), F32),
        in_specs=[SM] + [HBM] * 4,
        out_specs=VM,
        scratch_shapes=[
            pltpu.VMEM((N_Q, COLS, HD), BF16),
            pltpu.VMEM((N_Q, COLS, HD), BF16),
            pltpu.VMEM((2, WIDE, 2 * HD), F32),
            pltpu.SemaphoreType.DMA((2,)),
        ]
        + keys_bufs(WIDE),
        compiler_params=pltpu.CompilerParams(vmem_limit_bytes=12 * MIB),
    )(plan, wq, wdo, e, u)


def sum_kernel(place, own, a, b, c, out):
    for d in range(4):
        at = slice(d * BLK, (d + 1) * BLK)
        total = own[at] + a[at].astype(F32) + b[at].astype(F32) + c[at].astype(F32)
        out[place[AT_Z + d]] = total.astype(BF16)


def run_sum(place, own, a, b, c):
    return pl.pallas_call(
        sum_kernel,
        out_shape=struct((4, BLK, 2 * HD), BF16),
        in_specs=[SM] + [VM] * 4,
        out_specs=VM,
        compiler_params=pltpu.CompilerParams(vmem_limit_bytes=6 * MIB),
    )(place, own, a, b, c)


def queries_kernel(place, parts, stats, out):
    own = place[AT_G]
    ms = [stats[j, pl.ds(own, 1), :] for j in range(N_Q)]
    ls = [stats[j, pl.ds(N_Q + own, 1), :] for j in range(N_Q)]
    top = functools.reduce(jnp.maximum, ms)
    es = [jnp.exp2((m - top) * EXP_SCALE) for m in ms]
    tot = sum(l * e for l, e in zip(ls, es))
    for h in range(HEADS):
        at = slice(h * HD, (h + 1) * HD)
        total = sum(parts[j, :, at].astype(F32) * es[j][:, at] for j in range(N_Q))
        out[:, at] = (total * (SCALING / tot[:, at])).T


def run_queries(place, parts, stats):
    return pl.pallas_call(
        queries_kernel,
        out_shape=struct((BLK, COLS), F32),
        in_specs=[SM, VM, VM],
        out_specs=VM,
        compiler_params=pltpu.CompilerParams(vmem_limit_bytes=6 * MIB),
    )(place, parts, stats)


def exchange(x, dx=0, dz=0, dy=0, dc=0):
    perm = []
    for b in range(16):
        for r in range(16):
            px = (b // 8) * 2 + (r // 2) % 2
            pz, py, pc = b % 8, r // 4, r % 2
            px, pz, py, pc = px ^ dx, pz ^ (2 * dz), py ^ dy, pc ^ dc
            other = (px // 2) * 8 + pz, py * 4 + (px % 2) * 2 + pc
            perm.append((b * 16 + r, other[0] * 16 + other[1]))
    return lax.ppermute(x, ("blk", "rows"), perm)


Q_GROUPS = [[r for r in range(16) if (r // 2) % 2 == lo] for lo in range(2)]
Z_GROUPS = [[8 * hi + 2 * z + par for z in range(4)] for hi in range(2) for par in range(2)]


def to_group(x):
    return lax.all_to_all(x, "rows", 0, 0, axis_index_groups=Q_GROUPS, tiled=True)


def per_device(queries, keys, values, forward_out, grad_out, block_mask):
    b, r = lax.axis_index("blk"), lax.axis_index("rows")
    x = ((b >> 3) << 1) | ((r >> 1) & 1)
    zz, y, core = (b >> 1) & 3, r >> 2, r & 1
    slot_q = jnp.arange(N_Q)
    yq, cq = y ^ (slot_q & 3), core ^ (slot_q >> 2)
    q_blocks = ((b >> 1) << 4) + (yq << 2) + ((x & 1) << 1) + cq
    slot_k = jnp.arange(N_K)
    quad, a = slot_k >> 2, slot_k & 3
    xk = x ^ (((quad >> 1) << 1) | (a >> 1))
    zk = zz ^ (((quad & 1) << 1) | (a & 1))
    k_blocks = ((((xk >> 1) << 2) + zk) << 4) + (y << 2) + ((xk & 1) << 1) + core
    place = jnp.concatenate(
        [(b & 1)[None], q_blocks, k_blocks, (yq << 1) + cq, zz ^ jnp.arange(4)]
    ).astype(jnp.int32)

    kv = pack_keys(keys, values)
    qdo = pack_queries(queries, grad_out, forward_out)

    kv_z = jnp.concatenate([kv] + [exchange(kv, dz=d) for d in (1, 2, 3)], axis=0)
    kvs = [kv_z] + [exchange(kv_z, dx=d) for d in (1, 2, 3)]
    others = [exchange(qdo, dy=d) for d in (1, 2, 3)]
    plan = run_plan(place, block_mask)
    *others, k1, k2, k3, plan = lax.optimization_barrier((*others, *kvs[1:], plan))
    kvs = [kv_z, k1, k2, k3]
    near = jnp.concatenate([qdo, *others], axis=0)
    far = exchange(near, dc=1)

    e, stat = run_scores(place, plan, near, far, kvs)
    e = pltpu.with_memory_space_constraint(e, pltpu.HBM)
    stats = to_group(stat)
    u, dq = run_parts(place, plan, near, far, kvs, e)
    u = pltpu.with_memory_space_constraint(u, pltpu.HBM)
    *remote, wq, wdo = run_far(place, plan, stats, near, far, e, u)
    wq, wdo = [pltpu.with_memory_space_constraint(w, pltpu.HBM) for w in (wq, wdo)]
    got1, got2, got3 = [exchange(f, dx=d) for d, f in zip((1, 2, 3), remote)]
    own = run_own(plan, wq, wdo, e, u)
    got1, dq = lax.optimization_barrier((got1, dq))
    dq_parts = to_group(dq)
    summed = run_sum(place, own, got1, got2, got3)
    back = lax.all_to_all(summed, "blk", 0, 0, axis_index_groups=Z_GROUPS, tiled=True)
    grad_queries = run_queries(place, dq_parts, stats)
    total = jnp.sum(back.astype(F32), axis=0)
    return grad_queries, total[:, :HD] * SCALING, total[:, HD:]


def solution(mesh):
    spec = P(("blk", "rows"), None)
    return jax.shard_map(
        per_device,
        mesh=mesh,
        in_specs=(spec, spec, spec, spec, spec, P()),
        out_specs=(spec, spec, spec),
        check_vma=False,
    )
```

```python
import functools
import math

import jax
import jax.numpy as jnp
from jax import lax
from jax.experimental import pallas as pl
from jax.experimental.pallas import tpu as pltpu
from jax.sharding import PartitionSpec as P

BLK = 128
HEADS = 4
HD = 128
COLS = HEADS * HD
N_Q = 8
N_K = 16
N_QUAD = N_K // 4
QUAD = 4 * BLK
WIDE = 2 * BLK
EXTRA = 16
D_ROWS = BLK + EXTRA
ROWS = BLK + D_ROWS
NEGATIVE = -1e30
FLOOR = -1e6
SCALING = 1.0 / math.sqrt(HD)
EXP_SCALE = SCALING * math.log2(math.e)
MIB = 1024 * 1024
F32 = jnp.float32
BF16 = jnp.bfloat16
ANY = pl.BlockSpec(memory_space=pl.ANY)
HBM = pl.BlockSpec(memory_space=pltpu.HBM)
VM = pl.BlockSpec(memory_space=pltpu.VMEM)
SM = pl.BlockSpec(memory_space=pltpu.SMEM)

NT = (((1,), (1,)), ((), ()))
NN = (((1,), (0,)), ((), ()))


def dot(a, b, dims):
    return lax.dot_general(a, b, dims, preferred_element_type=F32)


def struct(shape, dtype):
    return jax.ShapeDtypeStruct(shape, dtype)


def copy_all(pairs, sem):
    return [pltpu.make_async_copy(a, b, sem.at[n]) for n, (a, b) in enumerate(pairs)]


def pack_keys_kernel(k_ref, v_ref, kv_ref, sem):
    copies = copy_all(
        [(k_ref, kv_ref.at[:, pl.ds(0, HD)]), (v_ref, kv_ref.at[:, pl.ds(HD, HD)])], sem
    )
    for c in copies:
        c.start()
    for c in copies:
        c.wait()


def pack_queries_kernel(q_ref, do_ref, o_ref, qdo_ref, o_buf, sem):
    copies = copy_all(
        [
            (do_ref, qdo_ref.at[pl.ds(BLK, BLK)]),
            (o_ref, o_buf),
            (q_ref, qdo_ref.at[pl.ds(0, BLK)]),
        ],
        sem,
    )
    for c in copies:
        c.start()
    for c in copies[:2]:
        c.wait()
    prod = qdo_ref[BLK : 2 * BLK, :].astype(F32) * o_buf[...].astype(F32)
    delta = jnp.concatenate(
        [
            jnp.sum(prod[:, h * HD : (h + 1) * HD].T, axis=0, keepdims=True)
            for h in range(HEADS)
        ],
        axis=1,
    )
    high = delta.astype(BF16).astype(F32)
    rest = delta - high
    mid = rest.astype(BF16).astype(F32)
    low = rest - mid
    row = lax.broadcasted_iota(jnp.int32, (EXTRA, COLS), 0)
    extra = jnp.where(row == 0, high, jnp.where(row == 1, mid, jnp.where(row == 2, low, 0.0)))
    qdo_ref[2 * BLK :, :] = extra.astype(BF16)
    copies[2].wait()


def pack_keys(keys, values):
    return pl.pallas_call(
        pack_keys_kernel,
        out_shape=struct((BLK, 2 * HD), BF16),
        in_specs=[HBM] * 2,
        out_specs=VM,
        scratch_shapes=[pltpu.SemaphoreType.DMA((2,))],
        compiler_params=pltpu.CompilerParams(vmem_limit_bytes=4 * MIB),
    )(*[pltpu.with_memory_space_constraint(a, pltpu.HBM) for a in (keys, values)])


def pack_queries(queries, grad_out, forward_out):
    return pl.pallas_call(
        pack_queries_kernel,
        out_shape=struct((ROWS, COLS), BF16),
        in_specs=[HBM] * 3,
        out_specs=VM,
        scratch_shapes=[pltpu.VMEM((BLK, COLS), BF16), pltpu.SemaphoreType.DMA((3,))],
        compiler_params=pltpu.CompilerParams(vmem_limit_bytes=6 * MIB),
    )(*[pltpu.with_memory_space_constraint(a, pltpu.HBM) for a in (queries, grad_out, forward_out)])


AT_Q, AT_K, AT_G, AT_Z = 1, 1 + N_Q, 1 + N_Q + N_K, 1 + 2 * N_Q + N_K
LIMITS, TABLE, ALL, FAR, NEAR, PLAN = 0, 128, 192, 256, 288, 320
T_ROW, T_COUNT = 8, 4


def plan_kernel(place, mask_hbm, plan, mask_s, found, sem):
    copy = pltpu.make_async_copy(mask_hbm.at[place[0]], mask_s, sem)
    copy.start()
    copy.wait()

    def row(i, carry):
        at = place[AT_Q + i]
        active = jnp.int32(0)
        for quad in range(N_QUAD):
            seen = jnp.int32(0)
            for a in range(4):
                level = mask_s[at, place[AT_K + 4 * quad + a]]
                plan[LIMITS + i * N_K + 4 * quad + a] = jnp.where(
                    level == 1, -BLK, jnp.where(level == 2, 0, BLK)
                )
                seen = seen | level
            plan[TABLE + i * T_ROW + active] = quad
            active += jnp.where(seen != 0, 1, 0)
        plan[TABLE + i * T_ROW + T_COUNT] = active
        return carry

    lax.fori_loop(0, N_Q, row, 0)

    n = jnp.int32(0)
    for i in range(N_Q):
        count = plan[TABLE + i * T_ROW + T_COUNT]
        for j in range(2):
            plan[ALL + 2 + n] = plan[TABLE + i * T_ROW + 2 * j] * N_Q + i
            plan[ALL + 3 + n] = plan[TABLE + i * T_ROW + 2 * j + 1] * N_Q + i
            n += jnp.where(count >= 2 * j + 2, 2, 0)
    plan[ALL] = n // 2
    for i in range(N_Q):
        count = plan[TABLE + i * T_ROW + T_COUNT]
        plan[ALL + 2 + n] = plan[TABLE + i * T_ROW + jnp.maximum(count - 1, 0)] * N_Q + i
        n += count % 2
    plan[ALL + 1] = n

    for base, quads in ((NEAR, (0, 1)), (FAR, (2, 3))):
        counts = []
        for k, quad in enumerate(quads):
            c = jnp.int32(0)
            for i in range(N_Q):
                found[k * 16 + c] = quad * N_Q + i
                has = jnp.int32(0)
                for s in range(N_QUAD):
                    here = (plan[TABLE + i * T_ROW + s] == quad) & (
                        s < plan[TABLE + i * T_ROW + T_COUNT]
                    )
                    has = has | jnp.where(here, 1, 0)
                c += has
            counts.append(c)
        n = jnp.int32(0)
        for k in range(2):
            for j in range(N_Q // 2):
                plan[base + 2 + n] = found[k * 16 + 2 * j]
                plan[base + 3 + n] = found[k * 16 + 2 * j + 1]
                n += jnp.where(counts[k] >= 2 * j + 2, 2, 0)
        plan[base] = n // 2
        for k in range(2):
            plan[base + 2 + n] = found[k * 16 + jnp.maximum(counts[k] - 1, 0)]
            n += counts[k] % 2
        plan[base + 1] = n


def run_plan(place, mask):
    return pl.pallas_call(
        plan_kernel,
        out_shape=struct((PLAN,), jnp.int32),
        in_specs=[SM, HBM],
        out_specs=SM,
        scratch_shapes=[
            pltpu.SMEM((BLK, BLK), jnp.int32),
            pltpu.SMEM((32,), jnp.int32),
            pltpu.SemaphoreType.DMA(()),
        ],
        compiler_params=pltpu.CompilerParams(vmem_limit_bytes=4 * MIB),
    )(place, mask)


def queries_of(near, far, i):
    at = (i % 4) * ROWS
    return (near, far)[i // 4][at : at + BLK]


def grads_of(near, far, i):
    at = (i % 4) * ROWS + BLK
    return (near, far)[i // 4][at : at + D_ROWS]


def fill_quads(kvs, cols, buf):
    for quad in range(N_QUAD):
        for odd in range(2):
            at = slice((quad % 2) * WIDE, (quad % 2 + 1) * WIDE)
            buf[quad, odd * WIDE : (odd + 1) * WIDE] = kvs[2 * (quad // 2) + odd][at, cols]


def heads(ref, i, hp):
    c = hp * WIDE
    return jnp.concatenate([ref[i, :BLK, c : c + HD], ref[i, :BLK, c + HD : c + 2 * HD]], axis=0)


E_SLOTS = 4


def scores_kernel(
    place, plan, near, far, kv0, kv1, kv2, kv3,
    e_hbm, stats_hbm,
    qs, ks, sc, ebuf, mx, lacc, st, count, e_sem, st_sem,
):
    count[0] = 0
    fill_quads((kv0, kv1, kv2, kv3), slice(0, HD), ks)
    for i in range(N_Q):
        qs[i] = queries_of(near, far, i)
    diff = (
        lax.broadcasted_iota(jnp.int32, (BLK, WIDE), 1) % BLK
        - lax.broadcasted_iota(jnp.int32, (BLK, WIDE), 0)
    )

    def out_copy(slot, unit):
        return pltpu.make_async_copy(ebuf.at[slot], e_hbm.at[unit], e_sem.at[slot])

    def query_block(i, carry):
        base = TABLE + i * T_ROW
        active = plan[base + T_COUNT]
        mx[...] = jnp.full(mx.shape, NEGATIVE, F32)
        lacc[...] = jnp.zeros(lacc.shape, F32)

        def score_quads(quads):
            for hp in range(2):
                cols = slice(hp * WIDE, (hp + 1) * WIDE)
                rhs = heads(qs, i, hp)
                best = mx[:, cols]
                for quad in quads:
                    s = dot(ks[quad], rhs, NT)
                    for a in range(4):
                        at = slice(a * BLK, (a + 1) * BLK)
                        limit = plan[LIMITS + i * N_K + 4 * quad + a]
                        part = jnp.where(diff >= limit, s[at], NEGATIVE)
                        sc[quad, at, cols] = part
                        best = jnp.maximum(
                            best, jnp.max(part.reshape(BLK // 8, 8, WIDE), axis=0)
                        )
                mx[:, cols] = best

        def score_pair(n, carry):
            score_quads([plan[base + 2 * n], plan[base + 2 * n + 1]])
            return carry

        lax.fori_loop(0, active // 2, score_pair, 0)

        @pl.when(active % 2 == 1)
        def _():
            score_quads([plan[base + active - 1]])

        m = jnp.maximum(jnp.max(mx[...], axis=0, keepdims=True), FLOOR)

        def exp_quad(k, carry):
            quad = plan[base + k]
            n = count[0]
            slot = n % E_SLOTS

            @pl.when(n >= E_SLOTS)
            def _():
                out_copy(slot, 0).wait()

            for hp in range(2):
                cols = slice(hp * WIDE, (hp + 1) * WIDE)
                e = jnp.exp2((sc[quad, :, cols] - m[:, cols]) * EXP_SCALE)
                lacc[:, cols] += jnp.sum(e.reshape(QUAD // 8, 8, WIDE), axis=0)
                ebuf[slot, :, cols] = e.astype(BF16)
            out_copy(slot, quad * N_Q + i).start()
            count[0] = n + 1
            return carry

        lax.fori_loop(0, active, exp_quad, 0)
        g = place[AT_G + i]
        st[pl.ds(g, 1), :] = m
        st[pl.ds(N_Q + g, 1), :] = jnp.sum(lacc[...], axis=0, keepdims=True)
        return carry

    lax.fori_loop(0, N_Q, query_block, 0)

    st_copies = copy_all([(st, stats_hbm.at[g]) for g in range(N_Q)], st_sem)
    for c in st_copies:
        c.start()
    for c in st_copies:
        c.wait()
    for slot_no in range(E_SLOTS):

        @pl.when(count[0] > slot_no)
        def _():
            out_copy(slot_no, 0).wait()


def run_scores(place, plan, near, far, kvs):
    return pl.pallas_call(
        scores_kernel,
        out_shape=[
            pltpu.HBM((N_QUAD * N_Q, QUAD, COLS), BF16),
            pltpu.HBM((N_Q, 2 * N_Q, COLS), F32),
        ],
        in_specs=[SM, SM] + [VM] * 6,
        out_specs=[HBM, HBM],
        scratch_shapes=[
            pltpu.VMEM((N_Q, BLK, COLS), BF16),
            pltpu.VMEM((N_QUAD, QUAD, HD), BF16),
            pltpu.VMEM((N_QUAD, QUAD, COLS), F32),
            pltpu.VMEM((E_SLOTS, QUAD, COLS), BF16),
            pltpu.VMEM((8, COLS), F32),
            pltpu.VMEM((8, COLS), F32),
            pltpu.VMEM((2 * N_Q, COLS), F32),
            pltpu.SMEM((1,), jnp.int32),
            pltpu.SemaphoreType.DMA((E_SLOTS,)),
            pltpu.SemaphoreType.DMA((N_Q,)),
        ],
        compiler_params=pltpu.CompilerParams(vmem_limit_bytes=14 * MIB),
    )(place, plan, near, far, *kvs)


DEPTH = 4


def loop_units(plan, base, visit):
    pairs, total = plan[base], plan[base + 1]

    def pair(n, carry):
        visit(2 * n, 2)
        return carry

    def single(n, carry):
        visit(n, 1)
        return carry

    lax.fori_loop(0, pairs, pair, 0)
    lax.fori_loop(2 * pairs, total, single, 0)


def prefetch(plan, base, copies, first, number):
    total = plan[base + 1]
    for k in range(number):

        @pl.when(first + k + 2 < total)
        def _():
            for c in copies(first + k + 2):
                c.start()

    for k in range(number):
        for c in copies(first + k):
            c.wait()


def start_first(plan, base, copies):
    for n in range(2):

        @pl.when(n < plan[base + 1])
        def _():
            for c in copies(n):
                c.start()


def parts_kernel(
    place, plan, near, far, kv0, kv1, kv2, kv3, e_hbm,
    u_hbm, dq_hbm,
    ds, ks, vs, kts, ebuf, ubuf, dqs, dq_low, e_sem, u_sem, dq_sem,
):
    def in_copies(n):
        unit, at = plan[ALL + 2 + n], n % DEPTH
        return (pltpu.make_async_copy(e_hbm.at[unit], ebuf.at[at], e_sem.at[at]),)

    def out_copy(n, unit):
        at = n % DEPTH
        return pltpu.make_async_copy(ubuf.at[at], u_hbm.at[unit], u_sem.at[at])

    start_first(plan, ALL, in_copies)
    kvs = (kv0, kv1, kv2, kv3)
    fill_quads(kvs, slice(0, HD), ks)
    fill_quads(kvs, slice(HD, 2 * HD), vs)
    for i in range(N_Q):
        ds[i] = grads_of(near, far, i)
    dqs[...] = jnp.zeros(dqs.shape, F32)
    for quad in range(N_QUAD):
        kts[quad] = ks[quad].T

    def visit(first, number):
        units = [plan[ALL + 2 + first + k] for k in range(number)]
        i = units[0] % N_Q
        for k in range(number):

            @pl.when(first + k >= DEPTH)
            def _():
                out_copy(first + k, 0).wait()

        prefetch(plan, ALL, in_copies, first, number)
        extra = ds[i, BLK:, :].astype(F32)
        delta = extra[0:1] + extra[1:2] + extra[2:3]
        for hp in range(2):
            cols = slice(hp * WIDE, (hp + 1) * WIDE)
            rhs = heads(ds, i, hp)
            dq = dqs[i, :, cols]
            for k in range(number):
                quad, at = units[k] // N_Q, (first + k) % DEPTH
                da = dot(vs[quad], rhs, NT)
                e = ebuf[at, :, cols].astype(F32)
                u = (e * (da - delta[:, cols])).astype(BF16)
                ubuf[at, :, cols] = u
                dq += dot(kts[quad], u, NN)
            dqs[i, :, cols] = dq
        for k in range(number):
            out_copy(first + k, units[k]).start()

    loop_units(plan, ALL, visit)
    dq_copies = copy_all([(dq_low.at[i], dq_hbm.at[place[AT_G + i]]) for i in range(N_Q)], dq_sem)
    for i in range(N_Q):
        dq_low[i] = dqs[i].astype(BF16)
        dq_copies[i].start()
    for c in dq_copies:
        c.wait()
    for n in range(DEPTH):

        @pl.when(n < plan[ALL + 1])
        def _():
            out_copy(n, 0).wait()


def run_parts(place, plan, near, far, kvs, e):
    dma = pltpu.SemaphoreType.DMA
    return pl.pallas_call(
        parts_kernel,
        out_shape=[
            pltpu.HBM((N_QUAD * N_Q, QUAD, COLS), BF16),
            pltpu.HBM((N_Q, HD, COLS), BF16),
        ],
        in_specs=[SM, SM] + [VM] * 6 + [HBM],
        out_specs=[HBM, HBM],
        scratch_shapes=[
            pltpu.VMEM((N_Q, D_ROWS, COLS), BF16),
            pltpu.VMEM((N_QUAD, QUAD, HD), BF16),
            pltpu.VMEM((N_QUAD, QUAD, HD), BF16),
            pltpu.VMEM((N_QUAD, HD, QUAD), BF16),
            pltpu.VMEM((DEPTH, QUAD, COLS), BF16),
            pltpu.VMEM((DEPTH, QUAD, COLS), BF16),
            pltpu.VMEM((N_Q, HD, COLS), F32),
            pltpu.VMEM((N_Q, HD, COLS), BF16),
            dma((DEPTH,)),
            dma((DEPTH,)),
            dma((N_Q,)),
        ],
        compiler_params=pltpu.CompilerParams(vmem_limit_bytes=18 * MIB),
    )(place, plan, near, far, *kvs, e)


def row_weights(place, stats, near, far, ws, wq, wdo):
    ms = [stats[j, :N_Q, :] for j in range(N_Q)]
    top = functools.reduce(jnp.maximum, ms)
    tot = sum(stats[j, N_Q:, :] * jnp.exp2((ms[j] - top) * EXP_SCALE) for j in range(N_Q))
    ws[...] = jnp.exp2((stats[place[AT_G], :N_Q, :] - top) * EXP_SCALE) / tot
    rows = []
    for i in range(N_Q):
        w = ws[pl.ds(place[AT_G + i], 1), :]
        rows += [w[:, h * BLK : (h + 1) * BLK] for h in range(HEADS)]
    rows.append(jnp.zeros((BLK - len(rows), BLK), F32))
    cols = jnp.concatenate(rows, axis=0).T
    for i in range(N_Q):
        q = queries_of(near, far, i)
        do = grads_of(near, far, i)
        for h in range(HEADS):
            w = cols[:, i * HEADS + h : i * HEADS + h + 1]
            at = slice(h * BLK, (h + 1) * BLK)
            c = slice(h * HD, (h + 1) * HD)
            wq[i, at, :] = (q[:, c].astype(F32) * w).astype(BF16)
            wdo[i, at, :] = (do[:BLK, c].astype(F32) * w).astype(BF16)


def sum_keys(plan, base, first_quad, rows, wq, wdo, e_hbm, u_hbm, acc, bufs, between=None):
    ebuf, ubuf, e_sem, u_sem = bufs
    size = acc.shape[1]

    def in_copies(n):
        unit, at = plan[base + 2 + n], n % DEPTH
        return [
            pltpu.make_async_copy(
                hbm.at[unit, pl.ds(rows, size)], buf.at[at, pl.ds(0, size)], sem.at[at]
            )
            for hbm, buf, sem in ((e_hbm, ebuf, e_sem), (u_hbm, ubuf, u_sem))
        ]

    start_first(plan, base, in_copies)
    acc[...] = jnp.zeros(acc.shape, F32)
    if between is not None:
        between()

    def visit(first, number):
        units = [plan[base + 2 + first + k] for k in range(number)]
        quad = units[0] // N_Q - first_quad
        prefetch(plan, base, in_copies, first, number)
        for buf, w, cols in ((ubuf, wq, slice(0, HD)), (ebuf, wdo, slice(HD, 2 * HD))):
            total = acc[quad, :, cols]
            for k in range(number):
                total += dot(buf[(first + k) % DEPTH, :size], w[units[k] % N_Q], NN)
            acc[quad, :, cols] = total

    loop_units(plan, base, visit)


def far_kernel(
    place, plan, stats, near, far, e_hbm, u_hbm,
    out1, out2, out3, wq_hbm, wdo_hbm,
    ws, wq, wdo, acc, acc_odd, w_sem, *bufs,
):
    w_copies = copy_all([(wq, wq_hbm), (wdo, wdo_hbm)], w_sem)

    def weigh():
        row_weights(place, stats, near, far, ws, wq, wdo)
        for c in w_copies:
            c.start()

    sum_keys(plan, FAR, 2, 0, wq, wdo, e_hbm, u_hbm, acc, bufs, weigh)
    sum_keys(plan, NEAR, 0, WIDE, wq, wdo, e_hbm, u_hbm, acc_odd, bufs)
    for quad in range(2):
        at = slice(quad * WIDE, (quad + 1) * WIDE)
        out1[at, :] = acc_odd[quad].astype(BF16)
        out2[at, :] = acc[quad, :WIDE].astype(BF16)
        out3[at, :] = acc[quad, WIDE:].astype(BF16)
    for c in w_copies:
        c.wait()


def own_kernel(plan, wq_hbm, wdo_hbm, e_hbm, u_hbm, out, wq, wdo, acc, w_sem, *bufs):
    w_copies = copy_all([(wq_hbm, wq), (wdo_hbm, wdo)], w_sem)
    for c in w_copies:
        c.start()

    def wait():
        for c in w_copies:
            c.wait()

    sum_keys(plan, NEAR, 0, 0, wq, wdo, e_hbm, u_hbm, acc, bufs, wait)
    for quad in range(2):
        out[quad * WIDE : (quad + 1) * WIDE, :] = acc[quad]


def keys_bufs(rows):
    return [
        pltpu.VMEM((DEPTH, rows, COLS), BF16),
        pltpu.VMEM((DEPTH, rows, COLS), BF16),
        pltpu.SemaphoreType.DMA((DEPTH,)),
        pltpu.SemaphoreType.DMA((DEPTH,)),
    ]


def run_far(place, plan, stats, near, far, e, u):
    return pl.pallas_call(
        far_kernel,
        out_shape=[struct((QUAD, 2 * HD), BF16)] * 3 + [pltpu.HBM((N_Q, COLS, HD), BF16)] * 2,
        in_specs=[SM, SM] + [VM] * 3 + [HBM, HBM],
        out_specs=[VM] * 3 + [HBM] * 2,
        scratch_shapes=[
            pltpu.VMEM((N_Q, COLS), F32),
            pltpu.VMEM((N_Q, COLS, HD), BF16),
            pltpu.VMEM((N_Q, COLS, HD), BF16),
            pltpu.VMEM((2, QUAD, 2 * HD), F32),
            pltpu.VMEM((2, WIDE, 2 * HD), F32),
            pltpu.SemaphoreType.DMA((2,)),
        ]
        + keys_bufs(QUAD),
        compiler_params=pltpu.CompilerParams(vmem_limit_bytes=18 * MIB),
    )(place, plan, stats, near, far, e, u)


def run_own(plan, wq, wdo, e, u):
    return pl.pallas_call(
        own_kernel,
        out_shape=struct((QUAD, 2 * HD), F32),
        in_specs=[SM] + [HBM] * 4,
        out_specs=VM,
        scratch_shapes=[
            pltpu.VMEM((N_Q, COLS, HD), BF16),
            pltpu.VMEM((N_Q, COLS, HD), BF16),
            pltpu.VMEM((2, WIDE, 2 * HD), F32),
            pltpu.SemaphoreType.DMA((2,)),
        ]
        + keys_bufs(WIDE),
        compiler_params=pltpu.CompilerParams(vmem_limit_bytes=12 * MIB),
    )(plan, wq, wdo, e, u)


def sum_kernel(place, own, a, b, c, out):
    for d in range(4):
        at = slice(d * BLK, (d + 1) * BLK)
        total = own[at] + a[at].astype(F32) + b[at].astype(F32) + c[at].astype(F32)
        out[place[AT_Z + d]] = total.astype(BF16)


def run_sum(place, own, a, b, c):
    return pl.pallas_call(
        sum_kernel,
        out_shape=struct((4, BLK, 2 * HD), BF16),
        in_specs=[SM] + [VM] * 4,
        out_specs=VM,
        compiler_params=pltpu.CompilerParams(vmem_limit_bytes=6 * MIB),
    )(place, own, a, b, c)


def queries_kernel(place, parts, stats, out):
    own = place[AT_G]
    ms = [stats[j, pl.ds(own, 1), :] for j in range(N_Q)]
    ls = [stats[j, pl.ds(N_Q + own, 1), :] for j in range(N_Q)]
    top = functools.reduce(jnp.maximum, ms)
    es = [jnp.exp2((m - top) * EXP_SCALE) for m in ms]
    tot = sum(l * e for l, e in zip(ls, es))
    for h in range(HEADS):
        at = slice(h * HD, (h + 1) * HD)
        total = sum(parts[j, :, at].astype(F32) * es[j][:, at] for j in range(N_Q))
        out[:, at] = (total * (SCALING / tot[:, at])).T


def run_queries(place, parts, stats):
    return pl.pallas_call(
        queries_kernel,
        out_shape=struct((BLK, COLS), F32),
        in_specs=[SM, VM, VM],
        out_specs=VM,
        compiler_params=pltpu.CompilerParams(vmem_limit_bytes=6 * MIB),
    )(place, parts, stats)


def exchange(x, dx=0, dz=0, dy=0, dc=0):
    perm = []
    for b in range(16):
        for r in range(16):
            px = (b // 8) * 2 + (r // 2) % 2
            pz, py, pc = b % 8, r // 4, r % 2
            px, pz, py, pc = px ^ dx, pz ^ (2 * dz), py ^ dy, pc ^ dc
            other = (px // 2) * 8 + pz, py * 4 + (px % 2) * 2 + pc
            perm.append((b * 16 + r, other[0] * 16 + other[1]))
    return lax.ppermute(x, ("blk", "rows"), perm)


Q_GROUPS = [[r for r in range(16) if (r // 2) % 2 == lo] for lo in range(2)]
Z_GROUPS = [[8 * hi + 2 * z + par for z in range(4)] for hi in range(2) for par in range(2)]


def to_group(x):
    return lax.all_to_all(x, "rows", 0, 0, axis_index_groups=Q_GROUPS, tiled=True)


def per_device(queries, keys, values, forward_out, grad_out, block_mask):
    b, r = lax.axis_index("blk"), lax.axis_index("rows")
    x = ((b >> 3) << 1) | ((r >> 1) & 1)
    zz, y, core = (b >> 1) & 3, r >> 2, r & 1
    slot_q = jnp.arange(N_Q)
    yq, cq = y ^ (slot_q & 3), core ^ (slot_q >> 2)
    q_blocks = ((b >> 1) << 4) + (yq << 2) + ((x & 1) << 1) + cq
    slot_k = jnp.arange(N_K)
    quad, a = slot_k >> 2, slot_k & 3
    xk = x ^ (((quad >> 1) << 1) | (a >> 1))
    zk = zz ^ (((quad & 1) << 1) | (a & 1))
    k_blocks = ((((xk >> 1) << 2) + zk) << 4) + (y << 2) + ((xk & 1) << 1) + core
    place = jnp.concatenate(
        [(b & 1)[None], q_blocks, k_blocks, (yq << 1) + cq, zz ^ jnp.arange(4)]
    ).astype(jnp.int32)

    kv = pack_keys(keys, values)
    kv, queries = lax.optimization_barrier((kv, queries))
    qdo = pack_queries(queries, grad_out, forward_out)

    kv_z = jnp.concatenate([kv] + [exchange(kv, dz=d) for d in (1, 2, 3)], axis=0)
    kvs = [kv_z] + [exchange(kv_z, dx=d) for d in (1, 2, 3)]
    others = [exchange(qdo, dy=d) for d in (1, 2, 3)]
    plan = run_plan(place, pltpu.with_memory_space_constraint(block_mask, pltpu.HBM))
    *others, k1, k2, k3, plan = lax.optimization_barrier((*others, *kvs[1:], plan))
    kvs = [kv_z, k1, k2, k3]
    near = jnp.concatenate([qdo, *others], axis=0)
    far = exchange(near, dc=1)

    e, stat = run_scores(place, plan, near, far, kvs)
    e = pltpu.with_memory_space_constraint(e, pltpu.HBM)
    stats = to_group(stat)
    u, dq = run_parts(place, plan, near, far, kvs, e)
    u = pltpu.with_memory_space_constraint(u, pltpu.HBM)
    dq_parts = to_group(dq)
    *remote, wq, wdo = run_far(place, plan, stats, near, far, e, u)
    wq, wdo = [pltpu.with_memory_space_constraint(w, pltpu.HBM) for w in (wq, wdo)]
    got1, got2, got3 = [exchange(f, dx=d) for d, f in zip((1, 2, 3), remote)]
    wq, dq_parts = lax.optimization_barrier((wq, dq_parts))
    own = run_own(plan, wq, wdo, e, u)
    summed = run_sum(place, own, got1, got2, got3)
    back = lax.all_to_all(summed, "blk", 0, 0, axis_index_groups=Z_GROUPS, tiled=True)
    grad_queries = run_queries(place, dq_parts, stats)
    total = jnp.sum(back.astype(F32), axis=0)
    return grad_queries, total[:, :HD] * SCALING, total[:, HD:]


def solution(mesh):
    spec = P(("blk", "rows"), None)
    return jax.shard_map(
        per_device,
        mesh=mesh,
        in_specs=(spec, spec, spec, spec, spec, P()),
        out_specs=(spec, spec, spec),
        check_vma=False,
    )
```

```python
import functools
import math

import jax
import jax.numpy as jnp
from jax import lax
from jax.experimental import pallas as pl
from jax.experimental.pallas import tpu as pltpu
from jax.sharding import PartitionSpec as P

BLK = 128
HEADS = 4
HD = 128
COLS = HEADS * HD
N_Q = 8
N_K = 16
N_QUAD = N_K // 4
QUAD = 4 * BLK
WIDE = 2 * BLK
EXTRA = 16
D_ROWS = BLK + EXTRA
ROWS = BLK + D_ROWS
NEGATIVE = -1e30
FLOOR = -1e6
SCALING = 1.0 / math.sqrt(HD)
EXP_SCALE = SCALING * math.log2(math.e)
MIB = 1024 * 1024
F32 = jnp.float32
BF16 = jnp.bfloat16
ANY = pl.BlockSpec(memory_space=pl.ANY)
HBM = pl.BlockSpec(memory_space=pltpu.HBM)
VM = pl.BlockSpec(memory_space=pltpu.VMEM)
SM = pl.BlockSpec(memory_space=pltpu.SMEM)

NT = (((1,), (1,)), ((), ()))
NN = (((1,), (0,)), ((), ()))


def dot(a, b, dims):
    return lax.dot_general(a, b, dims, preferred_element_type=F32)


def struct(shape, dtype):
    return jax.ShapeDtypeStruct(shape, dtype)


def copy_all(pairs, sem):
    return [pltpu.make_async_copy(a, b, sem.at[n]) for n, (a, b) in enumerate(pairs)]


def pack_keys_kernel(k_ref, v_ref, kv_ref, sem):
    copies = copy_all(
        [(k_ref, kv_ref.at[:, pl.ds(0, HD)]), (v_ref, kv_ref.at[:, pl.ds(HD, HD)])], sem
    )
    for c in copies:
        c.start()
    for c in copies:
        c.wait()


def pack_queries_kernel(q_ref, do_ref, o_ref, qdo_ref, o_buf, sem):
    copies = copy_all(
        [
            (do_ref, qdo_ref.at[pl.ds(BLK, BLK)]),
            (o_ref, o_buf),
            (q_ref, qdo_ref.at[pl.ds(0, BLK)]),
        ],
        sem,
    )
    for c in copies:
        c.start()
    for c in copies[:2]:
        c.wait()
    prod = qdo_ref[BLK : 2 * BLK, :].astype(F32) * o_buf[...].astype(F32)
    delta = jnp.concatenate(
        [
            jnp.sum(prod[:, h * HD : (h + 1) * HD].T, axis=0, keepdims=True)
            for h in range(HEADS)
        ],
        axis=1,
    )
    high = delta.astype(BF16).astype(F32)
    rest = delta - high
    mid = rest.astype(BF16).astype(F32)
    low = rest - mid
    row = lax.broadcasted_iota(jnp.int32, (EXTRA, COLS), 0)
    extra = jnp.where(row == 0, high, jnp.where(row == 1, mid, jnp.where(row == 2, low, 0.0)))
    qdo_ref[2 * BLK :, :] = extra.astype(BF16)
    copies[2].wait()


def pack_keys(keys, values):
    return pl.pallas_call(
        pack_keys_kernel,
        out_shape=struct((BLK, 2 * HD), BF16),
        in_specs=[HBM] * 2,
        out_specs=VM,
        scratch_shapes=[pltpu.SemaphoreType.DMA((2,))],
        compiler_params=pltpu.CompilerParams(vmem_limit_bytes=4 * MIB),
    )(*[pltpu.with_memory_space_constraint(a, pltpu.HBM) for a in (keys, values)])


def pack_queries(queries, grad_out, forward_out):
    return pl.pallas_call(
        pack_queries_kernel,
        out_shape=struct((ROWS, COLS), BF16),
        in_specs=[HBM] * 3,
        out_specs=VM,
        scratch_shapes=[pltpu.VMEM((BLK, COLS), BF16), pltpu.SemaphoreType.DMA((3,))],
        compiler_params=pltpu.CompilerParams(vmem_limit_bytes=6 * MIB),
    )(*[pltpu.with_memory_space_constraint(a, pltpu.HBM) for a in (queries, grad_out, forward_out)])


AT_Q, AT_K, AT_G = 1, 1 + N_Q, 1 + N_Q + N_K
LIMITS, TABLE, ALL, FAR, NEAR, PLAN = 0, 128, 192, 256, 288, 320
T_ROW, T_COUNT = 8, 4


def plan_kernel(place, mask_hbm, plan, mask_s, found, sem):
    copy = pltpu.make_async_copy(mask_hbm.at[place[0]], mask_s, sem)
    copy.start()
    copy.wait()

    def row(i, carry):
        at = place[AT_Q + i]
        active = jnp.int32(0)
        for quad in range(N_QUAD):
            seen = jnp.int32(0)
            for a in range(4):
                level = mask_s[at, place[AT_K + 4 * quad + a]]
                plan[LIMITS + i * N_K + 4 * quad + a] = jnp.where(
                    level == 1, -BLK, jnp.where(level == 2, 0, BLK)
                )
                seen = seen | level
            plan[TABLE + i * T_ROW + active] = quad
            active += jnp.where(seen != 0, 1, 0)
        plan[TABLE + i * T_ROW + T_COUNT] = active
        return carry

    lax.fori_loop(0, N_Q, row, 0)

    n = jnp.int32(0)
    for i in range(N_Q):
        count = plan[TABLE + i * T_ROW + T_COUNT]
        for j in range(2):
            plan[ALL + 2 + n] = plan[TABLE + i * T_ROW + 2 * j] * N_Q + i
            plan[ALL + 3 + n] = plan[TABLE + i * T_ROW + 2 * j + 1] * N_Q + i
            n += jnp.where(count >= 2 * j + 2, 2, 0)
    plan[ALL] = n // 2
    for i in range(N_Q):
        count = plan[TABLE + i * T_ROW + T_COUNT]
        plan[ALL + 2 + n] = plan[TABLE + i * T_ROW + jnp.maximum(count - 1, 0)] * N_Q + i
        n += count % 2
    plan[ALL + 1] = n

    for base, quads in ((NEAR, (0, 1)), (FAR, (2, 3))):
        n = jnp.int32(0)
        for i in range(N_Q):
            has = [jnp.int32(0), jnp.int32(0)]
            for k in range(2):
                for a in range(N_QUAD):
                    here = (plan[TABLE + i * T_ROW + a] == quads[k]) & (
                        a < plan[TABLE + i * T_ROW + T_COUNT]
                    )
                    has[k] = has[k] | jnp.where(here, 1, 0)
            found[2 * i] = has[0]
            found[2 * i + 1] = has[1]
            plan[base + 2 + n] = quads[0] * N_Q + i
            plan[base + 3 + n] = quads[1] * N_Q + i
            n += 2 * (has[0] & has[1])
        plan[base] = n // 2
        for i in range(N_Q):
            plan[base + 2 + n] = (quads[0] + found[2 * i + 1]) * N_Q + i
            n += found[2 * i] ^ found[2 * i + 1]
        plan[base + 1] = n


def run_plan(place, mask):
    return pl.pallas_call(
        plan_kernel,
        out_shape=struct((PLAN,), jnp.int32),
        in_specs=[SM, HBM],
        out_specs=SM,
        scratch_shapes=[
            pltpu.SMEM((BLK, BLK), jnp.int32),
            pltpu.SMEM((32,), jnp.int32),
            pltpu.SemaphoreType.DMA(()),
        ],
        compiler_params=pltpu.CompilerParams(vmem_limit_bytes=4 * MIB),
    )(place, mask)


def queries_of(near, far, i):
    at = (i % 4) * ROWS
    return (near, far)[i // 4][at : at + BLK]


def grads_of(near, far, i):
    at = (i % 4) * ROWS + BLK
    return (near, far)[i // 4][at : at + D_ROWS]


def fill_quads(kvs, cols, buf):
    for quad in range(N_QUAD):
        for odd in range(2):
            at = slice((quad % 2) * WIDE, (quad % 2 + 1) * WIDE)
            buf[quad, odd * WIDE : (odd + 1) * WIDE] = kvs[2 * (quad // 2) + odd][at, cols]


def join(parts, axis=0):
    return parts[0] if len(parts) == 1 else jnp.concatenate(parts, axis=axis)


def heads(ref, i):
    return jnp.concatenate([ref[i, :BLK, h * HD : (h + 1) * HD] for h in range(HEADS)], axis=0)


E_SLOTS = 4


def scores_kernel(
    place, plan, near, far, kv0, kv1, kv2, kv3,
    e_hbm, stats_hbm,
    qs, ks, sc, ebuf, mx, lacc, st, count, e_sem, st_sem,
):
    count[0] = 0
    fill_quads((kv0, kv1, kv2, kv3), slice(0, HD), ks)
    for i in range(N_Q):
        qs[i] = queries_of(near, far, i)
    diff = (
        lax.broadcasted_iota(jnp.int32, (BLK, WIDE), 1) % BLK
        - lax.broadcasted_iota(jnp.int32, (BLK, WIDE), 0)
    )

    def out_copy(slot, unit):
        return pltpu.make_async_copy(ebuf.at[slot], e_hbm.at[unit], e_sem.at[slot])

    def query_block(i, carry):
        base = TABLE + i * T_ROW
        active = plan[base + T_COUNT]
        mx[...] = jnp.full(mx.shape, NEGATIVE, F32)
        lacc[...] = jnp.zeros(lacc.shape, F32)

        def score_quads(quads):
            joined = dot(join([ks[quad] for quad in quads]), heads(qs, i), NT)
            for hp in range(2):
                cols = slice(hp * WIDE, (hp + 1) * WIDE)
                best = mx[:, cols]
                for k, quad in enumerate(quads):
                    for a in range(4):
                        at = slice(a * BLK, (a + 1) * BLK)
                        s = joined[k * QUAD + a * BLK : k * QUAD + (a + 1) * BLK, cols]
                        limit = plan[LIMITS + i * N_K + 4 * quad + a]
                        part = jnp.where(diff >= limit, s, NEGATIVE)
                        sc[quad, at, cols] = part
                        best = jnp.maximum(
                            best, jnp.max(part.reshape(BLK // 8, 8, WIDE), axis=0)
                        )
                mx[:, cols] = best

        def score_pair(n, carry):
            score_quads([plan[base + 2 * n], plan[base + 2 * n + 1]])
            return carry

        lax.fori_loop(0, active // 2, score_pair, 0)

        @pl.when(active % 2 == 1)
        def _():
            score_quads([plan[base + active - 1]])

        m = jnp.maximum(jnp.max(mx[...], axis=0, keepdims=True), FLOOR)

        def exp_quad(k, carry):
            quad = plan[base + k]
            n = count[0]
            slot = n % E_SLOTS

            @pl.when(n >= E_SLOTS)
            def _():
                out_copy(slot, 0).wait()

            for hp in range(2):
                cols = slice(hp * WIDE, (hp + 1) * WIDE)
                e = jnp.exp2((sc[quad, :, cols] - m[:, cols]) * EXP_SCALE)
                lacc[:, cols] += jnp.sum(e.reshape(QUAD // 8, 8, WIDE), axis=0)
                ebuf[slot, :, cols] = e.astype(BF16)
            out_copy(slot, quad * N_Q + i).start()
            count[0] = n + 1
            return carry

        lax.fori_loop(0, active, exp_quad, 0)
        g = place[AT_G + i]
        st[pl.ds(g, 1), :] = m
        st[pl.ds(N_Q + g, 1), :] = jnp.sum(lacc[...], axis=0, keepdims=True)
        return carry

    lax.fori_loop(0, N_Q, query_block, 0)

    st_copies = copy_all([(st, stats_hbm.at[g]) for g in range(N_Q)], st_sem)
    for c in st_copies:
        c.start()
    for c in st_copies:
        c.wait()
    for slot_no in range(E_SLOTS):

        @pl.when(count[0] > slot_no)
        def _():
            out_copy(slot_no, 0).wait()


def run_scores(place, plan, near, far, kvs):
    return pl.pallas_call(
        scores_kernel,
        out_shape=[
            pltpu.HBM((N_QUAD * N_Q, QUAD, COLS), BF16),
            pltpu.HBM((N_Q, 2 * N_Q, COLS), F32),
        ],
        in_specs=[SM, SM] + [VM] * 6,
        out_specs=[HBM, HBM],
        scratch_shapes=[
            pltpu.VMEM((N_Q, BLK, COLS), BF16),
            pltpu.VMEM((N_QUAD, QUAD, HD), BF16),
            pltpu.VMEM((N_QUAD, QUAD, COLS), F32),
            pltpu.VMEM((E_SLOTS, QUAD, COLS), BF16),
            pltpu.VMEM((8, COLS), F32),
            pltpu.VMEM((8, COLS), F32),
            pltpu.VMEM((2 * N_Q, COLS), F32),
            pltpu.SMEM((1,), jnp.int32),
            pltpu.SemaphoreType.DMA((E_SLOTS,)),
            pltpu.SemaphoreType.DMA((N_Q,)),
        ],
        compiler_params=pltpu.CompilerParams(vmem_limit_bytes=20 * MIB),
    )(place, plan, near, far, *kvs)


DEPTH = 4


def loop_units(plan, base, visit):
    pairs, total = plan[base], plan[base + 1]

    def pair(n, carry):
        visit(2 * n, 2)
        return carry

    def single(n, carry):
        visit(n, 1)
        return carry

    lax.fori_loop(0, pairs, pair, 0)
    lax.fori_loop(2 * pairs, total, single, 0)


def prefetch(plan, base, copies, first, number):
    total = plan[base + 1]
    for k in range(number):

        @pl.when(first + k + 2 < total)
        def _():
            for c in copies(first + k + 2):
                c.start()

    for k in range(number):
        for c in copies(first + k):
            c.wait()


def start_first(plan, base, copies):
    for n in range(2):

        @pl.when(n < plan[base + 1])
        def _():
            for c in copies(n):
                c.start()


def parts_kernel(
    place, plan, near, far, kv0, kv1, kv2, kv3, e_hbm,
    u_hbm, dq_hbm,
    ds, ks, vs, kts, ebuf, ubuf, dqs, dq_low, e_sem, u_sem, dq_sem,
):
    def in_copies(n):
        unit, at = plan[ALL + 2 + n], n % DEPTH
        return (pltpu.make_async_copy(e_hbm.at[unit], ebuf.at[at], e_sem.at[at]),)

    def out_copy(n, unit):
        at = n % DEPTH
        return pltpu.make_async_copy(ubuf.at[at], u_hbm.at[unit], u_sem.at[at])

    start_first(plan, ALL, in_copies)
    kvs = (kv0, kv1, kv2, kv3)
    fill_quads(kvs, slice(0, HD), ks)
    fill_quads(kvs, slice(HD, 2 * HD), vs)
    for i in range(N_Q):
        ds[i] = grads_of(near, far, i)
    dqs[...] = jnp.zeros(dqs.shape, F32)
    for quad in range(N_QUAD):
        kts[quad] = ks[quad].T

    def visit(first, number):
        units = [plan[ALL + 2 + first + k] for k in range(number)]
        i = units[0] % N_Q
        for k in range(number):

            @pl.when(first + k >= DEPTH)
            def _():
                out_copy(first + k, 0).wait()

        prefetch(plan, ALL, in_copies, first, number)
        extra = ds[i, BLK:, :].astype(F32)
        delta = extra[0:1] + extra[1:2] + extra[2:3]
        quads = [unit // N_Q for unit in units]
        da = dot(join([vs[quad] for quad in quads]), heads(ds, i), NT)
        us = []
        for k in range(number):
            at = (first + k) % DEPTH
            u = (ebuf[at].astype(F32) * (da[k * QUAD : (k + 1) * QUAD] - delta)).astype(BF16)
            ubuf[at] = u
            us.append(u)
        dqs[i] += dot(join([kts[quad] for quad in quads], axis=1), join(us), NN)
        for k in range(number):
            out_copy(first + k, units[k]).start()

    loop_units(plan, ALL, visit)
    dq_copies = copy_all([(dq_low.at[i], dq_hbm.at[place[AT_G + i]]) for i in range(N_Q)], dq_sem)
    for i in range(N_Q):
        dq_low[i] = dqs[i].astype(BF16)
        dq_copies[i].start()
    for c in dq_copies:
        c.wait()
    for n in range(DEPTH):

        @pl.when(n < plan[ALL + 1])
        def _():
            out_copy(n, 0).wait()


def run_parts(place, plan, near, far, kvs, e):
    dma = pltpu.SemaphoreType.DMA
    return pl.pallas_call(
        parts_kernel,
        out_shape=[
            pltpu.HBM((N_QUAD * N_Q, QUAD, COLS), BF16),
            pltpu.HBM((N_Q, HD, COLS), BF16),
        ],
        in_specs=[SM, SM] + [VM] * 6 + [HBM],
        out_specs=[HBM, HBM],
        scratch_shapes=[
            pltpu.VMEM((N_Q, D_ROWS, COLS), BF16),
            pltpu.VMEM((N_QUAD, QUAD, HD), BF16),
            pltpu.VMEM((N_QUAD, QUAD, HD), BF16),
            pltpu.VMEM((N_QUAD, HD, QUAD), BF16),
            pltpu.VMEM((DEPTH, QUAD, COLS), BF16),
            pltpu.VMEM((DEPTH, QUAD, COLS), BF16),
            pltpu.VMEM((N_Q, HD, COLS), F32),
            pltpu.VMEM((N_Q, HD, COLS), BF16),
            dma((DEPTH,)),
            dma((DEPTH,)),
            dma((N_Q,)),
        ],
        compiler_params=pltpu.CompilerParams(vmem_limit_bytes=24 * MIB),
    )(place, plan, near, far, *kvs, e)


def row_weights(place, stats, near, far, ws, wq, wdo):
    ms = [stats[j, :N_Q, :] for j in range(N_Q)]
    top = functools.reduce(jnp.maximum, ms)
    tot = sum(stats[j, N_Q:, :] * jnp.exp2((ms[j] - top) * EXP_SCALE) for j in range(N_Q))
    ws[...] = jnp.exp2((stats[place[AT_G], :N_Q, :] - top) * EXP_SCALE) / tot
    rows = []
    for i in range(N_Q):
        w = ws[pl.ds(place[AT_G + i], 1), :]
        rows += [w[:, h * BLK : (h + 1) * BLK] for h in range(HEADS)]
    rows.append(jnp.zeros((BLK - len(rows), BLK), F32))
    cols = jnp.concatenate(rows, axis=0).T
    for i in range(N_Q):
        q = queries_of(near, far, i)
        do = grads_of(near, far, i)
        for h in range(HEADS):
            w = cols[:, i * HEADS + h : i * HEADS + h + 1]
            at = slice(h * BLK, (h + 1) * BLK)
            c = slice(h * HD, (h + 1) * HD)
            wq[i, at, :] = (q[:, c].astype(F32) * w).astype(BF16)
            wdo[i, at, :] = (do[:BLK, c].astype(F32) * w).astype(BF16)


def sum_keys(plan, base, first_quad, rows, wq, wdo, e_hbm, u_hbm, acc, bufs, between=None):
    ebuf, ubuf, e_sem, u_sem = bufs
    size = acc.shape[1]

    def in_copies(n):
        unit, at = plan[base + 2 + n], n % DEPTH
        return [
            pltpu.make_async_copy(
                hbm.at[unit, pl.ds(rows, size)], buf.at[at, pl.ds(0, size)], sem.at[at]
            )
            for hbm, buf, sem in ((e_hbm, ebuf, e_sem), (u_hbm, ubuf, u_sem))
        ]

    start_first(plan, base, in_copies)
    acc[...] = jnp.zeros(acc.shape, F32)
    if between is not None:
        between()

    def visit(first, number):
        unit = plan[base + 2 + first]
        i, quad = unit % N_Q, unit // N_Q - first_quad
        prefetch(plan, base, in_copies, first, number)
        for buf, w, cols in ((ubuf, wq, slice(0, HD)), (ebuf, wdo, slice(HD, 2 * HD))):
            joined = dot(
                join([buf[(first + k) % DEPTH, :size] for k in range(number)]), w[i], NN
            )
            for k in range(number):
                acc[quad + k, :, cols] += joined[k * size : (k + 1) * size]

    loop_units(plan, base, visit)


def far_kernel(
    place, plan, stats, near, far, e_hbm, u_hbm,
    out1, out2, out3, wq_hbm, wdo_hbm,
    ws, wq, wdo, acc, acc_odd, w_sem, *bufs,
):
    w_copies = copy_all([(wq, wq_hbm), (wdo, wdo_hbm)], w_sem)

    def weigh():
        row_weights(place, stats, near, far, ws, wq, wdo)
        for c in w_copies:
            c.start()

    sum_keys(plan, FAR, 2, 0, wq, wdo, e_hbm, u_hbm, acc, bufs, weigh)
    sum_keys(plan, NEAR, 0, WIDE, wq, wdo, e_hbm, u_hbm, acc_odd, bufs)
    for quad in range(2):
        at = slice(quad * WIDE, (quad + 1) * WIDE)
        out1[at, :] = acc_odd[quad].astype(BF16)
        out2[at, :] = acc[quad, :WIDE].astype(BF16)
        out3[at, :] = acc[quad, WIDE:].astype(BF16)
    for c in w_copies:
        c.wait()


def own_kernel(plan, wq_hbm, wdo_hbm, e_hbm, u_hbm, out, wq, wdo, acc, w_sem, *bufs):
    w_copies = copy_all([(wq_hbm, wq), (wdo_hbm, wdo)], w_sem)
    for c in w_copies:
        c.start()

    def wait():
        for c in w_copies:
            c.wait()

    sum_keys(plan, NEAR, 0, 0, wq, wdo, e_hbm, u_hbm, acc, bufs, wait)
    for quad in range(2):
        out[quad * WIDE : (quad + 1) * WIDE, :] = acc[quad]


def keys_bufs(rows):
    return [
        pltpu.VMEM((DEPTH, rows, COLS), BF16),
        pltpu.VMEM((DEPTH, rows, COLS), BF16),
        pltpu.SemaphoreType.DMA((DEPTH,)),
        pltpu.SemaphoreType.DMA((DEPTH,)),
    ]


def run_far(place, plan, stats, near, far, e, u):
    return pl.pallas_call(
        far_kernel,
        out_shape=[struct((QUAD, 2 * HD), BF16)] * 3 + [pltpu.HBM((N_Q, COLS, HD), BF16)] * 2,
        in_specs=[SM, SM] + [VM] * 3 + [HBM, HBM],
        out_specs=[VM] * 3 + [HBM] * 2,
        scratch_shapes=[
            pltpu.VMEM((N_Q, COLS), F32),
            pltpu.VMEM((N_Q, COLS, HD), BF16),
            pltpu.VMEM((N_Q, COLS, HD), BF16),
            pltpu.VMEM((2, QUAD, 2 * HD), F32),
            pltpu.VMEM((2, WIDE, 2 * HD), F32),
            pltpu.SemaphoreType.DMA((2,)),
        ]
        + keys_bufs(QUAD),
        compiler_params=pltpu.CompilerParams(vmem_limit_bytes=18 * MIB),
    )(place, plan, stats, near, far, e, u)


def run_own(plan, wq, wdo, e, u):
    return pl.pallas_call(
        own_kernel,
        out_shape=struct((QUAD, 2 * HD), F32),
        in_specs=[SM] + [HBM] * 4,
        out_specs=VM,
        scratch_shapes=[
            pltpu.VMEM((N_Q, COLS, HD), BF16),
            pltpu.VMEM((N_Q, COLS, HD), BF16),
            pltpu.VMEM((2, WIDE, 2 * HD), F32),
            pltpu.SemaphoreType.DMA((2,)),
        ]
        + keys_bufs(WIDE),
        compiler_params=pltpu.CompilerParams(vmem_limit_bytes=12 * MIB),
    )(plan, wq, wdo, e, u)


def sum_kernel(own, a, b, c, out0, out1, out2, out3):
    for d, out in enumerate((out0, out1, out2, out3)):
        at = slice(d * BLK, (d + 1) * BLK)
        total = own[at] + a[at].astype(F32) + b[at].astype(F32) + c[at].astype(F32)
        out[...] = total.astype(out.dtype)


def run_sum(own, a, b, c):
    return pl.pallas_call(
        sum_kernel,
        out_shape=[struct((BLK, 2 * HD), F32)] + [struct((BLK, 2 * HD), BF16)] * 3,
        in_specs=[VM] * 4,
        out_specs=[VM] * 4,
        compiler_params=pltpu.CompilerParams(vmem_limit_bytes=6 * MIB),
    )(own, a, b, c)


def queries_kernel(place, parts, stats, out):
    own = place[AT_G]
    ms = [stats[j, pl.ds(own, 1), :] for j in range(N_Q)]
    ls = [stats[j, pl.ds(N_Q + own, 1), :] for j in range(N_Q)]
    top = functools.reduce(jnp.maximum, ms)
    es = [jnp.exp2((m - top) * EXP_SCALE) for m in ms]
    tot = sum(l * e for l, e in zip(ls, es))
    for h in range(HEADS):
        at = slice(h * HD, (h + 1) * HD)
        total = sum(parts[j, :, at].astype(F32) * es[j][:, at] for j in range(N_Q))
        out[:, at] = (total * (SCALING / tot[:, at])).T


def run_queries(place, parts, stats):
    return pl.pallas_call(
        queries_kernel,
        out_shape=struct((BLK, COLS), F32),
        in_specs=[SM, VM, VM],
        out_specs=VM,
        compiler_params=pltpu.CompilerParams(vmem_limit_bytes=6 * MIB),
    )(place, parts, stats)


def exchange(x, dx=0, dz=0, dy=0, dc=0):
    perm = []
    for b in range(16):
        for r in range(16):
            px = (b // 8) * 2 + (r // 2) % 2
            pz, py, pc = b % 8, r // 4, r % 2
            px, pz, py, pc = px ^ dx, pz ^ (2 * dz), py ^ dy, pc ^ dc
            other = (px // 2) * 8 + pz, py * 4 + (px % 2) * 2 + pc
            perm.append((b * 16 + r, other[0] * 16 + other[1]))
    return lax.ppermute(x, ("blk", "rows"), perm)


Q_GROUPS = [[r for r in range(16) if (r // 2) % 2 == lo] for lo in range(2)]


def to_group(x):
    return lax.all_to_all(x, "rows", 0, 0, axis_index_groups=Q_GROUPS, tiled=True)


def per_device(queries, keys, values, forward_out, grad_out, block_mask):
    b, r = lax.axis_index("blk"), lax.axis_index("rows")
    x = ((b >> 3) << 1) | ((r >> 1) & 1)
    zz, y, core = (b >> 1) & 3, r >> 2, r & 1
    slot_q = jnp.arange(N_Q)
    yq, cq = y ^ (slot_q & 3), core ^ (slot_q >> 2)
    q_blocks = ((b >> 1) << 4) + (yq << 2) + ((x & 1) << 1) + cq
    slot_k = jnp.arange(N_K)
    quad, a = slot_k >> 2, slot_k & 3
    xk = x ^ (((quad >> 1) << 1) | (a >> 1))
    zk = zz ^ (((quad & 1) << 1) | (a & 1))
    k_blocks = ((((xk >> 1) << 2) + zk) << 4) + (y << 2) + ((xk & 1) << 1) + core
    place = jnp.concatenate([(b & 1)[None], q_blocks, k_blocks, (yq << 1) + cq]).astype(jnp.int32)

    kv = pack_keys(keys, values)
    kv, queries = lax.optimization_barrier((kv, queries))
    qdo = pack_queries(queries, grad_out, forward_out)

    kv_z = jnp.concatenate([kv] + [exchange(kv, dz=d) for d in (1, 2, 3)], axis=0)
    kvs = [kv_z] + [exchange(kv_z, dx=d) for d in (1, 2, 3)]
    others = [exchange(qdo, dy=d) for d in (1, 2, 3)]
    plan = run_plan(place, pltpu.with_memory_space_constraint(block_mask, pltpu.HBM))
    *others, k1, k2, k3, plan = lax.optimization_barrier((*others, *kvs[1:], plan))
    kvs = [kv_z, k1, k2, k3]
    near = jnp.concatenate([qdo, *others], axis=0)
    far = exchange(near, dc=1)

    e, stat = run_scores(place, plan, near, far, kvs)
    e = pltpu.with_memory_space_constraint(e, pltpu.HBM)
    stats = to_group(stat)
    u, dq = run_parts(place, plan, near, far, kvs, e)
    u = pltpu.with_memory_space_constraint(u, pltpu.HBM)
    dq_parts = to_group(dq)
    *remote, wq, wdo = run_far(place, plan, stats, near, far, e, u)
    wq, wdo = [pltpu.with_memory_space_constraint(w, pltpu.HBM) for w in (wq, wdo)]
    got1, got2, got3 = [exchange(f, dx=d) for d, f in zip((1, 2, 3), remote)]
    wq, dq_parts = lax.optimization_barrier((wq, dq_parts))
    own = run_own(plan, wq, wdo, e, u)
    mine, *rest = run_sum(own, got1, got2, got3)
    back = [exchange(part, dz=d) for d, part in zip((1, 2, 3), rest)]
    grad_queries = run_queries(place, dq_parts, stats)
    total = mine + sum(part.astype(F32) for part in back)
    return grad_queries, total[:, :HD] * SCALING, total[:, HD:]


def solution(mesh):
    spec = P(("blk", "rows"), None)
    return jax.shard_map(
        per_device,
        mesh=mesh,
        in_specs=(spec, spec, spec, spec, spec, P()),
        out_specs=(spec, spec, spec),
        check_vma=False,
    )
```

```python
import functools
import math

import jax
import jax.numpy as jnp
from jax import lax
from jax.experimental import pallas as pl
from jax.experimental.pallas import tpu as pltpu
from jax.sharding import PartitionSpec as P

BLK = 128
HEADS = 4
HD = 128
COLS = HEADS * HD
N_Q = 8
N_K = 16
N_QUAD = N_K // 4
QUAD = 4 * BLK
WIDE = 2 * BLK
EXTRA = 16
D_ROWS = BLK + EXTRA
ROWS = BLK + D_ROWS
NEGATIVE = -1e30
FLOOR = -1e6
SCALING = 1.0 / math.sqrt(HD)
EXP_SCALE = SCALING * math.log2(math.e)
MIB = 1024 * 1024
F32 = jnp.float32
BF16 = jnp.bfloat16
ANY = pl.BlockSpec(memory_space=pl.ANY)
HBM = pl.BlockSpec(memory_space=pltpu.HBM)
VM = pl.BlockSpec(memory_space=pltpu.VMEM)
SM = pl.BlockSpec(memory_space=pltpu.SMEM)

NT = (((1,), (1,)), ((), ()))
NN = (((1,), (0,)), ((), ()))


def dot(a, b, dims):
    return lax.dot_general(a, b, dims, preferred_element_type=F32)


def struct(shape, dtype):
    return jax.ShapeDtypeStruct(shape, dtype)


def copy_all(pairs, sem):
    return [pltpu.make_async_copy(a, b, sem.at[n]) for n, (a, b) in enumerate(pairs)]


def pack_keys_kernel(k_ref, v_ref, kv_ref, sem):
    copies = copy_all(
        [(k_ref, kv_ref.at[:, pl.ds(0, HD)]), (v_ref, kv_ref.at[:, pl.ds(HD, HD)])], sem
    )
    for c in copies:
        c.start()
    for c in copies:
        c.wait()


def pack_queries_kernel(q_ref, do_ref, o_ref, qdo_ref, o_buf, sem):
    copies = copy_all(
        [
            (do_ref, qdo_ref.at[pl.ds(BLK, BLK)]),
            (o_ref, o_buf),
            (q_ref, qdo_ref.at[pl.ds(0, BLK)]),
        ],
        sem,
    )
    for c in copies:
        c.start()
    for c in copies[:2]:
        c.wait()
    prod = qdo_ref[BLK : 2 * BLK, :].astype(F32) * o_buf[...].astype(F32)
    delta = jnp.concatenate(
        [
            jnp.sum(prod[:, h * HD : (h + 1) * HD].T, axis=0, keepdims=True)
            for h in range(HEADS)
        ],
        axis=1,
    )
    high = delta.astype(BF16).astype(F32)
    rest = delta - high
    mid = rest.astype(BF16).astype(F32)
    low = rest - mid
    row = lax.broadcasted_iota(jnp.int32, (EXTRA, COLS), 0)
    extra = jnp.where(row == 0, high, jnp.where(row == 1, mid, jnp.where(row == 2, low, 0.0)))
    qdo_ref[2 * BLK :, :] = extra.astype(BF16)
    copies[2].wait()


def pack_keys(keys, values):
    return pl.pallas_call(
        pack_keys_kernel,
        out_shape=struct((BLK, 2 * HD), BF16),
        in_specs=[HBM] * 2,
        out_specs=VM,
        scratch_shapes=[pltpu.SemaphoreType.DMA((2,))],
        compiler_params=pltpu.CompilerParams(vmem_limit_bytes=4 * MIB),
    )(*[pltpu.with_memory_space_constraint(a, pltpu.HBM) for a in (keys, values)])


def pack_queries(queries, grad_out, forward_out):
    return pl.pallas_call(
        pack_queries_kernel,
        out_shape=struct((ROWS, COLS), BF16),
        in_specs=[HBM] * 3,
        out_specs=VM,
        scratch_shapes=[pltpu.VMEM((BLK, COLS), BF16), pltpu.SemaphoreType.DMA((3,))],
        compiler_params=pltpu.CompilerParams(vmem_limit_bytes=6 * MIB),
    )(*[pltpu.with_memory_space_constraint(a, pltpu.HBM) for a in (queries, grad_out, forward_out)])


AT_Q, AT_K, AT_G = 1, 1 + N_Q, 1 + N_Q + N_K
LIMITS, TABLE, ALL, FAR, NEAR, PLAN = 0, 128, 192, 256, 288, 320
T_ROW, T_COUNT = 8, 4


def plan_kernel(place, mask_hbm, plan, mask_s, found, sem):
    copy = pltpu.make_async_copy(mask_hbm.at[place[0]], mask_s, sem)
    copy.start()
    copy.wait()

    def row(i, carry):
        at = place[AT_Q + i]
        active = jnp.int32(0)
        for quad in range(N_QUAD):
            seen = jnp.int32(0)
            for a in range(4):
                level = mask_s[at, place[AT_K + 4 * quad + a]]
                plan[LIMITS + i * N_K + 4 * quad + a] = jnp.where(
                    level == 1, -BLK, jnp.where(level == 2, 0, BLK)
                )
                seen = seen | level
            plan[TABLE + i * T_ROW + active] = quad
            active += jnp.where(seen != 0, 1, 0)
        plan[TABLE + i * T_ROW + T_COUNT] = active
        return carry

    lax.fori_loop(0, N_Q, row, 0)

    n = jnp.int32(0)
    for i in range(N_Q):
        count = plan[TABLE + i * T_ROW + T_COUNT]
        for j in range(2):
            plan[ALL + 2 + n] = plan[TABLE + i * T_ROW + 2 * j] * N_Q + i
            plan[ALL + 3 + n] = plan[TABLE + i * T_ROW + 2 * j + 1] * N_Q + i
            n += jnp.where(count >= 2 * j + 2, 2, 0)
    plan[ALL] = n // 2
    for i in range(N_Q):
        count = plan[TABLE + i * T_ROW + T_COUNT]
        plan[ALL + 2 + n] = plan[TABLE + i * T_ROW + jnp.maximum(count - 1, 0)] * N_Q + i
        n += count % 2
    plan[ALL + 1] = n

    for base, quads in ((NEAR, (0, 1)), (FAR, (2, 3))):
        n = jnp.int32(0)
        for i in range(N_Q):
            has = [jnp.int32(0), jnp.int32(0)]
            for k in range(2):
                for a in range(N_QUAD):
                    here = (plan[TABLE + i * T_ROW + a] == quads[k]) & (
                        a < plan[TABLE + i * T_ROW + T_COUNT]
                    )
                    has[k] = has[k] | jnp.where(here, 1, 0)
            found[2 * i] = has[0]
            found[2 * i + 1] = has[1]
            plan[base + 2 + n] = quads[0] * N_Q + i
            plan[base + 3 + n] = quads[1] * N_Q + i
            n += 2 * (has[0] & has[1])
        plan[base] = n // 2
        for i in range(N_Q):
            plan[base + 2 + n] = (quads[0] + found[2 * i + 1]) * N_Q + i
            n += found[2 * i] ^ found[2 * i + 1]
        plan[base + 1] = n


def run_plan(place, mask):
    return pl.pallas_call(
        plan_kernel,
        out_shape=struct((PLAN,), jnp.int32),
        in_specs=[SM, HBM],
        out_specs=SM,
        scratch_shapes=[
            pltpu.SMEM((BLK, BLK), jnp.int32),
            pltpu.SMEM((32,), jnp.int32),
            pltpu.SemaphoreType.DMA(()),
        ],
        compiler_params=pltpu.CompilerParams(vmem_limit_bytes=4 * MIB),
    )(place, mask)


def queries_of(near, far, i):
    at = (i % 4) * ROWS
    return (near, far)[i // 4][at : at + BLK]


def grads_of(near, far, i):
    at = (i % 4) * ROWS + BLK
    return (near, far)[i // 4][at : at + D_ROWS]


def fill_quads(kvs, cols, buf):
    for quad in range(N_QUAD):
        for odd in range(2):
            at = slice((quad % 2) * WIDE, (quad % 2 + 1) * WIDE)
            buf[quad, odd * WIDE : (odd + 1) * WIDE] = kvs[2 * (quad // 2) + odd][at, cols]


def join(parts, axis=0):
    return parts[0] if len(parts) == 1 else jnp.concatenate(parts, axis=axis)


def heads(ref, i):
    return jnp.concatenate([ref[i, :BLK, h * HD : (h + 1) * HD] for h in range(HEADS)], axis=0)


E_SLOTS = 8


def scores_kernel(
    place, plan, near, far, kv0, kv1, kv2, kv3,
    e_hbm, stats_hbm,
    qs, ks, sc, ebuf, mx, lacc, st, count, e_sem, st_sem,
):
    count[0] = 0
    fill_quads((kv0, kv1, kv2, kv3), slice(0, HD), ks)
    for i in range(N_Q):
        qs[i] = queries_of(near, far, i)
    diff = (
        lax.broadcasted_iota(jnp.int32, (BLK, WIDE), 1) % BLK
        - lax.broadcasted_iota(jnp.int32, (BLK, WIDE), 0)
    )

    def out_copy(slot, unit):
        return pltpu.make_async_copy(ebuf.at[slot], e_hbm.at[unit], e_sem.at[slot])

    def query_block(i, carry):
        base = TABLE + i * T_ROW
        active = plan[base + T_COUNT]
        mx[...] = jnp.full(mx.shape, NEGATIVE, F32)
        lacc[...] = jnp.zeros(lacc.shape, F32)

        def score_quads(quads):
            joined = dot(join([ks[quad] for quad in quads]), heads(qs, i), NT)
            for hp in range(2):
                cols = slice(hp * WIDE, (hp + 1) * WIDE)
                best = mx[:, cols]
                for k, quad in enumerate(quads):
                    for a in range(4):
                        at = slice(a * BLK, (a + 1) * BLK)
                        s = joined[k * QUAD + a * BLK : k * QUAD + (a + 1) * BLK, cols]
                        limit = plan[LIMITS + i * N_K + 4 * quad + a]
                        part = jnp.where(diff >= limit, s, NEGATIVE)
                        sc[quad, at, cols] = part
                        best = jnp.maximum(
                            best, jnp.max(part.reshape(BLK // 8, 8, WIDE), axis=0)
                        )
                mx[:, cols] = best

        def score_pair(n, carry):
            score_quads([plan[base + 2 * n], plan[base + 2 * n + 1]])
            return carry

        lax.fori_loop(0, active // 2, score_pair, 0)

        @pl.when(active % 2 == 1)
        def _():
            score_quads([plan[base + active - 1]])

        m = jnp.maximum(jnp.max(mx[...], axis=0, keepdims=True), FLOOR)

        def exp_quad(k, carry):
            quad = plan[base + k]
            n = count[0]
            slot = n % E_SLOTS

            @pl.when(n >= E_SLOTS)
            def _():
                out_copy(slot, 0).wait()

            for hp in range(2):
                cols = slice(hp * WIDE, (hp + 1) * WIDE)
                e = jnp.exp2((sc[quad, :, cols] - m[:, cols]) * EXP_SCALE)
                lacc[:, cols] += jnp.sum(e.reshape(QUAD // 8, 8, WIDE), axis=0)
                ebuf[slot, :, cols] = e.astype(BF16)
            out_copy(slot, quad * N_Q + i).start()
            count[0] = n + 1
            return carry

        lax.fori_loop(0, active, exp_quad, 0)
        g = place[AT_G + i]
        st[pl.ds(g, 1), :] = m
        st[pl.ds(N_Q + g, 1), :] = jnp.sum(lacc[...], axis=0, keepdims=True)
        return carry

    lax.fori_loop(0, N_Q, query_block, 0)

    st_copies = copy_all([(st, stats_hbm.at[g]) for g in range(N_Q)], st_sem)
    for c in st_copies:
        c.start()
    for c in st_copies:
        c.wait()
    for slot_no in range(E_SLOTS):

        @pl.when(count[0] > slot_no)
        def _():
            out_copy(slot_no, 0).wait()


def run_scores(place, plan, near, far, kvs):
    return pl.pallas_call(
        scores_kernel,
        out_shape=[
            pltpu.HBM((N_QUAD * N_Q, QUAD, COLS), BF16),
            pltpu.HBM((N_Q, 2 * N_Q, COLS), F32),
        ],
        in_specs=[SM, SM] + [VM] * 6,
        out_specs=[HBM, HBM],
        scratch_shapes=[
            pltpu.VMEM((N_Q, BLK, COLS), BF16),
            pltpu.VMEM((N_QUAD, QUAD, HD), BF16),
            pltpu.VMEM((N_QUAD, QUAD, COLS), F32),
            pltpu.VMEM((E_SLOTS, QUAD, COLS), BF16),
            pltpu.VMEM((8, COLS), F32),
            pltpu.VMEM((8, COLS), F32),
            pltpu.VMEM((2 * N_Q, COLS), F32),
            pltpu.SMEM((1,), jnp.int32),
            pltpu.SemaphoreType.DMA((E_SLOTS,)),
            pltpu.SemaphoreType.DMA((N_Q,)),
        ],
        compiler_params=pltpu.CompilerParams(vmem_limit_bytes=22 * MIB),
    )(place, plan, near, far, *kvs)


DEPTH, AHEAD = 8, 6


def loop_units(plan, base, visit):
    pairs, total = plan[base], plan[base + 1]

    def pair(n, carry):
        visit(2 * n, 2)
        return carry

    def single(n, carry):
        visit(n, 1)
        return carry

    lax.fori_loop(0, pairs, pair, 0)
    lax.fori_loop(2 * pairs, total, single, 0)


def prefetch(plan, base, copies, first, number):
    total = plan[base + 1]
    for k in range(number):

        @pl.when(first + k + AHEAD < total)
        def _():
            for c in copies(first + k + AHEAD):
                c.start()

    for k in range(number):
        for c in copies(first + k):
            c.wait()


def start_first(plan, base, copies):
    for n in range(AHEAD):

        @pl.when(n < plan[base + 1])
        def _():
            for c in copies(n):
                c.start()


def parts_kernel(
    place, plan, near, far, kv0, kv1, kv2, kv3, e_hbm,
    u_hbm, dq_hbm,
    ds, ks, vs, kts, ebuf, ubuf, dqs, dq_low, e_sem, u_sem, dq_sem,
):
    def in_copies(n):
        unit, at = plan[ALL + 2 + n], n % DEPTH
        return (pltpu.make_async_copy(e_hbm.at[unit], ebuf.at[at], e_sem.at[at]),)

    def out_copy(n, unit):
        at = n % DEPTH
        return pltpu.make_async_copy(ubuf.at[at], u_hbm.at[unit], u_sem.at[at])

    start_first(plan, ALL, in_copies)
    kvs = (kv0, kv1, kv2, kv3)
    fill_quads(kvs, slice(0, HD), ks)
    fill_quads(kvs, slice(HD, 2 * HD), vs)
    for i in range(N_Q):
        ds[i] = grads_of(near, far, i)
    dqs[...] = jnp.zeros(dqs.shape, F32)
    for quad in range(N_QUAD):
        kts[quad] = ks[quad].T

    def visit(first, number):
        units = [plan[ALL + 2 + first + k] for k in range(number)]
        i = units[0] % N_Q
        for k in range(number):

            @pl.when(first + k >= DEPTH)
            def _():
                out_copy(first + k, 0).wait()

        prefetch(plan, ALL, in_copies, first, number)
        extra = ds[i, BLK:, :].astype(F32)
        delta = extra[0:1] + extra[1:2] + extra[2:3]
        quads = [unit // N_Q for unit in units]
        da = dot(join([vs[quad] for quad in quads]), heads(ds, i), NT)
        us = []
        for k in range(number):
            at = (first + k) % DEPTH
            u = (ebuf[at].astype(F32) * (da[k * QUAD : (k + 1) * QUAD] - delta)).astype(BF16)
            ubuf[at] = u
            us.append(u)
        dqs[i] += dot(join([kts[quad] for quad in quads], axis=1), join(us), NN)
        for k in range(number):
            out_copy(first + k, units[k]).start()

    loop_units(plan, ALL, visit)
    dq_copies = copy_all([(dq_low.at[i], dq_hbm.at[place[AT_G + i]]) for i in range(N_Q)], dq_sem)
    for i in range(N_Q):
        dq_low[i] = dqs[i].astype(BF16)
        dq_copies[i].start()
    for c in dq_copies:
        c.wait()
    for n in range(DEPTH):

        @pl.when(n < plan[ALL + 1])
        def _():
            out_copy(n, 0).wait()


def run_parts(place, plan, near, far, kvs, e):
    dma = pltpu.SemaphoreType.DMA
    return pl.pallas_call(
        parts_kernel,
        out_shape=[
            pltpu.HBM((N_QUAD * N_Q, QUAD, COLS), BF16),
            pltpu.HBM((N_Q, HD, COLS), BF16),
        ],
        in_specs=[SM, SM] + [VM] * 6 + [HBM],
        out_specs=[HBM, HBM],
        scratch_shapes=[
            pltpu.VMEM((N_Q, D_ROWS, COLS), BF16),
            pltpu.VMEM((N_QUAD, QUAD, HD), BF16),
            pltpu.VMEM((N_QUAD, QUAD, HD), BF16),
            pltpu.VMEM((N_QUAD, HD, QUAD), BF16),
            pltpu.VMEM((DEPTH, QUAD, COLS), BF16),
            pltpu.VMEM((DEPTH, QUAD, COLS), BF16),
            pltpu.VMEM((N_Q, HD, COLS), F32),
            pltpu.VMEM((N_Q, HD, COLS), BF16),
            dma((DEPTH,)),
            dma((DEPTH,)),
            dma((N_Q,)),
        ],
        compiler_params=pltpu.CompilerParams(vmem_limit_bytes=28 * MIB),
    )(place, plan, near, far, *kvs, e)


def row_weights(place, stats, near, far, ws, wq, wdo):
    ms = [stats[j, :N_Q, :] for j in range(N_Q)]
    top = functools.reduce(jnp.maximum, ms)
    tot = sum(stats[j, N_Q:, :] * jnp.exp2((ms[j] - top) * EXP_SCALE) for j in range(N_Q))
    ws[...] = jnp.exp2((stats[place[AT_G], :N_Q, :] - top) * EXP_SCALE) / tot
    rows = []
    for i in range(N_Q):
        w = ws[pl.ds(place[AT_G + i], 1), :]
        rows += [w[:, h * BLK : (h + 1) * BLK] for h in range(HEADS)]
    rows.append(jnp.zeros((BLK - len(rows), BLK), F32))
    cols = jnp.concatenate(rows, axis=0).T
    for i in range(N_Q):
        q = queries_of(near, far, i)
        do = grads_of(near, far, i)
        for h in range(HEADS):
            w = cols[:, i * HEADS + h : i * HEADS + h + 1]
            at = slice(h * BLK, (h + 1) * BLK)
            c = slice(h * HD, (h + 1) * HD)
            wq[i, at, :] = (q[:, c].astype(F32) * w).astype(BF16)
            wdo[i, at, :] = (do[:BLK, c].astype(F32) * w).astype(BF16)


def sum_keys(plan, base, first_quad, rows, wq, wdo, e_hbm, u_hbm, acc, bufs):
    ebuf, ubuf, e_sem, u_sem = bufs
    size = acc.shape[1]

    def in_copies(n):
        unit, at = plan[base + 2 + n], n % DEPTH
        return [
            pltpu.make_async_copy(
                hbm.at[unit, pl.ds(rows, size)], buf.at[at, pl.ds(0, size)], sem.at[at]
            )
            for hbm, buf, sem in ((e_hbm, ebuf, e_sem), (u_hbm, ubuf, u_sem))
        ]

    start_first(plan, base, in_copies)
    acc[...] = jnp.zeros(acc.shape, F32)

    def visit(first, number):
        unit = plan[base + 2 + first]
        i, quad = unit % N_Q, unit // N_Q - first_quad
        prefetch(plan, base, in_copies, first, number)
        for buf, w, cols in ((ubuf, wq, slice(0, HD)), (ebuf, wdo, slice(HD, 2 * HD))):
            joined = dot(
                join([buf[(first + k) % DEPTH, :size] for k in range(number)]), w[i], NN
            )
            for k in range(number):
                acc[quad + k, :, cols] += joined[k * size : (k + 1) * size]

    return lambda: loop_units(plan, base, visit)


def far_kernel(
    place, plan, stats, near, far, e_hbm, u_hbm,
    out1, out2, out3, wq_hbm, wdo_hbm,
    ws, wq, wdo, acc, acc_odd, w_sem, *bufs,
):
    w_copies = copy_all([(wq, wq_hbm), (wdo, wdo_hbm)], w_sem)

    sum_far = sum_keys(plan, FAR, 2, 0, wq, wdo, e_hbm, u_hbm, acc, bufs[:4])
    sum_odd = sum_keys(plan, NEAR, 0, WIDE, wq, wdo, e_hbm, u_hbm, acc_odd, bufs[4:])
    row_weights(place, stats, near, far, ws, wq, wdo)
    for c in w_copies:
        c.start()
    sum_far()
    sum_odd()
    for quad in range(2):
        at = slice(quad * WIDE, (quad + 1) * WIDE)
        out1[at, :] = acc_odd[quad].astype(BF16)
        out2[at, :] = acc[quad, :WIDE].astype(BF16)
        out3[at, :] = acc[quad, WIDE:].astype(BF16)
    for c in w_copies:
        c.wait()


def own_kernel(plan, wq_hbm, wdo_hbm, e_hbm, u_hbm, out, wq, wdo, acc, w_sem, *bufs):
    w_copies = copy_all([(wq_hbm, wq), (wdo_hbm, wdo)], w_sem)
    for c in w_copies:
        c.start()

    sum_own = sum_keys(plan, NEAR, 0, 0, wq, wdo, e_hbm, u_hbm, acc, bufs)
    for c in w_copies:
        c.wait()
    sum_own()
    for quad in range(2):
        out[quad * WIDE : (quad + 1) * WIDE, :] = acc[quad]


def keys_bufs(rows):
    return [
        pltpu.VMEM((DEPTH, rows, COLS), BF16),
        pltpu.VMEM((DEPTH, rows, COLS), BF16),
        pltpu.SemaphoreType.DMA((DEPTH,)),
        pltpu.SemaphoreType.DMA((DEPTH,)),
    ]


def run_far(place, plan, stats, near, far, e, u):
    return pl.pallas_call(
        far_kernel,
        out_shape=[struct((QUAD, 2 * HD), BF16)] * 3 + [pltpu.HBM((N_Q, COLS, HD), BF16)] * 2,
        in_specs=[SM, SM] + [VM] * 3 + [HBM, HBM],
        out_specs=[VM] * 3 + [HBM] * 2,
        scratch_shapes=[
            pltpu.VMEM((N_Q, COLS), F32),
            pltpu.VMEM((N_Q, COLS, HD), BF16),
            pltpu.VMEM((N_Q, COLS, HD), BF16),
            pltpu.VMEM((2, QUAD, 2 * HD), F32),
            pltpu.VMEM((2, WIDE, 2 * HD), F32),
            pltpu.SemaphoreType.DMA((2,)),
        ]
        + keys_bufs(QUAD)
        + keys_bufs(WIDE),
        compiler_params=pltpu.CompilerParams(vmem_limit_bytes=24 * MIB),
    )(place, plan, stats, near, far, e, u)


def run_own(plan, wq, wdo, e, u):
    return pl.pallas_call(
        own_kernel,
        out_shape=struct((QUAD, 2 * HD), F32),
        in_specs=[SM] + [HBM] * 4,
        out_specs=VM,
        scratch_shapes=[
            pltpu.VMEM((N_Q, COLS, HD), BF16),
            pltpu.VMEM((N_Q, COLS, HD), BF16),
            pltpu.VMEM((2, WIDE, 2 * HD), F32),
            pltpu.SemaphoreType.DMA((2,)),
        ]
        + keys_bufs(WIDE),
        compiler_params=pltpu.CompilerParams(vmem_limit_bytes=14 * MIB),
    )(plan, wq, wdo, e, u)


def sum_kernel(own, a, b, c, out0, out1, out2, out3):
    for d, out in enumerate((out0, out1, out2, out3)):
        at = slice(d * BLK, (d + 1) * BLK)
        total = own[at] + a[at].astype(F32) + b[at].astype(F32) + c[at].astype(F32)
        out[...] = total.astype(out.dtype)


def run_sum(own, a, b, c):
    return pl.pallas_call(
        sum_kernel,
        out_shape=[struct((BLK, 2 * HD), F32)] + [struct((BLK, 2 * HD), BF16)] * 3,
        in_specs=[VM] * 4,
        out_specs=[VM] * 4,
        compiler_params=pltpu.CompilerParams(vmem_limit_bytes=6 * MIB),
    )(own, a, b, c)


def queries_kernel(place, parts, stats, out):
    own = place[AT_G]
    ms = [stats[j, pl.ds(own, 1), :] for j in range(N_Q)]
    ls = [stats[j, pl.ds(N_Q + own, 1), :] for j in range(N_Q)]
    top = functools.reduce(jnp.maximum, ms)
    es = [jnp.exp2((m - top) * EXP_SCALE) for m in ms]
    tot = sum(l * e for l, e in zip(ls, es))
    for h in range(HEADS):
        at = slice(h * HD, (h + 1) * HD)
        total = sum(parts[j, :, at].astype(F32) * es[j][:, at] for j in range(N_Q))
        out[:, at] = (total * (SCALING / tot[:, at])).T


def run_queries(place, parts, stats):
    return pl.pallas_call(
        queries_kernel,
        out_shape=struct((BLK, COLS), F32),
        in_specs=[SM, VM, VM],
        out_specs=VM,
        compiler_params=pltpu.CompilerParams(vmem_limit_bytes=6 * MIB),
    )(place, parts, stats)


def exchange(x, dx=0, dz=0, dy=0, dc=0):
    perm = []
    for b in range(16):
        for r in range(16):
            px = (b // 8) * 2 + (r // 2) % 2
            pz, py, pc = b % 8, r // 4, r % 2
            px, pz, py, pc = px ^ dx, pz ^ (2 * dz), py ^ dy, pc ^ dc
            other = (px // 2) * 8 + pz, py * 4 + (px % 2) * 2 + pc
            perm.append((b * 16 + r, other[0] * 16 + other[1]))
    return lax.ppermute(x, ("blk", "rows"), perm)


Q_GROUPS = [[r for r in range(16) if (r // 2) % 2 == lo] for lo in range(2)]


def to_group(x):
    return lax.all_to_all(x, "rows", 0, 0, axis_index_groups=Q_GROUPS, tiled=True)


def per_device(queries, keys, values, forward_out, grad_out, block_mask):
    b, r = lax.axis_index("blk"), lax.axis_index("rows")
    x = ((b >> 3) << 1) | ((r >> 1) & 1)
    zz, y, core = (b >> 1) & 3, r >> 2, r & 1
    slot_q = jnp.arange(N_Q)
    yq, cq = y ^ (slot_q & 3), core ^ (slot_q >> 2)
    q_blocks = ((b >> 1) << 4) + (yq << 2) + ((x & 1) << 1) + cq
    slot_k = jnp.arange(N_K)
    quad, a = slot_k >> 2, slot_k & 3
    xk = x ^ (((quad >> 1) << 1) | (a >> 1))
    zk = zz ^ (((quad & 1) << 1) | (a & 1))
    k_blocks = ((((xk >> 1) << 2) + zk) << 4) + (y << 2) + ((xk & 1) << 1) + core
    place = jnp.concatenate([(b & 1)[None], q_blocks, k_blocks, (yq << 1) + cq]).astype(jnp.int32)

    kv = pack_keys(keys, values)
    kv, queries = lax.optimization_barrier((kv, queries))
    qdo = pack_queries(queries, grad_out, forward_out)

    kv_z = jnp.concatenate([kv] + [exchange(kv, dz=d) for d in (1, 2, 3)], axis=0)
    kvs = [kv_z] + [exchange(kv_z, dx=d) for d in (1, 2, 3)]
    others = [exchange(qdo, dy=d) for d in (1, 2, 3)]
    plan = run_plan(place, pltpu.with_memory_space_constraint(block_mask, pltpu.HBM))
    *others, k1, k2, k3, plan = lax.optimization_barrier((*others, *kvs[1:], plan))
    kvs = [kv_z, k1, k2, k3]
    near = jnp.concatenate([qdo, *others], axis=0)
    far = exchange(near, dc=1)

    e, stat = run_scores(place, plan, near, far, kvs)
    e = pltpu.with_memory_space_constraint(e, pltpu.HBM)
    stats = to_group(stat)
    u, dq = run_parts(place, plan, near, far, kvs, e)
    u = pltpu.with_memory_space_constraint(u, pltpu.HBM)
    dq_parts = to_group(dq)
    *remote, wq, wdo = run_far(place, plan, stats, near, far, e, u)
    wq, wdo = [pltpu.with_memory_space_constraint(w, pltpu.HBM) for w in (wq, wdo)]
    got1, got2, got3 = [exchange(f, dx=d) for d, f in zip((1, 2, 3), remote)]
    wq, dq_parts = lax.optimization_barrier((wq, dq_parts))
    own = run_own(plan, wq, wdo, e, u)
    mine, *rest = run_sum(own, got1, got2, got3)
    back = [exchange(part, dz=d) for d, part in zip((1, 2, 3), rest)]
    grad_queries = run_queries(place, dq_parts, stats)
    total = mine + sum(part.astype(F32) for part in back)
    return grad_queries, total[:, :HD] * SCALING, total[:, HD:]


def solution(mesh):
    spec = P(("blk", "rows"), None)
    return jax.shard_map(
        per_device,
        mesh=mesh,
        in_specs=(spec, spec, spec, spec, spec, P()),
        out_specs=(spec, spec, spec),
        check_vma=False,
    )
```

```python
import functools
import math

import jax
import jax.numpy as jnp
from jax import lax
from jax.experimental import pallas as pl
from jax.experimental.pallas import tpu as pltpu
from jax.sharding import PartitionSpec as P

BLK = 128
HEADS = 4
HD = 128
COLS = HEADS * HD
N_Q = 8
N_K = 16
N_QUAD = N_K // 4
QUAD = 4 * BLK
WIDE = 2 * BLK
EXTRA = 16
D_ROWS = BLK + EXTRA
ROWS = BLK + D_ROWS
NEGATIVE = -1e30
FLOOR = -1e6
SCALING = 1.0 / math.sqrt(HD)
EXP_SCALE = SCALING * math.log2(math.e)
MIB = 1024 * 1024
F32 = jnp.float32
BF16 = jnp.bfloat16
ANY = pl.BlockSpec(memory_space=pl.ANY)
HBM = pl.BlockSpec(memory_space=pltpu.HBM)
VM = pl.BlockSpec(memory_space=pltpu.VMEM)
SM = pl.BlockSpec(memory_space=pltpu.SMEM)

NT = (((1,), (1,)), ((), ()))
NN = (((1,), (0,)), ((), ()))


def dot(a, b, dims):
    return lax.dot_general(a, b, dims, preferred_element_type=F32)


def struct(shape, dtype):
    return jax.ShapeDtypeStruct(shape, dtype)


def copy_all(pairs, sem):
    return [pltpu.make_async_copy(a, b, sem.at[n]) for n, (a, b) in enumerate(pairs)]


def pack_keys_kernel(k_ref, v_ref, kv_ref, sem):
    copies = copy_all(
        [(k_ref, kv_ref.at[:, pl.ds(0, HD)]), (v_ref, kv_ref.at[:, pl.ds(HD, HD)])], sem
    )
    for c in copies:
        c.start()
    for c in copies:
        c.wait()


def pack_queries_kernel(q_ref, do_ref, o_ref, qdo_ref, o_buf, sem):
    copies = copy_all(
        [
            (do_ref, qdo_ref.at[pl.ds(BLK, BLK)]),
            (o_ref, o_buf),
            (q_ref, qdo_ref.at[pl.ds(0, BLK)]),
        ],
        sem,
    )
    for c in copies:
        c.start()
    for c in copies[:2]:
        c.wait()
    prod = qdo_ref[BLK : 2 * BLK, :].astype(F32) * o_buf[...].astype(F32)
    delta = jnp.concatenate(
        [
            jnp.sum(prod[:, h * HD : (h + 1) * HD].T, axis=0, keepdims=True)
            for h in range(HEADS)
        ],
        axis=1,
    )
    high = delta.astype(BF16).astype(F32)
    rest = delta - high
    mid = rest.astype(BF16).astype(F32)
    low = rest - mid
    row = lax.broadcasted_iota(jnp.int32, (EXTRA, COLS), 0)
    extra = jnp.where(row == 0, high, jnp.where(row == 1, mid, jnp.where(row == 2, low, 0.0)))
    qdo_ref[2 * BLK :, :] = extra.astype(BF16)
    copies[2].wait()


def pack_keys(keys, values):
    return pl.pallas_call(
        pack_keys_kernel,
        out_shape=struct((BLK, 2 * HD), BF16),
        in_specs=[HBM] * 2,
        out_specs=VM,
        scratch_shapes=[pltpu.SemaphoreType.DMA((2,))],
        compiler_params=pltpu.CompilerParams(vmem_limit_bytes=4 * MIB),
    )(*[pltpu.with_memory_space_constraint(a, pltpu.HBM) for a in (keys, values)])


def pack_queries(queries, grad_out, forward_out):
    return pl.pallas_call(
        pack_queries_kernel,
        out_shape=struct((ROWS, COLS), BF16),
        in_specs=[HBM] * 3,
        out_specs=VM,
        scratch_shapes=[pltpu.VMEM((BLK, COLS), BF16), pltpu.SemaphoreType.DMA((3,))],
        compiler_params=pltpu.CompilerParams(vmem_limit_bytes=6 * MIB),
    )(*[pltpu.with_memory_space_constraint(a, pltpu.HBM) for a in (queries, grad_out, forward_out)])


AT_Q, AT_K, AT_G, AT_OWN = 1, 1 + N_Q, 1 + N_Q + N_K, 1 + 2 * N_Q + N_K
LIMITS, TABLE, ALL, FAR, NEAR, PLAN = 0, 128, 192, 256, 288, 320
T_ROW, T_COUNT = 8, 4


def plan_kernel(place, mask_hbm, plan, mask_s, found, sem):
    copy = pltpu.make_async_copy(mask_hbm.at[place[0]], mask_s, sem)
    copy.start()
    copy.wait()

    def row(i, carry):
        at = place[AT_Q + i]
        active = jnp.int32(0)
        for quad in range(N_QUAD):
            seen = jnp.int32(0)
            for a in range(4):
                level = mask_s[at, place[AT_K + 4 * quad + a]]
                plan[LIMITS + i * N_K + 4 * quad + a] = jnp.where(
                    level == 1, -BLK, jnp.where(level == 2, 0, BLK)
                )
                seen = seen | level
            plan[TABLE + i * T_ROW + active] = quad
            active += jnp.where(seen != 0, 1, 0)
        plan[TABLE + i * T_ROW + T_COUNT] = active
        return carry

    lax.fori_loop(0, N_Q, row, 0)

    n = jnp.int32(0)
    for i in range(N_Q):
        count = plan[TABLE + i * T_ROW + T_COUNT]
        for j in range(2):
            plan[ALL + 2 + n] = plan[TABLE + i * T_ROW + 2 * j] * N_Q + i
            plan[ALL + 3 + n] = plan[TABLE + i * T_ROW + 2 * j + 1] * N_Q + i
            n += jnp.where(count >= 2 * j + 2, 2, 0)
    plan[ALL] = n // 2
    for i in range(N_Q):
        count = plan[TABLE + i * T_ROW + T_COUNT]
        plan[ALL + 2 + n] = plan[TABLE + i * T_ROW + jnp.maximum(count - 1, 0)] * N_Q + i
        n += count % 2
    plan[ALL + 1] = n

    for base, quads in ((NEAR, (0, 1)), (FAR, (2, 3))):
        n = jnp.int32(0)
        for i in range(N_Q):
            has = [jnp.int32(0), jnp.int32(0)]
            for k in range(2):
                for a in range(N_QUAD):
                    here = (plan[TABLE + i * T_ROW + a] == quads[k]) & (
                        a < plan[TABLE + i * T_ROW + T_COUNT]
                    )
                    has[k] = has[k] | jnp.where(here, 1, 0)
            found[2 * i] = has[0]
            found[2 * i + 1] = has[1]
            plan[base + 2 + n] = quads[0] * N_Q + i
            plan[base + 3 + n] = quads[1] * N_Q + i
            n += 2 * (has[0] & has[1])
        plan[base] = n // 2
        for i in range(N_Q):
            plan[base + 2 + n] = (quads[0] + found[2 * i + 1]) * N_Q + i
            n += found[2 * i] ^ found[2 * i + 1]
        plan[base + 1] = n


def run_plan(place, mask):
    return pl.pallas_call(
        plan_kernel,
        out_shape=struct((PLAN,), jnp.int32),
        in_specs=[SM, HBM],
        out_specs=SM,
        scratch_shapes=[
            pltpu.SMEM((BLK, BLK), jnp.int32),
            pltpu.SMEM((32,), jnp.int32),
            pltpu.SemaphoreType.DMA(()),
        ],
        compiler_params=pltpu.CompilerParams(vmem_limit_bytes=4 * MIB),
    )(place, mask)


def queries_of(near, far, i):
    at = (i % 4) * ROWS
    return (near, far)[i // 4][at : at + BLK]


def grads_of(near, far, i):
    at = (i % 4) * ROWS + BLK
    return (near, far)[i // 4][at : at + D_ROWS]


def fill_quads(kvs, cols, buf):
    for quad in range(N_QUAD):
        for odd in range(2):
            at = slice((quad % 2) * WIDE, (quad % 2 + 1) * WIDE)
            buf[quad, odd * WIDE : (odd + 1) * WIDE] = kvs[2 * (quad // 2) + odd][at, cols]


def join(parts, axis=0):
    return parts[0] if len(parts) == 1 else jnp.concatenate(parts, axis=axis)


def heads(ref, i):
    return jnp.concatenate([ref[i, :BLK, h * HD : (h + 1) * HD] for h in range(HEADS)], axis=0)


E_SLOTS = 8


def scores_kernel(
    place, plan, near, far, kv0, kv1, kv2, kv3,
    e_hbm, stats_hbm,
    qs, ks, sc, ebuf, mx, lacc, st, count, e_sem, st_sem,
):
    count[0] = 0
    fill_quads((kv0, kv1, kv2, kv3), slice(0, HD), ks)
    for i in range(N_Q):
        qs[i] = queries_of(near, far, i)
    diff = (
        lax.broadcasted_iota(jnp.int32, (BLK, WIDE), 1) % BLK
        - lax.broadcasted_iota(jnp.int32, (BLK, WIDE), 0)
    )

    def out_copy(slot, unit):
        return pltpu.make_async_copy(ebuf.at[slot], e_hbm.at[unit], e_sem.at[slot])

    def query_block(i, carry):
        base = TABLE + i * T_ROW
        active = plan[base + T_COUNT]
        mx[...] = jnp.full(mx.shape, NEGATIVE, F32)
        lacc[...] = jnp.zeros(lacc.shape, F32)

        def score_quads(quads):
            limits = [plan[LIMITS + i * N_K + 4 * quad + a] for quad in quads for a in range(4)]
            masked = functools.reduce(jnp.maximum, limits) > -BLK

            @pl.when(masked)
            def _():
                score(quads, limits)

            @pl.when(jnp.logical_not(masked))
            def _():
                score(quads, None)

        def score(quads, limits):
            joined = dot(join([ks[quad] for quad in quads]), heads(qs, i), NT)
            for hp in range(2):
                cols = slice(hp * WIDE, (hp + 1) * WIDE)
                best = mx[:, cols]
                for k, quad in enumerate(quads):
                    for a in range(4):
                        at = slice(a * BLK, (a + 1) * BLK)
                        s = joined[k * QUAD + a * BLK : k * QUAD + (a + 1) * BLK, cols]
                        part = s
                        if limits is not None:
                            part = jnp.where(diff >= limits[4 * k + a], s, NEGATIVE)
                        sc[quad, at, cols] = part
                        best = jnp.maximum(
                            best, jnp.max(part.reshape(BLK // 8, 8, WIDE), axis=0)
                        )
                mx[:, cols] = best

        def score_pair(n, carry):
            score_quads([plan[base + 2 * n], plan[base + 2 * n + 1]])
            return carry

        lax.fori_loop(0, active // 2, score_pair, 0)

        @pl.when(active % 2 == 1)
        def _():
            score_quads([plan[base + active - 1]])

        m = jnp.maximum(jnp.max(mx[...], axis=0, keepdims=True), FLOOR)

        def exp_quad(k, carry):
            quad = plan[base + k]
            n = count[0]
            slot = n % E_SLOTS

            @pl.when(n >= E_SLOTS)
            def _():
                out_copy(slot, 0).wait()

            for hp in range(2):
                cols = slice(hp * WIDE, (hp + 1) * WIDE)
                e = jnp.exp2((sc[quad, :, cols] - m[:, cols]) * EXP_SCALE)
                lacc[:, cols] += jnp.sum(e.reshape(QUAD // 8, 8, WIDE), axis=0)
                ebuf[slot, :, cols] = e.astype(BF16)
            out_copy(slot, quad * N_Q + i).start()
            count[0] = n + 1
            return carry

        lax.fori_loop(0, active, exp_quad, 0)
        g = place[AT_G + i]
        st[pl.ds(g, 1), :] = m
        st[pl.ds(N_Q + g, 1), :] = jnp.sum(lacc[...], axis=0, keepdims=True)
        return carry

    lax.fori_loop(0, N_Q, query_block, 0)

    st_copies = copy_all([(st, stats_hbm.at[g]) for g in range(N_Q)], st_sem)
    for c in st_copies:
        c.start()
    for c in st_copies:
        c.wait()
    for slot_no in range(E_SLOTS):

        @pl.when(count[0] > slot_no)
        def _():
            out_copy(slot_no, 0).wait()


def run_scores(place, plan, near, far, kvs):
    return pl.pallas_call(
        scores_kernel,
        out_shape=[
            pltpu.HBM((N_QUAD * N_Q, QUAD, COLS), BF16),
            pltpu.HBM((N_Q, 2 * N_Q, COLS), F32),
        ],
        in_specs=[SM, SM] + [VM] * 6,
        out_specs=[HBM, HBM],
        scratch_shapes=[
            pltpu.VMEM((N_Q, BLK, COLS), BF16),
            pltpu.VMEM((N_QUAD, QUAD, HD), BF16),
            pltpu.VMEM((N_QUAD, QUAD, COLS), F32),
            pltpu.VMEM((E_SLOTS, QUAD, COLS), BF16),
            pltpu.VMEM((8, COLS), F32),
            pltpu.VMEM((8, COLS), F32),
            pltpu.VMEM((2 * N_Q, COLS), F32),
            pltpu.SMEM((1,), jnp.int32),
            pltpu.SemaphoreType.DMA((E_SLOTS,)),
            pltpu.SemaphoreType.DMA((N_Q,)),
        ],
        compiler_params=pltpu.CompilerParams(vmem_limit_bytes=22 * MIB),
    )(place, plan, near, far, *kvs)


DEPTH, AHEAD = 8, 6


def loop_units(plan, base, visit):
    pairs, total = plan[base], plan[base + 1]

    def pair(n, carry):
        visit(2 * n, 2)
        return carry

    def single(n, carry):
        visit(n, 1)
        return carry

    lax.fori_loop(0, pairs, pair, 0)
    lax.fori_loop(2 * pairs, total, single, 0)


def prefetch(plan, base, copies, first, number):
    total = plan[base + 1]
    for k in range(number):

        @pl.when(first + k + AHEAD < total)
        def _():
            for c in copies(first + k + AHEAD):
                c.start()

    for k in range(number):
        for c in copies(first + k):
            c.wait()


def start_first(plan, base, copies):
    for n in range(AHEAD):

        @pl.when(n < plan[base + 1])
        def _():
            for c in copies(n):
                c.start()


def parts_kernel(
    place, plan, near, far, kv0, kv1, kv2, kv3, e_hbm,
    u_hbm, dq_hbm,
    ds, ks, vs, kts, ebuf, ubuf, dqs, dq_low, e_sem, u_sem, dq_sem,
):
    def in_copies(n):
        unit, at = plan[ALL + 2 + n], n % DEPTH
        return (pltpu.make_async_copy(e_hbm.at[unit], ebuf.at[at], e_sem.at[at]),)

    def out_copy(n, unit):
        at = n % DEPTH
        return pltpu.make_async_copy(ubuf.at[at], u_hbm.at[unit], u_sem.at[at])

    start_first(plan, ALL, in_copies)
    kvs = (kv0, kv1, kv2, kv3)
    fill_quads(kvs, slice(0, HD), ks)
    fill_quads(kvs, slice(HD, 2 * HD), vs)
    for i in range(N_Q):
        ds[i] = grads_of(near, far, i)
    dqs[...] = jnp.zeros(dqs.shape, F32)
    for quad in range(N_QUAD):
        kts[quad] = ks[quad].T

    def visit(first, number):
        units = [plan[ALL + 2 + first + k] for k in range(number)]
        i = units[0] % N_Q
        for k in range(number):

            @pl.when(first + k >= DEPTH)
            def _():
                out_copy(first + k, 0).wait()

        prefetch(plan, ALL, in_copies, first, number)
        extra = ds[i, BLK:, :].astype(F32)
        delta = extra[0:1] + extra[1:2] + extra[2:3]
        quads = [unit // N_Q for unit in units]
        da = dot(join([vs[quad] for quad in quads]), heads(ds, i), NT)
        us = []
        for k in range(number):
            at = (first + k) % DEPTH
            u = (ebuf[at].astype(F32) * (da[k * QUAD : (k + 1) * QUAD] - delta)).astype(BF16)
            ubuf[at] = u
            us.append(u)
        dqs[i] += dot(join([kts[quad] for quad in quads], axis=1), join(us), NN)
        for k in range(number):
            out_copy(first + k, units[k]).start()

    loop_units(plan, ALL, visit)
    dq_copies = copy_all([(dq_low.at[i], dq_hbm.at[place[AT_G + i]]) for i in range(N_Q)], dq_sem)
    for i in range(N_Q):
        dq_low[i] = dqs[i].astype(BF16)
        dq_copies[i].start()
    for c in dq_copies:
        c.wait()
    for n in range(DEPTH):

        @pl.when(n < plan[ALL + 1])
        def _():
            out_copy(n, 0).wait()


def run_parts(place, plan, near, far, kvs, e):
    dma = pltpu.SemaphoreType.DMA
    return pl.pallas_call(
        parts_kernel,
        out_shape=[
            pltpu.HBM((N_QUAD * N_Q, QUAD, COLS), BF16),
            pltpu.HBM((N_Q, HD, COLS), BF16),
        ],
        in_specs=[SM, SM] + [VM] * 6 + [HBM],
        out_specs=[HBM, HBM],
        scratch_shapes=[
            pltpu.VMEM((N_Q, D_ROWS, COLS), BF16),
            pltpu.VMEM((N_QUAD, QUAD, HD), BF16),
            pltpu.VMEM((N_QUAD, QUAD, HD), BF16),
            pltpu.VMEM((N_QUAD, HD, QUAD), BF16),
            pltpu.VMEM((DEPTH, QUAD, COLS), BF16),
            pltpu.VMEM((DEPTH, QUAD, COLS), BF16),
            pltpu.VMEM((N_Q, HD, COLS), F32),
            pltpu.VMEM((N_Q, HD, COLS), BF16),
            dma((DEPTH,)),
            dma((DEPTH,)),
            dma((N_Q,)),
        ],
        compiler_params=pltpu.CompilerParams(vmem_limit_bytes=28 * MIB),
    )(place, plan, near, far, *kvs, e)


def row_weights(place, stats, near, far, ws, wq, wdo):
    ms = [stats[j, :N_Q, :] for j in range(N_Q)]
    top = functools.reduce(jnp.maximum, ms)
    tot = sum(stats[j, N_Q:, :] * jnp.exp2((ms[j] - top) * EXP_SCALE) for j in range(N_Q))
    ws[...] = jnp.exp2((stats[place[AT_OWN], :N_Q, :] - top) * EXP_SCALE) / tot
    rows = []
    for i in range(N_Q):
        w = ws[pl.ds(place[AT_G + i], 1), :]
        rows += [w[:, h * BLK : (h + 1) * BLK] for h in range(HEADS)]
    rows.append(jnp.zeros((BLK - len(rows), BLK), F32))
    cols = jnp.concatenate(rows, axis=0).T
    for i in range(N_Q):
        q = queries_of(near, far, i)
        do = grads_of(near, far, i)
        for h in range(HEADS):
            w = cols[:, i * HEADS + h : i * HEADS + h + 1]
            at = slice(h * BLK, (h + 1) * BLK)
            c = slice(h * HD, (h + 1) * HD)
            wq[i, at, :] = (q[:, c].astype(F32) * w).astype(BF16)
            wdo[i, at, :] = (do[:BLK, c].astype(F32) * w).astype(BF16)


def sum_keys(plan, base, first_quad, rows, wq, wdo, e_hbm, u_hbm, acc, bufs):
    ebuf, ubuf, e_sem, u_sem = bufs
    size = acc.shape[1]

    def in_copies(n):
        unit, at = plan[base + 2 + n], n % DEPTH
        return [
            pltpu.make_async_copy(
                hbm.at[unit, pl.ds(rows, size)], buf.at[at, pl.ds(0, size)], sem.at[at]
            )
            for hbm, buf, sem in ((e_hbm, ebuf, e_sem), (u_hbm, ubuf, u_sem))
        ]

    start_first(plan, base, in_copies)
    acc[...] = jnp.zeros(acc.shape, F32)

    def visit(first, number):
        unit = plan[base + 2 + first]
        i, quad = unit % N_Q, unit // N_Q - first_quad
        prefetch(plan, base, in_copies, first, number)
        for buf, w, cols in ((ubuf, wq, slice(0, HD)), (ebuf, wdo, slice(HD, 2 * HD))):
            joined = dot(
                join([buf[(first + k) % DEPTH, :size] for k in range(number)]), w[i], NN
            )
            for k in range(number):
                acc[quad + k, :, cols] += joined[k * size : (k + 1) * size]

    return lambda: loop_units(plan, base, visit)


def far_kernel(
    place, plan, stats, near, far, e_hbm, u_hbm,
    out1, out2, out3, wq_hbm, wdo_hbm,
    ws, wq, wdo, acc, acc_odd, w_sem, *bufs,
):
    w_copies = copy_all([(wq, wq_hbm), (wdo, wdo_hbm)], w_sem)

    sum_far = sum_keys(plan, FAR, 2, 0, wq, wdo, e_hbm, u_hbm, acc, bufs[:4])
    sum_odd = sum_keys(plan, NEAR, 0, WIDE, wq, wdo, e_hbm, u_hbm, acc_odd, bufs[4:])
    row_weights(place, stats, near, far, ws, wq, wdo)
    for c in w_copies:
        c.start()
    sum_far()
    sum_odd()
    for quad in range(2):
        at = slice(quad * WIDE, (quad + 1) * WIDE)
        out1[at, :] = acc_odd[quad].astype(BF16)
        out2[at, :] = acc[quad, :WIDE].astype(BF16)
        out3[at, :] = acc[quad, WIDE:].astype(BF16)
    for c in w_copies:
        c.wait()


def own_kernel(plan, wq_hbm, wdo_hbm, e_hbm, u_hbm, out, wq, wdo, acc, w_sem, *bufs):
    w_copies = copy_all([(wq_hbm, wq), (wdo_hbm, wdo)], w_sem)
    for c in w_copies:
        c.start()

    sum_own = sum_keys(plan, NEAR, 0, 0, wq, wdo, e_hbm, u_hbm, acc, bufs)
    for c in w_copies:
        c.wait()
    sum_own()
    for quad in range(2):
        out[quad * WIDE : (quad + 1) * WIDE, :] = acc[quad]


def keys_bufs(rows):
    return [
        pltpu.VMEM((DEPTH, rows, COLS), BF16),
        pltpu.VMEM((DEPTH, rows, COLS), BF16),
        pltpu.SemaphoreType.DMA((DEPTH,)),
        pltpu.SemaphoreType.DMA((DEPTH,)),
    ]


def run_far(place, plan, stats, near, far, e, u):
    return pl.pallas_call(
        far_kernel,
        out_shape=[struct((QUAD, 2 * HD), BF16)] * 3 + [pltpu.HBM((N_Q, COLS, HD), BF16)] * 2,
        in_specs=[SM, SM] + [VM] * 3 + [HBM, HBM],
        out_specs=[VM] * 3 + [HBM] * 2,
        scratch_shapes=[
            pltpu.VMEM((N_Q, COLS), F32),
            pltpu.VMEM((N_Q, COLS, HD), BF16),
            pltpu.VMEM((N_Q, COLS, HD), BF16),
            pltpu.VMEM((2, QUAD, 2 * HD), F32),
            pltpu.VMEM((2, WIDE, 2 * HD), F32),
            pltpu.SemaphoreType.DMA((2,)),
        ]
        + keys_bufs(QUAD)
        + keys_bufs(WIDE),
        compiler_params=pltpu.CompilerParams(vmem_limit_bytes=24 * MIB),
    )(place, plan, stats, near, far, e, u)


def run_own(plan, wq, wdo, e, u):
    return pl.pallas_call(
        own_kernel,
        out_shape=struct((QUAD, 2 * HD), F32),
        in_specs=[SM] + [HBM] * 4,
        out_specs=VM,
        scratch_shapes=[
            pltpu.VMEM((N_Q, COLS, HD), BF16),
            pltpu.VMEM((N_Q, COLS, HD), BF16),
            pltpu.VMEM((2, WIDE, 2 * HD), F32),
            pltpu.SemaphoreType.DMA((2,)),
        ]
        + keys_bufs(WIDE),
        compiler_params=pltpu.CompilerParams(vmem_limit_bytes=14 * MIB),
    )(plan, wq, wdo, e, u)


def sum_kernel(own, a, b, c, out0, out1, out2, out3):
    for d, out in enumerate((out0, out1, out2, out3)):
        at = slice(d * BLK, (d + 1) * BLK)
        total = own[at] + a[at].astype(F32) + b[at].astype(F32) + c[at].astype(F32)
        out[...] = total.astype(out.dtype)


def run_sum(own, a, b, c):
    return pl.pallas_call(
        sum_kernel,
        out_shape=[struct((BLK, 2 * HD), F32)] + [struct((BLK, 2 * HD), BF16)] * 3,
        in_specs=[VM] * 4,
        out_specs=[VM] * 4,
        compiler_params=pltpu.CompilerParams(vmem_limit_bytes=6 * MIB),
    )(own, a, b, c)


def queries_kernel(place, parts, stats, out):
    own = place[AT_OWN]
    ms = [stats[j, pl.ds(own, 1), :] for j in range(N_Q)]
    ls = [stats[j, pl.ds(N_Q + own, 1), :] for j in range(N_Q)]
    top = functools.reduce(jnp.maximum, ms)
    es = [jnp.exp2((m - top) * EXP_SCALE) for m in ms]
    tot = sum(l * e for l, e in zip(ls, es))
    for h in range(HEADS):
        at = slice(h * HD, (h + 1) * HD)
        total = sum(parts[j, :, at].astype(F32) * es[j][:, at] for j in range(N_Q))
        out[:, at] = (total * (SCALING / tot[:, at])).T


def run_queries(place, parts, stats):
    return pl.pallas_call(
        queries_kernel,
        out_shape=struct((BLK, COLS), F32),
        in_specs=[SM, VM, VM],
        out_specs=VM,
        compiler_params=pltpu.CompilerParams(vmem_limit_bytes=6 * MIB),
    )(place, parts, stats)


def exchange(x, dx=0, dz=0, dy=0, dc=0):
    perm = []
    for b in range(16):
        for r in range(16):
            px = (b // 8) * 2 + (r // 2) % 2
            pz, py, pc = b % 8, r // 4, r % 2
            px, pz, py, pc = px ^ dx, pz ^ (2 * dz), py ^ dy, pc ^ dc
            other = (px // 2) * 8 + pz, py * 4 + (px % 2) * 2 + pc
            perm.append((b * 16 + r, other[0] * 16 + other[1]))
    return lax.ppermute(x, ("blk", "rows"), perm)


Q_GROUPS = [[r for r in range(16) if (r // 2) % 2 == lo] for lo in range(2)]


def to_group(x):
    return lax.all_to_all(x, "rows", 0, 0, axis_index_groups=Q_GROUPS, tiled=True)


def per_device(queries, keys, values, forward_out, grad_out, block_mask):
    b, r = lax.axis_index("blk"), lax.axis_index("rows")
    x = ((b >> 3) << 1) | ((r >> 1) & 1)
    zz, y, core = (b >> 1) & 3, r >> 2, r & 1
    slot_q = jnp.arange(N_Q)
    yq, cq = y ^ jnp.array((2, 0, 1, 3) * 2), core ^ (slot_q >> 2)
    q_blocks = ((b >> 1) << 4) + (yq << 2) + ((x & 1) << 1) + cq
    slot_k = jnp.arange(N_K)
    quad, a = slot_k >> 2, slot_k & 3
    xk = x ^ (((quad >> 1) << 1) | (a >> 1))
    zk = zz ^ (((quad & 1) << 1) | (a & 1))
    k_blocks = ((((xk >> 1) << 2) + zk) << 4) + (y << 2) + ((xk & 1) << 1) + core
    place = jnp.concatenate(
        [(b & 1)[None], q_blocks, k_blocks, (yq << 1) + cq, ((y << 1) + core)[None]]
    ).astype(jnp.int32)

    kv = pack_keys(keys, values)
    kv, queries = lax.optimization_barrier((kv, queries))
    qdo = pack_queries(queries, grad_out, forward_out)

    kv_z = jnp.concatenate([kv] + [exchange(kv, dz=d) for d in (1, 2, 3)], axis=0)
    kvs = [kv_z] + [exchange(kv_z, dx=d) for d in (1, 2, 3)]
    y1, y2, y3 = [exchange(qdo, dy=d) for d in (1, 2, 3)]
    near = jnp.concatenate([y2, qdo, y1, y3], axis=0)
    place, _ = lax.optimization_barrier((place, kv_z))
    plan = run_plan(place, pltpu.with_memory_space_constraint(block_mask, pltpu.HBM))
    near, k1, k3, k2, plan = lax.optimization_barrier((near, kvs[1], kvs[3], kvs[2], plan))
    kvs = [kv_z, k1, k2, k3]
    far = exchange(near, dc=1)

    e, stat = run_scores(place, plan, near, far, kvs)
    e = pltpu.with_memory_space_constraint(e, pltpu.HBM)
    stats = to_group(stat)
    u, dq = run_parts(place, plan, near, far, kvs, e)
    u = pltpu.with_memory_space_constraint(u, pltpu.HBM)
    dq_parts = to_group(dq)
    *remote, wq, wdo = run_far(place, plan, stats, near, far, e, u)
    wq, wdo = [pltpu.with_memory_space_constraint(w, pltpu.HBM) for w in (wq, wdo)]
    got = [exchange(remote[d - 1], dx=d) for d in (2, 1, 3)]
    wq, dq_parts = lax.optimization_barrier((wq, dq_parts))
    own = run_own(plan, wq, wdo, e, u)
    mine, *rest = run_sum(own, *got)
    back = [exchange(rest[d - 1], dz=d) for d in (2, 1, 3)]
    grad_queries = run_queries(place, dq_parts, stats)
    total = mine + sum(part.astype(F32) for part in back)
    return grad_queries, total[:, :HD] * SCALING, total[:, HD:]


def solution(mesh):
    spec = P(("blk", "rows"), None)
    return jax.shard_map(
        per_device,
        mesh=mesh,
        in_specs=(spec, spec, spec, spec, spec, P()),
        out_specs=(spec, spec, spec),
        check_vma=False,
    )
```

```python
import functools
import math

import jax
import jax.numpy as jnp
from jax import lax
from jax.experimental import pallas as pl
from jax.experimental.pallas import tpu as pltpu
from jax.sharding import PartitionSpec as P

BLK = 128
HEADS = 4
HD = 128
COLS = HEADS * HD
N_Q = 8
N_K = 16
N_QUAD = N_K // 4
QUAD = 4 * BLK
WIDE = 2 * BLK
EXTRA = 16
D_ROWS = BLK + EXTRA
ROWS = BLK + D_ROWS
NEGATIVE = -1e30
FLOOR = -1e6
SCALING = 1.0 / math.sqrt(HD)
EXP_SCALE = SCALING * math.log2(math.e)
MIB = 1024 * 1024
F32 = jnp.float32
BF16 = jnp.bfloat16
ANY = pl.BlockSpec(memory_space=pl.ANY)
HBM = pl.BlockSpec(memory_space=pltpu.HBM)
VM = pl.BlockSpec(memory_space=pltpu.VMEM)
SM = pl.BlockSpec(memory_space=pltpu.SMEM)

NT = (((1,), (1,)), ((), ()))
NN = (((1,), (0,)), ((), ()))


def dot(a, b, dims):
    return lax.dot_general(a, b, dims, preferred_element_type=F32)


def struct(shape, dtype):
    return jax.ShapeDtypeStruct(shape, dtype)


def copy_all(pairs, sem):
    return [pltpu.make_async_copy(a, b, sem.at[n]) for n, (a, b) in enumerate(pairs)]


def pack_keys_kernel(k_ref, v_ref, kv_ref, sem):
    copies = copy_all(
        [(k_ref, kv_ref.at[:, pl.ds(0, HD)]), (v_ref, kv_ref.at[:, pl.ds(HD, HD)])], sem
    )
    for c in copies:
        c.start()
    for c in copies:
        c.wait()


def pack_queries_kernel(q_ref, do_ref, o_ref, qdo_ref, o_buf, sem):
    copies = copy_all(
        [
            (do_ref, qdo_ref.at[pl.ds(BLK, BLK)]),
            (o_ref, o_buf),
            (q_ref, qdo_ref.at[pl.ds(0, BLK)]),
        ],
        sem,
    )
    for c in copies:
        c.start()
    for c in copies[:2]:
        c.wait()
    prod = qdo_ref[BLK : 2 * BLK, :].astype(F32) * o_buf[...].astype(F32)
    delta = jnp.concatenate(
        [
            jnp.sum(prod[:, h * HD : (h + 1) * HD].T, axis=0, keepdims=True)
            for h in range(HEADS)
        ],
        axis=1,
    )
    high = delta.astype(BF16).astype(F32)
    rest = delta - high
    mid = rest.astype(BF16).astype(F32)
    low = rest - mid
    row = lax.broadcasted_iota(jnp.int32, (EXTRA, COLS), 0)
    extra = jnp.where(row == 0, high, jnp.where(row == 1, mid, jnp.where(row == 2, low, 0.0)))
    qdo_ref[2 * BLK :, :] = extra.astype(BF16)
    copies[2].wait()


def pack_keys(keys, values):
    return pl.pallas_call(
        pack_keys_kernel,
        out_shape=struct((BLK, 2 * HD), BF16),
        in_specs=[HBM] * 2,
        out_specs=VM,
        scratch_shapes=[pltpu.SemaphoreType.DMA((2,))],
        compiler_params=pltpu.CompilerParams(vmem_limit_bytes=4 * MIB),
    )(*[pltpu.with_memory_space_constraint(a, pltpu.HBM) for a in (keys, values)])


def pack_queries(queries, grad_out, forward_out):
    return pl.pallas_call(
        pack_queries_kernel,
        out_shape=struct((ROWS, COLS), BF16),
        in_specs=[HBM] * 3,
        out_specs=VM,
        scratch_shapes=[pltpu.VMEM((BLK, COLS), BF16), pltpu.SemaphoreType.DMA((3,))],
        compiler_params=pltpu.CompilerParams(vmem_limit_bytes=6 * MIB),
    )(*[pltpu.with_memory_space_constraint(a, pltpu.HBM) for a in (queries, grad_out, forward_out)])


AT_Q, AT_K, AT_G, AT_OWN = 1, 1 + N_Q, 1 + N_Q + N_K, 1 + 2 * N_Q + N_K
LIMITS, TABLE, ALL, FAR, NEAR, PLAN = 0, 128, 192, 256, 288, 320
T_ROW, T_COUNT = 8, 4


def plan_kernel(place, mask_hbm, plan, mask_s, found, sem):
    copy = pltpu.make_async_copy(mask_hbm.at[place[0]], mask_s, sem)
    copy.start()
    copy.wait()

    def row(i, carry):
        at = place[AT_Q + i]
        active = jnp.int32(0)
        for quad in range(N_QUAD):
            seen = jnp.int32(0)
            for a in range(4):
                level = mask_s[at, place[AT_K + 4 * quad + a]]
                plan[LIMITS + i * N_K + 4 * quad + a] = jnp.where(
                    level == 1, -BLK, jnp.where(level == 2, 0, BLK)
                )
                seen = seen | level
            plan[TABLE + i * T_ROW + active] = quad
            active += jnp.where(seen != 0, 1, 0)
        plan[TABLE + i * T_ROW + T_COUNT] = active
        return carry

    lax.fori_loop(0, N_Q, row, 0)

    n = jnp.int32(0)
    for i in range(N_Q):
        count = plan[TABLE + i * T_ROW + T_COUNT]
        for j in range(2):
            plan[ALL + 2 + n] = plan[TABLE + i * T_ROW + 2 * j] * N_Q + i
            plan[ALL + 3 + n] = plan[TABLE + i * T_ROW + 2 * j + 1] * N_Q + i
            n += jnp.where(count >= 2 * j + 2, 2, 0)
    plan[ALL] = n // 2
    for i in range(N_Q):
        count = plan[TABLE + i * T_ROW + T_COUNT]
        plan[ALL + 2 + n] = plan[TABLE + i * T_ROW + jnp.maximum(count - 1, 0)] * N_Q + i
        n += count % 2
    plan[ALL + 1] = n

    for base, quads in ((NEAR, (0, 1)), (FAR, (2, 3))):
        n = jnp.int32(0)
        for i in range(N_Q):
            has = [jnp.int32(0), jnp.int32(0)]
            for k in range(2):
                for a in range(N_QUAD):
                    here = (plan[TABLE + i * T_ROW + a] == quads[k]) & (
                        a < plan[TABLE + i * T_ROW + T_COUNT]
                    )
                    has[k] = has[k] | jnp.where(here, 1, 0)
            found[2 * i] = has[0]
            found[2 * i + 1] = has[1]
            plan[base + 2 + n] = quads[0] * N_Q + i
            plan[base + 3 + n] = quads[1] * N_Q + i
            n += 2 * (has[0] & has[1])
        plan[base] = n // 2
        for i in range(N_Q):
            plan[base + 2 + n] = (quads[0] + found[2 * i + 1]) * N_Q + i
            n += found[2 * i] ^ found[2 * i + 1]
        plan[base + 1] = n


def run_plan(place, mask):
    return pl.pallas_call(
        plan_kernel,
        out_shape=struct((PLAN,), jnp.int32),
        in_specs=[SM, HBM],
        out_specs=SM,
        scratch_shapes=[
            pltpu.SMEM((BLK, BLK), jnp.int32),
            pltpu.SMEM((32,), jnp.int32),
            pltpu.SemaphoreType.DMA(()),
        ],
        compiler_params=pltpu.CompilerParams(vmem_limit_bytes=4 * MIB),
    )(place, mask)


def queries_of(near, far, i):
    at = (i % 4) * ROWS
    return (near, far)[i // 4][at : at + BLK]


def grads_of(near, far, i):
    at = (i % 4) * ROWS + BLK
    return (near, far)[i // 4][at : at + D_ROWS]


def fill_quads(kvs, cols, buf):
    for quad in range(N_QUAD):
        for odd in range(2):
            at = slice((quad % 2) * WIDE, (quad % 2 + 1) * WIDE)
            buf[quad, odd * WIDE : (odd + 1) * WIDE] = kvs[2 * (quad // 2) + odd][at, cols]


def join(parts, axis=0):
    return parts[0] if len(parts) == 1 else jnp.concatenate(parts, axis=axis)


def heads(ref, i):
    return jnp.concatenate([ref[i, :BLK, h * HD : (h + 1) * HD] for h in range(HEADS)], axis=0)


E_SLOTS = 8


def scores_kernel(half, *refs):
    place, plan, q_in, kv0, kv1, kv2, kv3 = refs[:7]
    if half == 0:
        e_hbm, st, qs, ks, sc, ebuf, mx, lacc, count, e_sem = refs[7:]
    else:
        _, st_in, e_hbm, stats_hbm, qs, ks, sc, ebuf, mx, lacc, count, e_sem, st, st_sem = refs[7:]
        st[...] = st_in[...]
    count[0] = 0
    fill_quads((kv0, kv1, kv2, kv3), slice(0, HD), ks)
    for i in range(N_Q // 2):
        qs[i] = queries_of(q_in, q_in, i)
    diff = (
        lax.broadcasted_iota(jnp.int32, (BLK, WIDE), 1) % BLK
        - lax.broadcasted_iota(jnp.int32, (BLK, WIDE), 0)
    )

    def out_copy(slot, unit):
        return pltpu.make_async_copy(ebuf.at[slot], e_hbm.at[unit], e_sem.at[slot])

    def query_block(row, carry):
        i = half * (N_Q // 2) + row
        base = TABLE + i * T_ROW
        active = plan[base + T_COUNT]
        mx[...] = jnp.full(mx.shape, NEGATIVE, F32)
        lacc[...] = jnp.zeros(lacc.shape, F32)

        def score_quads(quads):
            limits = [plan[LIMITS + i * N_K + 4 * quad + a] for quad in quads for a in range(4)]
            joined = dot(join([ks[quad] for quad in quads]), heads(qs, row), NT)
            for hp in range(2):
                cols = slice(hp * WIDE, (hp + 1) * WIDE)
                best = mx[:, cols]
                for k, quad in enumerate(quads):
                    for a in range(4):
                        at = slice(a * BLK, (a + 1) * BLK)
                        s = joined[k * QUAD + a * BLK : k * QUAD + (a + 1) * BLK, cols]
                        part = jnp.where(diff >= limits[4 * k + a], s, NEGATIVE)
                        sc[quad, at, cols] = part
                        best = jnp.maximum(
                            best, jnp.max(part.reshape(BLK // 8, 8, WIDE), axis=0)
                        )
                mx[:, cols] = best

        def score_pair(n, carry):
            score_quads([plan[base + 2 * n], plan[base + 2 * n + 1]])
            return carry

        lax.fori_loop(0, active // 2, score_pair, 0)

        @pl.when(active % 2 == 1)
        def _():
            score_quads([plan[base + active - 1]])

        m = jnp.maximum(jnp.max(mx[...], axis=0, keepdims=True), FLOOR)

        def exp_quad(k, carry):
            quad = plan[base + k]
            n = count[0]
            slot = n % E_SLOTS

            @pl.when(n >= E_SLOTS)
            def _():
                out_copy(slot, 0).wait()

            for hp in range(2):
                cols = slice(hp * WIDE, (hp + 1) * WIDE)
                e = jnp.exp2((sc[quad, :, cols] - m[:, cols]) * EXP_SCALE)
                lacc[:, cols] += jnp.sum(e.reshape(QUAD // 8, 8, WIDE), axis=0)
                ebuf[slot, :, cols] = e.astype(BF16)
            out_copy(slot, quad * N_Q + i).start()
            count[0] = n + 1
            return carry

        lax.fori_loop(0, active, exp_quad, 0)
        g = place[AT_G + i]
        st[pl.ds(g, 1), :] = m
        st[pl.ds(N_Q + g, 1), :] = jnp.sum(lacc[...], axis=0, keepdims=True)
        return carry

    lax.fori_loop(0, N_Q // 2, query_block, 0)

    if half == 1:
        st_copies = copy_all([(st, stats_hbm.at[g]) for g in range(N_Q)], st_sem)
        for c in st_copies:
            c.start()
        for c in st_copies:
            c.wait()
    for slot_no in range(E_SLOTS):

        @pl.when(count[0] > slot_no)
        def _():
            out_copy(slot_no, 0).wait()


def run_scores(half, place, plan, queries, kvs, before=()):
    stats_shape = (2 * N_Q, COLS)
    return pl.pallas_call(
        functools.partial(scores_kernel, half),
        out_shape=[
            pltpu.HBM((N_QUAD * N_Q, QUAD, COLS), BF16),
            pltpu.HBM((N_Q, *stats_shape), F32) if half else struct(stats_shape, F32),
        ],
        in_specs=[SM, SM] + [VM] * 5 + ([HBM, VM] if half else []),
        out_specs=[HBM, HBM if half else VM],
        scratch_shapes=[
            pltpu.VMEM((N_Q // 2, BLK, COLS), BF16),
            pltpu.VMEM((N_QUAD, QUAD, HD), BF16),
            pltpu.VMEM((N_QUAD, QUAD, COLS), F32),
            pltpu.VMEM((E_SLOTS, QUAD, COLS), BF16),
            pltpu.VMEM((8, COLS), F32),
            pltpu.VMEM((8, COLS), F32),
            pltpu.SMEM((1,), jnp.int32),
            pltpu.SemaphoreType.DMA((E_SLOTS,)),
        ]
        + ([pltpu.VMEM(stats_shape, F32), pltpu.SemaphoreType.DMA((N_Q,))] if half else []),
        input_output_aliases={7: 0} if half else {},
        compiler_params=pltpu.CompilerParams(vmem_limit_bytes=20 * MIB),
    )(place, plan, queries, *kvs, *before)


DEPTH, AHEAD = 10, 6


def loop_units(plan, base, visit):
    pairs, total = plan[base], plan[base + 1]
    for start, count, number in ((0, pairs, 2), (2 * pairs, total - 2 * pairs, 1)):

        def two(n, carry, start=start, number=number):
            first = start + 2 * number * n
            visit([(first, number), (first + number, number)])
            return carry

        lax.fori_loop(0, count // 2, two, 0)

        @pl.when(count % 2 == 1)
        def _(start=start, count=count, number=number):
            visit([(start + (count - 1) * number, number)])


def prefetch(plan, base, copies, first, number):
    total = plan[base + 1]
    for k in range(number):

        @pl.when(first + k + AHEAD < total)
        def _():
            for c in copies(first + k + AHEAD):
                c.start()

    for k in range(number):
        for c in copies(first + k):
            c.wait()


def start_first(plan, base, copies):
    for n in range(AHEAD):

        @pl.when(n < plan[base + 1])
        def _():
            for c in copies(n):
                c.start()


def parts_kernel(
    place, plan, near, far, kv0, kv1, kv2, kv3, e_hbm,
    u_hbm, dq_hbm,
    ds, ks, vs, kts, ebuf, ubuf, dqs, dq_low, e_sem, u_sem, dq_sem,
):
    def in_copies(n):
        unit, at = plan[ALL + 2 + n], n % DEPTH
        return (pltpu.make_async_copy(e_hbm.at[unit], ebuf.at[at], e_sem.at[at]),)

    def out_copy(n, unit):
        at = n % DEPTH
        return pltpu.make_async_copy(ubuf.at[at], u_hbm.at[unit], u_sem.at[at])

    start_first(plan, ALL, in_copies)
    kvs = (kv0, kv1, kv2, kv3)
    fill_quads(kvs, slice(0, HD), ks)
    fill_quads(kvs, slice(HD, 2 * HD), vs)
    for i in range(N_Q):
        ds[i] = grads_of(near, far, i)
    dqs[...] = jnp.zeros(dqs.shape, F32)
    for quad in range(N_QUAD):
        kts[quad] = ks[quad].T

    def visit(groups):
        first, number = groups[0][0], sum(g[1] for g in groups)
        for k in range(number):

            @pl.when(first + k >= DEPTH)
            def _():
                out_copy(first + k, 0).wait()

        prefetch(plan, ALL, in_copies, first, number)
        done = []
        for start, size in groups:
            units = [plan[ALL + 2 + start + k] for k in range(size)]
            i, quads = units[0] % N_Q, [unit // N_Q for unit in units]
            extra = ds[i, BLK:, :].astype(F32)
            delta = extra[0:1] + extra[1:2] + extra[2:3]
            da = dot(join([vs[quad] for quad in quads]), heads(ds, i), NT)
            us = []
            for k in range(size):
                at = (start + k) % DEPTH
                u = (ebuf[at].astype(F32) * (da[k * QUAD : (k + 1) * QUAD] - delta)).astype(BF16)
                ubuf[at] = u
                us.append(u)
            done.append((i, dot(join([kts[quad] for quad in quads], axis=1), join(us), NN)))
            for k in range(size):
                out_copy(start + k, units[k]).start()
        for i, part in done:
            dqs[i] += part

    loop_units(plan, ALL, visit)
    dq_copies = copy_all([(dq_low.at[i], dq_hbm.at[place[AT_G + i]]) for i in range(N_Q)], dq_sem)
    for i in range(N_Q):
        dq_low[i] = dqs[i].astype(BF16)
        dq_copies[i].start()
    for c in dq_copies:
        c.wait()
    for n in range(DEPTH):

        @pl.when(n < plan[ALL + 1])
        def _():
            out_copy(n, 0).wait()


def run_parts(place, plan, near, far, kvs, e):
    dma = pltpu.SemaphoreType.DMA
    return pl.pallas_call(
        parts_kernel,
        out_shape=[
            pltpu.HBM((N_QUAD * N_Q, QUAD, COLS), BF16),
            pltpu.HBM((N_Q, HD, COLS), BF16),
        ],
        in_specs=[SM, SM] + [VM] * 6 + [HBM],
        out_specs=[HBM, HBM],
        scratch_shapes=[
            pltpu.VMEM((N_Q, D_ROWS, COLS), BF16),
            pltpu.VMEM((N_QUAD, QUAD, HD), BF16),
            pltpu.VMEM((N_QUAD, QUAD, HD), BF16),
            pltpu.VMEM((N_QUAD, HD, QUAD), BF16),
            pltpu.VMEM((DEPTH, QUAD, COLS), BF16),
            pltpu.VMEM((DEPTH, QUAD, COLS), BF16),
            pltpu.VMEM((N_Q, HD, COLS), F32),
            pltpu.VMEM((N_Q, HD, COLS), BF16),
            dma((DEPTH,)),
            dma((DEPTH,)),
            dma((N_Q,)),
        ],
        compiler_params=pltpu.CompilerParams(vmem_limit_bytes=34 * MIB),
    )(place, plan, near, far, *kvs, e)


def row_weights(place, stats, near, far, ws, wq, wdo):
    ms = [stats[j, :N_Q, :] for j in range(N_Q)]
    top = functools.reduce(jnp.maximum, ms)
    tot = sum(stats[j, N_Q:, :] * jnp.exp2((ms[j] - top) * EXP_SCALE) for j in range(N_Q))
    ws[...] = jnp.exp2((stats[place[AT_OWN], :N_Q, :] - top) * EXP_SCALE) / tot
    rows = []
    for i in range(N_Q):
        w = ws[pl.ds(place[AT_G + i], 1), :]
        rows += [w[:, h * BLK : (h + 1) * BLK] for h in range(HEADS)]
    rows.append(jnp.zeros((BLK - len(rows), BLK), F32))
    cols = jnp.concatenate(rows, axis=0).T
    for i in range(N_Q):
        q = queries_of(near, far, i)
        do = grads_of(near, far, i)
        for h in range(HEADS):
            w = cols[:, i * HEADS + h : i * HEADS + h + 1]
            at = slice(h * BLK, (h + 1) * BLK)
            c = slice(h * HD, (h + 1) * HD)
            wq[i, at, :] = (q[:, c].astype(F32) * w).astype(BF16)
            wdo[i, at, :] = (do[:BLK, c].astype(F32) * w).astype(BF16)


def sum_keys(plan, base, first_quad, rows, wq, wdo, e_hbm, u_hbm, acc, bufs):
    ebuf, ubuf, e_sem, u_sem = bufs
    size = acc.shape[1]

    def in_copies(n):
        unit, at = plan[base + 2 + n], n % DEPTH
        return [
            pltpu.make_async_copy(
                hbm.at[unit, pl.ds(rows, size)], buf.at[at, pl.ds(0, size)], sem.at[at]
            )
            for hbm, buf, sem in ((e_hbm, ebuf, e_sem), (u_hbm, ubuf, u_sem))
        ]

    start_first(plan, base, in_copies)
    acc[...] = jnp.zeros(acc.shape, F32)

    def visit(groups):
        prefetch(plan, base, in_copies, groups[0][0], sum(g[1] for g in groups))
        done = []
        for first, number in groups:
            unit = plan[base + 2 + first]
            i, quad = unit % N_Q, unit // N_Q - first_quad
            for buf, w, cols in ((ubuf, wq, slice(0, HD)), (ebuf, wdo, slice(HD, 2 * HD))):
                rows_of = [buf[(first + k) % DEPTH, :size] for k in range(number)]
                done.append((quad, number, cols, dot(join(rows_of), w[i], NN)))
        for quad, number, cols, part in done:
            for k in range(number):
                acc[quad + k, :, cols] += part[k * size : (k + 1) * size]

    return lambda: loop_units(plan, base, visit)


def far_kernel(
    place, plan, stats, near, far, e_hbm, u_hbm,
    out1, out2, out3, wq_hbm, wdo_hbm,
    ws, wq, wdo, acc, acc_odd, w_sem, *bufs,
):
    w_copies = copy_all([(wq, wq_hbm), (wdo, wdo_hbm)], w_sem)

    sum_far = sum_keys(plan, FAR, 2, 0, wq, wdo, e_hbm, u_hbm, acc, bufs[:4])
    sum_odd = sum_keys(plan, NEAR, 0, WIDE, wq, wdo, e_hbm, u_hbm, acc_odd, bufs[4:])
    row_weights(place, stats, near, far, ws, wq, wdo)
    for c in w_copies:
        c.start()
    sum_far()
    sum_odd()
    for quad in range(2):
        at = slice(quad * WIDE, (quad + 1) * WIDE)
        out1[at, :] = acc_odd[quad].astype(BF16)
        out2[at, :] = acc[quad, :WIDE].astype(BF16)
        out3[at, :] = acc[quad, WIDE:].astype(BF16)
    for c in w_copies:
        c.wait()


def own_kernel(plan, wq_hbm, wdo_hbm, e_hbm, u_hbm, out, wq, wdo, acc, w_sem, *bufs):
    w_copies = copy_all([(wq_hbm, wq), (wdo_hbm, wdo)], w_sem)
    for c in w_copies:
        c.start()

    sum_own = sum_keys(plan, NEAR, 0, 0, wq, wdo, e_hbm, u_hbm, acc, bufs)
    for c in w_copies:
        c.wait()
    sum_own()
    for quad in range(2):
        out[quad * WIDE : (quad + 1) * WIDE, :] = acc[quad]


def keys_bufs(rows):
    return [
        pltpu.VMEM((DEPTH, rows, COLS), BF16),
        pltpu.VMEM((DEPTH, rows, COLS), BF16),
        pltpu.SemaphoreType.DMA((DEPTH,)),
        pltpu.SemaphoreType.DMA((DEPTH,)),
    ]


def run_far(place, plan, stats, near, far, e, u):
    return pl.pallas_call(
        far_kernel,
        out_shape=[struct((QUAD, 2 * HD), BF16)] * 3 + [pltpu.HBM((N_Q, COLS, HD), BF16)] * 2,
        in_specs=[SM, SM] + [VM] * 3 + [HBM, HBM],
        out_specs=[VM] * 3 + [HBM] * 2,
        scratch_shapes=[
            pltpu.VMEM((N_Q, COLS), F32),
            pltpu.VMEM((N_Q, COLS, HD), BF16),
            pltpu.VMEM((N_Q, COLS, HD), BF16),
            pltpu.VMEM((2, QUAD, 2 * HD), F32),
            pltpu.VMEM((2, WIDE, 2 * HD), F32),
            pltpu.SemaphoreType.DMA((2,)),
        ]
        + keys_bufs(QUAD)
        + keys_bufs(WIDE),
        compiler_params=pltpu.CompilerParams(vmem_limit_bytes=30 * MIB),
    )(place, plan, stats, near, far, e, u)


def run_own(plan, wq, wdo, e, u):
    return pl.pallas_call(
        own_kernel,
        out_shape=struct((QUAD, 2 * HD), F32),
        in_specs=[SM] + [HBM] * 4,
        out_specs=VM,
        scratch_shapes=[
            pltpu.VMEM((N_Q, COLS, HD), BF16),
            pltpu.VMEM((N_Q, COLS, HD), BF16),
            pltpu.VMEM((2, WIDE, 2 * HD), F32),
            pltpu.SemaphoreType.DMA((2,)),
        ]
        + keys_bufs(WIDE),
        compiler_params=pltpu.CompilerParams(vmem_limit_bytes=18 * MIB),
    )(plan, wq, wdo, e, u)


def sum_kernel(own, a, b, c, out0, out1, out2, out3):
    for d, out in enumerate((out0, out1, out2, out3)):
        at = slice(d * BLK, (d + 1) * BLK)
        total = own[at] + a[at].astype(F32) + b[at].astype(F32) + c[at].astype(F32)
        out[...] = total.astype(out.dtype)


def run_sum(own, a, b, c):
    return pl.pallas_call(
        sum_kernel,
        out_shape=[struct((BLK, 2 * HD), F32)] + [struct((BLK, 2 * HD), BF16)] * 3,
        in_specs=[VM] * 4,
        out_specs=[VM] * 4,
        compiler_params=pltpu.CompilerParams(vmem_limit_bytes=6 * MIB),
    )(own, a, b, c)


def queries_kernel(place, parts, stats, out):
    own = place[AT_OWN]
    ms = [stats[j, pl.ds(own, 1), :] for j in range(N_Q)]
    ls = [stats[j, pl.ds(N_Q + own, 1), :] for j in range(N_Q)]
    top = functools.reduce(jnp.maximum, ms)
    es = [jnp.exp2((m - top) * EXP_SCALE) for m in ms]
    tot = sum(l * e for l, e in zip(ls, es))
    for h in range(HEADS):
        at = slice(h * HD, (h + 1) * HD)
        total = sum(parts[j, :, at].astype(F32) * es[j][:, at] for j in range(N_Q))
        out[:, at] = (total * (SCALING / tot[:, at])).T


def run_queries(place, parts, stats):
    return pl.pallas_call(
        queries_kernel,
        out_shape=struct((BLK, COLS), F32),
        in_specs=[SM, VM, VM],
        out_specs=VM,
        compiler_params=pltpu.CompilerParams(vmem_limit_bytes=6 * MIB),
    )(place, parts, stats)


def exchange(x, dx=0, dz=0, dy=0, dc=0):
    perm = []
    for b in range(16):
        for r in range(16):
            px = (b // 8) * 2 + (r // 2) % 2
            pz, py, pc = b % 8, r // 4, r % 2
            px, pz, py, pc = px ^ dx, pz ^ (2 * dz), py ^ dy, pc ^ dc
            other = (px // 2) * 8 + pz, py * 4 + (px % 2) * 2 + pc
            perm.append((b * 16 + r, other[0] * 16 + other[1]))
    return lax.ppermute(x, ("blk", "rows"), perm)


Q_GROUPS = [[r for r in range(16) if (r // 2) % 2 == lo] for lo in range(2)]


def to_group(x):
    return lax.all_to_all(x, "rows", 0, 0, axis_index_groups=Q_GROUPS, tiled=True)


def per_device(queries, keys, values, forward_out, grad_out, block_mask):
    b, r = lax.axis_index("blk"), lax.axis_index("rows")
    x = ((b >> 3) << 1) | ((r >> 1) & 1)
    zz, y, core = (b >> 1) & 3, r >> 2, r & 1
    slot_q = jnp.arange(N_Q)
    yq, cq = y ^ jnp.array((2, 0, 1, 3) * 2), core ^ (slot_q >> 2)
    q_blocks = ((b >> 1) << 4) + (yq << 2) + ((x & 1) << 1) + cq
    slot_k = jnp.arange(N_K)
    quad, a = slot_k >> 2, slot_k & 3
    xk = x ^ (((quad >> 1) << 1) | (a >> 1))
    zk = zz ^ (((quad & 1) << 1) | (a & 1))
    k_blocks = ((((xk >> 1) << 2) + zk) << 4) + (y << 2) + ((xk & 1) << 1) + core
    place = jnp.concatenate(
        [(b & 1)[None], q_blocks, k_blocks, (yq << 1) + cq, ((y << 1) + core)[None]]
    ).astype(jnp.int32)

    kv = pack_keys(keys, values)
    kv, queries = lax.optimization_barrier((kv, queries))
    qdo = pack_queries(queries, grad_out, forward_out)

    kv_z = jnp.concatenate([kv] + [exchange(kv, dz=d) for d in (1, 2, 3)], axis=0)
    kvs = [kv_z] + [exchange(kv_z, dx=d) for d in (1, 2, 3)]
    y1, y2, y3 = [exchange(qdo, dy=d) for d in (1, 2, 3)]
    near = jnp.concatenate([y2, qdo, y1, y3], axis=0)
    place, _ = lax.optimization_barrier((place, kv_z))
    plan = run_plan(place, pltpu.with_memory_space_constraint(block_mask, pltpu.HBM))
    near, k1, k3, k2, plan = lax.optimization_barrier((near, kvs[1], kvs[3], kvs[2], plan))
    kvs = [kv_z, k1, k2, k3]
    far = exchange(near, dc=1)

    e, totals = run_scores(0, place, plan, near, kvs)
    e = pltpu.with_memory_space_constraint(e, pltpu.HBM)
    e, stat = run_scores(1, place, plan, far, kvs, (e, totals))
    e = pltpu.with_memory_space_constraint(e, pltpu.HBM)
    stats = to_group(stat)
    u, dq = run_parts(place, plan, near, far, kvs, e)
    u = pltpu.with_memory_space_constraint(u, pltpu.HBM)
    dq_parts = to_group(dq)
    *remote, wq, wdo = run_far(place, plan, stats, near, far, e, u)
    wq, wdo = [pltpu.with_memory_space_constraint(w, pltpu.HBM) for w in (wq, wdo)]
    got = [exchange(remote[d - 1], dx=d) for d in (2, 1, 3)]
    wq, dq_parts = lax.optimization_barrier((wq, dq_parts))
    own = run_own(plan, wq, wdo, e, u)
    mine, *rest = run_sum(own, *got)
    back = [exchange(rest[d - 1], dz=d) for d in (2, 1, 3)]
    grad_queries = run_queries(place, dq_parts, stats)
    total = mine + sum(part.astype(F32) for part in back)
    return grad_queries, total[:, :HD] * SCALING, total[:, HD:]


def solution(mesh):
    spec = P(("blk", "rows"), None)
    return jax.shard_map(
        per_device,
        mesh=mesh,
        in_specs=(spec, spec, spec, spec, spec, P()),
        out_specs=(spec, spec, spec),
        check_vma=False,
    )
```

```python
import functools
import math

import jax
import jax.numpy as jnp
from jax import lax
from jax.experimental import pallas as pl
from jax.experimental.pallas import tpu as pltpu
from jax.sharding import PartitionSpec as P

BLK = 128
HEADS = 4
HD = 128
COLS = HEADS * HD
N_Q = 8
N_K = 16
N_QUAD = N_K // 4
QUAD = 4 * BLK
WIDE = 2 * BLK
EXTRA = 16
D_ROWS = BLK + EXTRA
ROWS = BLK + D_ROWS
NEGATIVE = -1e30
FLOOR = -1e6
SCALING = 1.0 / math.sqrt(HD)
EXP_SCALE = SCALING * math.log2(math.e)
MIB = 1024 * 1024
F32 = jnp.float32
BF16 = jnp.bfloat16
ANY = pl.BlockSpec(memory_space=pl.ANY)
HBM = pl.BlockSpec(memory_space=pltpu.HBM)
VM = pl.BlockSpec(memory_space=pltpu.VMEM)
SM = pl.BlockSpec(memory_space=pltpu.SMEM)

NT = (((1,), (1,)), ((), ()))
NN = (((1,), (0,)), ((), ()))


def dot(a, b, dims):
    return lax.dot_general(a, b, dims, preferred_element_type=F32)


def struct(shape, dtype):
    return jax.ShapeDtypeStruct(shape, dtype)


def copy_all(pairs, sem):
    return [pltpu.make_async_copy(a, b, sem.at[n]) for n, (a, b) in enumerate(pairs)]


def pack_keys_kernel(k_ref, v_ref, kv_ref, sem):
    copies = copy_all(
        [(k_ref, kv_ref.at[:, pl.ds(0, HD)]), (v_ref, kv_ref.at[:, pl.ds(HD, HD)])], sem
    )
    for c in copies:
        c.start()
    for c in copies:
        c.wait()


def pack_queries_kernel(q_ref, do_ref, o_ref, qdo_ref, o_buf, sem):
    copies = copy_all(
        [
            (do_ref, qdo_ref.at[pl.ds(BLK, BLK)]),
            (o_ref, o_buf),
            (q_ref, qdo_ref.at[pl.ds(0, BLK)]),
        ],
        sem,
    )
    for c in copies:
        c.start()
    for c in copies[:2]:
        c.wait()
    prod = qdo_ref[BLK : 2 * BLK, :].astype(F32) * o_buf[...].astype(F32)
    delta = jnp.concatenate(
        [
            jnp.sum(prod[:, h * HD : (h + 1) * HD].T, axis=0, keepdims=True)
            for h in range(HEADS)
        ],
        axis=1,
    )
    high = delta.astype(BF16).astype(F32)
    rest = delta - high
    mid = rest.astype(BF16).astype(F32)
    low = rest - mid
    row = lax.broadcasted_iota(jnp.int32, (EXTRA, COLS), 0)
    extra = jnp.where(row == 0, high, jnp.where(row == 1, mid, jnp.where(row == 2, low, 0.0)))
    qdo_ref[2 * BLK :, :] = extra.astype(BF16)
    copies[2].wait()


def pack_keys(keys, values):
    return pl.pallas_call(
        pack_keys_kernel,
        out_shape=struct((BLK, 2 * HD), BF16),
        in_specs=[HBM] * 2,
        out_specs=VM,
        scratch_shapes=[pltpu.SemaphoreType.DMA((2,))],
        compiler_params=pltpu.CompilerParams(vmem_limit_bytes=4 * MIB),
    )(*[pltpu.with_memory_space_constraint(a, pltpu.HBM) for a in (keys, values)])


def pack_queries(queries, grad_out, forward_out):
    return pl.pallas_call(
        pack_queries_kernel,
        out_shape=struct((ROWS, COLS), BF16),
        in_specs=[HBM] * 3,
        out_specs=VM,
        scratch_shapes=[pltpu.VMEM((BLK, COLS), BF16), pltpu.SemaphoreType.DMA((3,))],
        compiler_params=pltpu.CompilerParams(vmem_limit_bytes=6 * MIB),
    )(*[pltpu.with_memory_space_constraint(a, pltpu.HBM) for a in (queries, grad_out, forward_out)])


AT_Q, AT_K, AT_G, AT_OWN = 1, 1 + N_Q, 1 + N_Q + N_K, 1 + 2 * N_Q + N_K
LIMITS, TABLE, ALL, FAR, NEAR, PLAN = 0, 128, 192, 256, 288, 320
T_ROW, T_COUNT = 8, 4


def plan_kernel(place, mask_hbm, plan, mask_s, found, sem):
    copy = pltpu.make_async_copy(mask_hbm.at[place[0]], mask_s, sem)
    copy.start()
    copy.wait()

    def row(i, carry):
        at = place[AT_Q + i]
        active = jnp.int32(0)
        for quad in range(N_QUAD):
            seen = jnp.int32(0)
            for a in range(4):
                level = mask_s[at, place[AT_K + 4 * quad + a]]
                plan[LIMITS + i * N_K + 4 * quad + a] = jnp.where(
                    level == 1, -BLK, jnp.where(level == 2, 0, BLK)
                )
                seen = seen | level
            plan[TABLE + i * T_ROW + active] = quad
            active += jnp.where(seen != 0, 1, 0)
        plan[TABLE + i * T_ROW + T_COUNT] = active
        return carry

    lax.fori_loop(0, N_Q, row, 0)

    n = jnp.int32(0)
    for i in range(N_Q):
        count = plan[TABLE + i * T_ROW + T_COUNT]
        for j in range(2):
            plan[ALL + 2 + n] = plan[TABLE + i * T_ROW + 2 * j] * N_Q + i
            plan[ALL + 3 + n] = plan[TABLE + i * T_ROW + 2 * j + 1] * N_Q + i
            n += jnp.where(count >= 2 * j + 2, 2, 0)
    plan[ALL] = n // 2
    for i in range(N_Q):
        count = plan[TABLE + i * T_ROW + T_COUNT]
        plan[ALL + 2 + n] = plan[TABLE + i * T_ROW + jnp.maximum(count - 1, 0)] * N_Q + i
        n += count % 2
    plan[ALL + 1] = n

    for base, quads in ((NEAR, (0, 1)), (FAR, (2, 3))):
        n = jnp.int32(0)
        for i in range(N_Q):
            has = [jnp.int32(0), jnp.int32(0)]
            for k in range(2):
                for a in range(N_QUAD):
                    here = (plan[TABLE + i * T_ROW + a] == quads[k]) & (
                        a < plan[TABLE + i * T_ROW + T_COUNT]
                    )
                    has[k] = has[k] | jnp.where(here, 1, 0)
            found[2 * i] = has[0]
            found[2 * i + 1] = has[1]
            plan[base + 2 + n] = quads[0] * N_Q + i
            plan[base + 3 + n] = quads[1] * N_Q + i
            n += 2 * (has[0] & has[1])
        plan[base] = n // 2
        for i in range(N_Q):
            plan[base + 2 + n] = (quads[0] + found[2 * i + 1]) * N_Q + i
            n += found[2 * i] ^ found[2 * i + 1]
        plan[base + 1] = n


def run_plan(place, mask):
    return pl.pallas_call(
        plan_kernel,
        out_shape=struct((PLAN,), jnp.int32),
        in_specs=[SM, HBM],
        out_specs=SM,
        scratch_shapes=[
            pltpu.SMEM((BLK, BLK), jnp.int32),
            pltpu.SMEM((32,), jnp.int32),
            pltpu.SemaphoreType.DMA(()),
        ],
        compiler_params=pltpu.CompilerParams(vmem_limit_bytes=4 * MIB),
    )(place, mask)


def queries_of(near, far, i):
    at = (i % 4) * ROWS
    return (near, far)[i // 4][at : at + BLK]


def grads_of(near, far, i):
    at = (i % 4) * ROWS + BLK
    return (near, far)[i // 4][at : at + D_ROWS]


def fill_quads(kvs, cols, buf):
    for quad in range(N_QUAD):
        for odd in range(2):
            at = slice((quad % 2) * WIDE, (quad % 2 + 1) * WIDE)
            buf[quad, odd * WIDE : (odd + 1) * WIDE] = kvs[2 * (quad // 2) + odd][at, cols]


def join(parts, axis=0):
    return parts[0] if len(parts) == 1 else jnp.concatenate(parts, axis=axis)


def heads(ref, i):
    return jnp.concatenate([ref[i, :BLK, h * HD : (h + 1) * HD] for h in range(HEADS)], axis=0)


E_SLOTS = 8


def scores_kernel(half, *refs):
    place, plan, q_in, kv0, kv1, kv2, kv3 = refs[:7]
    if half == 0:
        e_hbm, st, qs, ks, sc, ebuf, mx, lacc, count, e_sem = refs[7:]
    else:
        _, st_in, e_hbm, stats_hbm, qs, ks, sc, ebuf, mx, lacc, count, e_sem, st, st_sem = refs[7:]
        st[...] = st_in[...]
    count[0] = 0
    fill_quads((kv0, kv1, kv2, kv3), slice(0, HD), ks)
    for i in range(N_Q // 2):
        qs[i] = queries_of(q_in, q_in, i)
    diff = (
        lax.broadcasted_iota(jnp.int32, (BLK, WIDE), 1) % BLK
        - lax.broadcasted_iota(jnp.int32, (BLK, WIDE), 0)
    )

    def out_copy(slot, unit):
        return pltpu.make_async_copy(ebuf.at[slot], e_hbm.at[unit], e_sem.at[slot])

    def query_block(row, carry):
        i = half * (N_Q // 2) + row
        base = TABLE + i * T_ROW
        active = plan[base + T_COUNT]
        mx[...] = jnp.full(mx.shape, NEGATIVE, F32)
        lacc[...] = jnp.zeros(lacc.shape, F32)

        def score_quads(quads):
            limits = [plan[LIMITS + i * N_K + 4 * quad + a] for quad in quads for a in range(4)]
            joined = dot(join([ks[quad] for quad in quads]), heads(qs, row), NT)
            for hp in range(2):
                cols = slice(hp * WIDE, (hp + 1) * WIDE)
                best = mx[:, cols]
                for k, quad in enumerate(quads):
                    for a in range(4):
                        at = slice(a * BLK, (a + 1) * BLK)
                        s = joined[k * QUAD + a * BLK : k * QUAD + (a + 1) * BLK, cols]
                        part = jnp.where(diff >= limits[4 * k + a], s, NEGATIVE)
                        sc[quad, at, cols] = part
                        best = jnp.maximum(
                            best, jnp.max(part.reshape(BLK // 8, 8, WIDE), axis=0)
                        )
                mx[:, cols] = best

        def score_pair(n, carry):
            score_quads([plan[base + 2 * n], plan[base + 2 * n + 1]])
            return carry

        lax.fori_loop(0, active // 2, score_pair, 0)

        @pl.when(active % 2 == 1)
        def _():
            score_quads([plan[base + active - 1]])

        m = jnp.maximum(jnp.max(mx[...], axis=0, keepdims=True), FLOOR)

        def exp_quad(k, carry):
            quad = plan[base + k]
            n = count[0]
            slot = n % E_SLOTS

            @pl.when(n >= E_SLOTS)
            def _():
                out_copy(slot, 0).wait()

            for hp in range(2):
                cols = slice(hp * WIDE, (hp + 1) * WIDE)
                e = jnp.exp2((sc[quad, :, cols] - m[:, cols]) * EXP_SCALE)
                lacc[:, cols] += jnp.sum(e.reshape(QUAD // 8, 8, WIDE), axis=0)
                ebuf[slot, :, cols] = e.astype(BF16)
            out_copy(slot, quad * N_Q + i).start()
            count[0] = n + 1
            return carry

        lax.fori_loop(0, active, exp_quad, 0)
        g = place[AT_G + i]
        st[pl.ds(g, 1), :] = m
        st[pl.ds(N_Q + g, 1), :] = jnp.sum(lacc[...], axis=0, keepdims=True)
        return carry

    lax.fori_loop(0, N_Q // 2, query_block, 0)

    if half == 1:
        st_copies = copy_all([(st, stats_hbm.at[g]) for g in range(N_Q)], st_sem)
        for c in st_copies:
            c.start()
        for c in st_copies:
            c.wait()
    for slot_no in range(E_SLOTS):

        @pl.when(count[0] > slot_no)
        def _():
            out_copy(slot_no, 0).wait()


def run_scores(half, place, plan, queries, kvs, before=()):
    stats_shape = (2 * N_Q, COLS)
    return pl.pallas_call(
        functools.partial(scores_kernel, half),
        out_shape=[
            pltpu.HBM((N_QUAD * N_Q, QUAD, COLS), BF16),
            pltpu.HBM((N_Q, *stats_shape), F32) if half else struct(stats_shape, F32),
        ],
        in_specs=[SM, SM] + [VM] * 5 + ([HBM, VM] if half else []),
        out_specs=[HBM, HBM if half else VM],
        scratch_shapes=[
            pltpu.VMEM((N_Q // 2, BLK, COLS), BF16),
            pltpu.VMEM((N_QUAD, QUAD, HD), BF16),
            pltpu.VMEM((N_QUAD, QUAD, COLS), F32),
            pltpu.VMEM((E_SLOTS, QUAD, COLS), BF16),
            pltpu.VMEM((8, COLS), F32),
            pltpu.VMEM((8, COLS), F32),
            pltpu.SMEM((1,), jnp.int32),
            pltpu.SemaphoreType.DMA((E_SLOTS,)),
        ]
        + ([pltpu.VMEM(stats_shape, F32), pltpu.SemaphoreType.DMA((N_Q,))] if half else []),
        input_output_aliases={7: 0} if half else {},
        compiler_params=pltpu.CompilerParams(vmem_limit_bytes=20 * MIB),
    )(place, plan, queries, *kvs, *before)


DEPTH, AHEAD = 8, 6


def loop_units(plan, base, visit):
    pairs, total = plan[base], plan[base + 1]
    singles = total - 2 * pairs

    def pair(n, carry):
        visit([(2 * n, 2)])
        return carry

    def two_singles(n, carry):
        first = 2 * (pairs + n)
        visit([(first, 1), (first + 1, 1)])
        return carry

    lax.fori_loop(0, pairs, pair, 0)
    lax.fori_loop(0, singles // 2, two_singles, 0)

    @pl.when(singles % 2 == 1)
    def _():
        visit([(total - 1, 1)])


def prefetch(plan, base, copies, first, number):
    total = plan[base + 1]
    for k in range(number):

        @pl.when(first + k + AHEAD < total)
        def _():
            for c in copies(first + k + AHEAD):
                c.start()

    for k in range(number):
        for c in copies(first + k):
            c.wait()


def start_first(plan, base, copies):
    for n in range(AHEAD):

        @pl.when(n < plan[base + 1])
        def _():
            for c in copies(n):
                c.start()


def parts_kernel(
    place, plan, near, far, kv0, kv1, kv2, kv3, e_hbm,
    u_hbm, dq_hbm,
    ds, ks, vs, kts, ebuf, ubuf, dqs, dq_low, e_sem, u_sem, dq_sem,
):
    def in_copies(n):
        unit, at = plan[ALL + 2 + n], n % DEPTH
        return (pltpu.make_async_copy(e_hbm.at[unit], ebuf.at[at], e_sem.at[at]),)

    def out_copy(n, unit):
        at = n % DEPTH
        return pltpu.make_async_copy(ubuf.at[at], u_hbm.at[unit], u_sem.at[at])

    start_first(plan, ALL, in_copies)
    kvs = (kv0, kv1, kv2, kv3)
    fill_quads(kvs, slice(0, HD), ks)
    fill_quads(kvs, slice(HD, 2 * HD), vs)
    for i in range(N_Q):
        ds[i] = grads_of(near, far, i)
    dqs[...] = jnp.zeros(dqs.shape, F32)
    for quad in range(N_QUAD):
        kts[quad] = ks[quad].T

    def visit(groups):
        first, number = groups[0][0], sum(g[1] for g in groups)
        for k in range(number):

            @pl.when(first + k >= DEPTH)
            def _():
                out_copy(first + k, 0).wait()

        prefetch(plan, ALL, in_copies, first, number)
        done = []
        for start, size in groups:
            units = [plan[ALL + 2 + start + k] for k in range(size)]
            i, quads = units[0] % N_Q, [unit // N_Q for unit in units]
            extra = ds[i, BLK:, :].astype(F32)
            delta = extra[0:1] + extra[1:2] + extra[2:3]
            da = dot(join([vs[quad] for quad in quads]), heads(ds, i), NT)
            us = []
            for k in range(size):
                at = (start + k) % DEPTH
                u = (ebuf[at].astype(F32) * (da[k * QUAD : (k + 1) * QUAD] - delta)).astype(BF16)
                ubuf[at] = u
                us.append(u)
            done.append((i, dot(join([kts[quad] for quad in quads], axis=1), join(us), NN)))
            for k in range(size):
                out_copy(start + k, units[k]).start()
        for i, part in done:
            dqs[i] += part

    loop_units(plan, ALL, visit)
    dq_copies = copy_all([(dq_low.at[i], dq_hbm.at[place[AT_G + i]]) for i in range(N_Q)], dq_sem)
    for i in range(N_Q):
        dq_low[i] = dqs[i].astype(BF16)
        dq_copies[i].start()
    for c in dq_copies:
        c.wait()
    for n in range(DEPTH):

        @pl.when(n < plan[ALL + 1])
        def _():
            out_copy(n, 0).wait()


def run_parts(place, plan, near, far, kvs, e):
    dma = pltpu.SemaphoreType.DMA
    return pl.pallas_call(
        parts_kernel,
        out_shape=[
            pltpu.HBM((N_QUAD * N_Q, QUAD, COLS), BF16),
            pltpu.HBM((N_Q, HD, COLS), BF16),
        ],
        in_specs=[SM, SM] + [VM] * 6 + [HBM],
        out_specs=[HBM, HBM],
        scratch_shapes=[
            pltpu.VMEM((N_Q, D_ROWS, COLS), BF16),
            pltpu.VMEM((N_QUAD, QUAD, HD), BF16),
            pltpu.VMEM((N_QUAD, QUAD, HD), BF16),
            pltpu.VMEM((N_QUAD, HD, QUAD), BF16),
            pltpu.VMEM((DEPTH, QUAD, COLS), BF16),
            pltpu.VMEM((DEPTH, QUAD, COLS), BF16),
            pltpu.VMEM((N_Q, HD, COLS), F32),
            pltpu.VMEM((N_Q, HD, COLS), BF16),
            dma((DEPTH,)),
            dma((DEPTH,)),
            dma((N_Q,)),
        ],
        compiler_params=pltpu.CompilerParams(vmem_limit_bytes=28 * MIB),
    )(place, plan, near, far, *kvs, e)


def row_weights(place, stats, near, far, ws, wq, wdo):
    ms = [stats[j, :N_Q, :] for j in range(N_Q)]
    top = functools.reduce(jnp.maximum, ms)
    tot = sum(stats[j, N_Q:, :] * jnp.exp2((ms[j] - top) * EXP_SCALE) for j in range(N_Q))
    ws[...] = jnp.exp2((stats[place[AT_OWN], :N_Q, :] - top) * EXP_SCALE) / tot
    rows = []
    for i in range(N_Q):
        w = ws[pl.ds(place[AT_G + i], 1), :]
        rows += [w[:, h * BLK : (h + 1) * BLK] for h in range(HEADS)]
    rows.append(jnp.zeros((BLK - len(rows), BLK), F32))
    cols = jnp.concatenate(rows, axis=0).T
    for i in range(N_Q):
        q = queries_of(near, far, i)
        do = grads_of(near, far, i)
        for h in range(HEADS):
            w = cols[:, i * HEADS + h : i * HEADS + h + 1]
            at = slice(h * BLK, (h + 1) * BLK)
            c = slice(h * HD, (h + 1) * HD)
            wq[i, at, :] = (q[:, c].astype(F32) * w).astype(BF16)
            wdo[i, at, :] = (do[:BLK, c].astype(F32) * w).astype(BF16)


def sum_keys(plan, base, first_quad, rows, wq, wdo, e_hbm, u_hbm, acc, bufs):
    ebuf, ubuf, e_sem, u_sem = bufs
    size = acc.shape[1]

    def in_copies(n):
        unit, at = plan[base + 2 + n], n % DEPTH
        return [
            pltpu.make_async_copy(
                hbm.at[unit, pl.ds(rows, size)], buf.at[at, pl.ds(0, size)], sem.at[at]
            )
            for hbm, buf, sem in ((e_hbm, ebuf, e_sem), (u_hbm, ubuf, u_sem))
        ]

    start_first(plan, base, in_copies)
    acc[...] = jnp.zeros(acc.shape, F32)

    def visit(groups):
        prefetch(plan, base, in_copies, groups[0][0], sum(g[1] for g in groups))
        done = []
        for first, number in groups:
            unit = plan[base + 2 + first]
            i, quad = unit % N_Q, unit // N_Q - first_quad
            for buf, w, cols in ((ubuf, wq, slice(0, HD)), (ebuf, wdo, slice(HD, 2 * HD))):
                rows_of = [buf[(first + k) % DEPTH, :size] for k in range(number)]
                done.append((quad, number, cols, dot(join(rows_of), w[i], NN)))
        for quad, number, cols, part in done:
            for k in range(number):
                acc[quad + k, :, cols] += part[k * size : (k + 1) * size]

    return lambda: loop_units(plan, base, visit)


def far_kernel(
    place, plan, stats, near, far, e_hbm, u_hbm,
    out1, out2, out3, wq_hbm, wdo_hbm,
    ws, wq, wdo, acc, acc_odd, w_sem, *bufs,
):
    w_copies = copy_all([(wq, wq_hbm), (wdo, wdo_hbm)], w_sem)

    sum_far = sum_keys(plan, FAR, 2, 0, wq, wdo, e_hbm, u_hbm, acc, bufs[:4])
    sum_odd = sum_keys(plan, NEAR, 0, WIDE, wq, wdo, e_hbm, u_hbm, acc_odd, bufs[4:])
    row_weights(place, stats, near, far, ws, wq, wdo)
    for c in w_copies:
        c.start()
    sum_far()
    sum_odd()
    for quad in range(2):
        at = slice(quad * WIDE, (quad + 1) * WIDE)
        out1[at, :] = acc_odd[quad].astype(BF16)
        out2[at, :] = acc[quad, :WIDE].astype(BF16)
        out3[at, :] = acc[quad, WIDE:].astype(BF16)
    for c in w_copies:
        c.wait()


def own_kernel(plan, wq_hbm, wdo_hbm, e_hbm, u_hbm, out, wq, wdo, acc, w_sem, *bufs):
    w_copies = copy_all([(wq_hbm, wq), (wdo_hbm, wdo)], w_sem)
    for c in w_copies:
        c.start()

    sum_own = sum_keys(plan, NEAR, 0, 0, wq, wdo, e_hbm, u_hbm, acc, bufs)
    for c in w_copies:
        c.wait()
    sum_own()
    for quad in range(2):
        out[quad * WIDE : (quad + 1) * WIDE, :] = acc[quad]


def keys_bufs(rows):
    return [
        pltpu.VMEM((DEPTH, rows, COLS), BF16),
        pltpu.VMEM((DEPTH, rows, COLS), BF16),
        pltpu.SemaphoreType.DMA((DEPTH,)),
        pltpu.SemaphoreType.DMA((DEPTH,)),
    ]


def run_far(place, plan, stats, near, far, e, u):
    return pl.pallas_call(
        far_kernel,
        out_shape=[struct((QUAD, 2 * HD), BF16)] * 3 + [pltpu.HBM((N_Q, COLS, HD), BF16)] * 2,
        in_specs=[SM, SM] + [VM] * 3 + [HBM, HBM],
        out_specs=[VM] * 3 + [HBM] * 2,
        scratch_shapes=[
            pltpu.VMEM((N_Q, COLS), F32),
            pltpu.VMEM((N_Q, COLS, HD), BF16),
            pltpu.VMEM((N_Q, COLS, HD), BF16),
            pltpu.VMEM((2, QUAD, 2 * HD), F32),
            pltpu.VMEM((2, WIDE, 2 * HD), F32),
            pltpu.SemaphoreType.DMA((2,)),
        ]
        + keys_bufs(QUAD)
        + keys_bufs(WIDE),
        compiler_params=pltpu.CompilerParams(vmem_limit_bytes=24 * MIB),
    )(place, plan, stats, near, far, e, u)


def run_own(plan, wq, wdo, e, u):
    return pl.pallas_call(
        own_kernel,
        out_shape=struct((QUAD, 2 * HD), F32),
        in_specs=[SM] + [HBM] * 4,
        out_specs=VM,
        scratch_shapes=[
            pltpu.VMEM((N_Q, COLS, HD), BF16),
            pltpu.VMEM((N_Q, COLS, HD), BF16),
            pltpu.VMEM((2, WIDE, 2 * HD), F32),
            pltpu.SemaphoreType.DMA((2,)),
        ]
        + keys_bufs(WIDE),
        compiler_params=pltpu.CompilerParams(vmem_limit_bytes=14 * MIB),
    )(plan, wq, wdo, e, u)


def sum_kernel(own, a, b, c, out0, out1, out2, out3):
    for d, out in enumerate((out0, out1, out2, out3)):
        at = slice(d * BLK, (d + 1) * BLK)
        total = own[at] + a[at].astype(F32) + b[at].astype(F32) + c[at].astype(F32)
        out[...] = total.astype(out.dtype)


def run_sum(own, a, b, c):
    return pl.pallas_call(
        sum_kernel,
        out_shape=[struct((BLK, 2 * HD), F32)] + [struct((BLK, 2 * HD), BF16)] * 3,
        in_specs=[VM] * 4,
        out_specs=[VM] * 4,
        compiler_params=pltpu.CompilerParams(vmem_limit_bytes=6 * MIB),
    )(own, a, b, c)


def queries_kernel(place, parts, stats, out):
    own = place[AT_OWN]
    ms = [stats[j, pl.ds(own, 1), :] for j in range(N_Q)]
    ls = [stats[j, pl.ds(N_Q + own, 1), :] for j in range(N_Q)]
    top = functools.reduce(jnp.maximum, ms)
    es = [jnp.exp2((m - top) * EXP_SCALE) for m in ms]
    tot = sum(l * e for l, e in zip(ls, es))
    for h in range(HEADS):
        at = slice(h * HD, (h + 1) * HD)
        total = sum(parts[j, :, at].astype(F32) * es[j][:, at] for j in range(N_Q))
        out[:, at] = (total * (SCALING / tot[:, at])).T


def run_queries(place, parts, stats):
    return pl.pallas_call(
        queries_kernel,
        out_shape=struct((BLK, COLS), F32),
        in_specs=[SM, VM, VM],
        out_specs=VM,
        compiler_params=pltpu.CompilerParams(vmem_limit_bytes=6 * MIB),
    )(place, parts, stats)


def exchange(x, dx=0, dz=0, dy=0, dc=0):
    perm = []
    for b in range(16):
        for r in range(16):
            px = (b // 8) * 2 + (r // 2) % 2
            pz, py, pc = b % 8, r // 4, r % 2
            px, pz, py, pc = px ^ dx, pz ^ (2 * dz), py ^ dy, pc ^ dc
            other = (px // 2) * 8 + pz, py * 4 + (px % 2) * 2 + pc
            perm.append((b * 16 + r, other[0] * 16 + other[1]))
    return lax.ppermute(x, ("blk", "rows"), perm)


Q_GROUPS = [[r for r in range(16) if (r // 2) % 2 == lo] for lo in range(2)]


def to_group(x):
    return lax.all_to_all(x, "rows", 0, 0, axis_index_groups=Q_GROUPS, tiled=True)


def per_device(queries, keys, values, forward_out, grad_out, block_mask):
    b, r = lax.axis_index("blk"), lax.axis_index("rows")
    x = ((b >> 3) << 1) | ((r >> 1) & 1)
    zz, y, core = (b >> 1) & 3, r >> 2, r & 1
    slot_q = jnp.arange(N_Q)
    yq, cq = y ^ jnp.array((2, 0, 1, 3) * 2), core ^ (slot_q >> 2)
    q_blocks = ((b >> 1) << 4) + (yq << 2) + ((x & 1) << 1) + cq
    slot_k = jnp.arange(N_K)
    quad, a = slot_k >> 2, slot_k & 3
    xk = x ^ (((quad >> 1) << 1) | (a >> 1))
    zk = zz ^ (((quad & 1) << 1) | (a & 1))
    k_blocks = ((((xk >> 1) << 2) + zk) << 4) + (y << 2) + ((xk & 1) << 1) + core
    place = jnp.concatenate(
        [(b & 1)[None], q_blocks, k_blocks, (yq << 1) + cq, ((y << 1) + core)[None]]
    ).astype(jnp.int32)

    kv = pack_keys(keys, values)
    kv, queries = lax.optimization_barrier((kv, queries))
    qdo = pack_queries(queries, grad_out, forward_out)

    kv_z = jnp.concatenate([kv] + [exchange(kv, dz=d) for d in (1, 2, 3)], axis=0)
    kvs = [kv_z] + [exchange(kv_z, dx=d) for d in (1, 2, 3)]
    y1, y2, y3 = [exchange(qdo, dy=d) for d in (1, 2, 3)]
    near = jnp.concatenate([y2, qdo, y1, y3], axis=0)
    near, place = lax.optimization_barrier((near, place))
    plan = run_plan(place, pltpu.with_memory_space_constraint(block_mask, pltpu.HBM))
    near, k1, k3, k2, plan = lax.optimization_barrier((near, kvs[1], kvs[3], kvs[2], plan))
    kvs = [kv_z, k1, k2, k3]
    far = exchange(near, dc=1)

    e, totals = run_scores(0, place, plan, near, kvs)
    e = pltpu.with_memory_space_constraint(e, pltpu.HBM)
    e, stat = run_scores(1, place, plan, far, kvs, (e, totals))
    e = pltpu.with_memory_space_constraint(e, pltpu.HBM)
    stats = to_group(stat)
    u, dq = run_parts(place, plan, near, far, kvs, e)
    u = pltpu.with_memory_space_constraint(u, pltpu.HBM)
    dq_parts = to_group(dq)
    *remote, wq, wdo = run_far(place, plan, stats, near, far, e, u)
    wq, wdo = [pltpu.with_memory_space_constraint(w, pltpu.HBM) for w in (wq, wdo)]
    got = [exchange(remote[d - 1], dx=d) for d in (2, 1, 3)]
    wq, dq_parts = lax.optimization_barrier((wq, dq_parts))
    own = run_own(plan, wq, wdo, e, u)
    mine, *rest = run_sum(own, *got)
    back = [exchange(rest[d - 1], dz=d) for d in (2, 1, 3)]
    grad_queries = run_queries(place, dq_parts, stats)
    total = mine + sum(part.astype(F32) for part in back)
    return grad_queries, total[:, :HD] * SCALING, total[:, HD:]


def solution(mesh):
    spec = P(("blk", "rows"), None)
    return jax.shard_map(
        per_device,
        mesh=mesh,
        in_specs=(spec, spec, spec, spec, spec, P()),
        out_specs=(spec, spec, spec),
        check_vma=False,
    )
```

```python
import functools
import math

import jax
import jax.numpy as jnp
from jax import lax
from jax.experimental import pallas as pl
from jax.experimental.pallas import tpu as pltpu
from jax.sharding import PartitionSpec as P

BLK = 128
HEADS = 4
HD = 128
COLS = HEADS * HD
N_Q = 8
N_K = 16
N_QUAD = N_K // 4
QUAD = 4 * BLK
WIDE = 2 * BLK
EXTRA = 16
D_ROWS = BLK + EXTRA
ROWS = BLK + D_ROWS
NEGATIVE = -1e30
FLOOR = -1e6
SCALING = 1.0 / math.sqrt(HD)
EXP_SCALE = SCALING * math.log2(math.e)
MIB = 1024 * 1024
F32 = jnp.float32
BF16 = jnp.bfloat16
ANY = pl.BlockSpec(memory_space=pl.ANY)
HBM = pl.BlockSpec(memory_space=pltpu.HBM)
VM = pl.BlockSpec(memory_space=pltpu.VMEM)
SM = pl.BlockSpec(memory_space=pltpu.SMEM)

NT = (((1,), (1,)), ((), ()))
NN = (((1,), (0,)), ((), ()))


def dot(a, b, dims):
    return lax.dot_general(a, b, dims, preferred_element_type=F32)


def struct(shape, dtype):
    return jax.ShapeDtypeStruct(shape, dtype)


def copy_all(pairs, sem):
    return [pltpu.make_async_copy(a, b, sem.at[n]) for n, (a, b) in enumerate(pairs)]


def pack_keys_kernel(k_ref, v_ref, kv_ref, sem):
    copies = copy_all(
        [(k_ref, kv_ref.at[:, pl.ds(0, HD)]), (v_ref, kv_ref.at[:, pl.ds(HD, HD)])], sem
    )
    for c in copies:
        c.start()
    for c in copies:
        c.wait()


def pack_queries_kernel(q_ref, do_ref, o_ref, qdo_ref, o_buf, sem):
    copies = copy_all(
        [
            (do_ref, qdo_ref.at[pl.ds(BLK, BLK)]),
            (o_ref, o_buf),
            (q_ref, qdo_ref.at[pl.ds(0, BLK)]),
        ],
        sem,
    )
    for c in copies:
        c.start()
    for c in copies[:2]:
        c.wait()
    prod = qdo_ref[BLK : 2 * BLK, :].astype(F32) * o_buf[...].astype(F32)
    delta = jnp.concatenate(
        [
            jnp.sum(prod[:, h * HD : (h + 1) * HD].T, axis=0, keepdims=True)
            for h in range(HEADS)
        ],
        axis=1,
    )
    high = delta.astype(BF16).astype(F32)
    rest = delta - high
    mid = rest.astype(BF16).astype(F32)
    low = rest - mid
    row = lax.broadcasted_iota(jnp.int32, (EXTRA, COLS), 0)
    extra = jnp.where(row == 0, high, jnp.where(row == 1, mid, jnp.where(row == 2, low, 0.0)))
    qdo_ref[2 * BLK :, :] = extra.astype(BF16)
    copies[2].wait()


def pack_keys(keys, values):
    return pl.pallas_call(
        pack_keys_kernel,
        out_shape=struct((BLK, 2 * HD), BF16),
        in_specs=[HBM] * 2,
        out_specs=VM,
        scratch_shapes=[pltpu.SemaphoreType.DMA((2,))],
        compiler_params=pltpu.CompilerParams(vmem_limit_bytes=4 * MIB),
    )(*[pltpu.with_memory_space_constraint(a, pltpu.HBM) for a in (keys, values)])


def pack_queries(queries, grad_out, forward_out):
    return pl.pallas_call(
        pack_queries_kernel,
        out_shape=struct((ROWS, COLS), BF16),
        in_specs=[HBM] * 3,
        out_specs=VM,
        scratch_shapes=[pltpu.VMEM((BLK, COLS), BF16), pltpu.SemaphoreType.DMA((3,))],
        compiler_params=pltpu.CompilerParams(vmem_limit_bytes=6 * MIB),
    )(*[pltpu.with_memory_space_constraint(a, pltpu.HBM) for a in (queries, grad_out, forward_out)])


AT_Q, AT_K, AT_G, AT_OWN = 1, 1 + N_Q, 1 + N_Q + N_K, 1 + 2 * N_Q + N_K
LIMITS, TABLE, ALL, FAR, NEAR, PLAN = 0, 128, 192, 256, 288, 320
T_ROW, T_COUNT = 8, 4


def plan_kernel(place, mask_hbm, plan, mask_s, found, sem):
    copy = pltpu.make_async_copy(mask_hbm.at[place[0]], mask_s, sem)
    copy.start()
    copy.wait()

    def row(i, carry):
        at = place[AT_Q + i]
        active = jnp.int32(0)
        for quad in range(N_QUAD):
            seen = jnp.int32(0)
            for a in range(4):
                level = mask_s[at, place[AT_K + 4 * quad + a]]
                plan[LIMITS + i * N_K + 4 * quad + a] = jnp.where(
                    level == 1, -BLK, jnp.where(level == 2, 0, BLK)
                )
                seen = seen | level
            plan[TABLE + i * T_ROW + active] = quad
            active += jnp.where(seen != 0, 1, 0)
        plan[TABLE + i * T_ROW + T_COUNT] = active
        return carry

    lax.fori_loop(0, N_Q, row, 0)

    n = jnp.int32(0)
    for i in range(N_Q):
        count = plan[TABLE + i * T_ROW + T_COUNT]
        for j in range(2):
            plan[ALL + 2 + n] = plan[TABLE + i * T_ROW + 2 * j] * N_Q + i
            plan[ALL + 3 + n] = plan[TABLE + i * T_ROW + 2 * j + 1] * N_Q + i
            n += jnp.where(count >= 2 * j + 2, 2, 0)
    plan[ALL] = n // 2
    for i in range(N_Q):
        count = plan[TABLE + i * T_ROW + T_COUNT]
        plan[ALL + 2 + n] = plan[TABLE + i * T_ROW + jnp.maximum(count - 1, 0)] * N_Q + i
        n += count % 2
    plan[ALL + 1] = n

    for base, quads in ((NEAR, (0, 1)), (FAR, (2, 3))):
        n = jnp.int32(0)
        for i in range(N_Q):
            has = [jnp.int32(0), jnp.int32(0)]
            for k in range(2):
                for a in range(N_QUAD):
                    here = (plan[TABLE + i * T_ROW + a] == quads[k]) & (
                        a < plan[TABLE + i * T_ROW + T_COUNT]
                    )
                    has[k] = has[k] | jnp.where(here, 1, 0)
            found[2 * i] = has[0]
            found[2 * i + 1] = has[1]
            plan[base + 2 + n] = quads[0] * N_Q + i
            plan[base + 3 + n] = quads[1] * N_Q + i
            n += 2 * (has[0] & has[1])
        plan[base] = n // 2
        for i in range(N_Q):
            plan[base + 2 + n] = (quads[0] + found[2 * i + 1]) * N_Q + i
            n += found[2 * i] ^ found[2 * i + 1]
        plan[base + 1] = n


def run_plan(place, mask):
    return pl.pallas_call(
        plan_kernel,
        out_shape=struct((PLAN,), jnp.int32),
        in_specs=[SM, HBM],
        out_specs=SM,
        scratch_shapes=[
            pltpu.SMEM((BLK, BLK), jnp.int32),
            pltpu.SMEM((32,), jnp.int32),
            pltpu.SemaphoreType.DMA(()),
        ],
        compiler_params=pltpu.CompilerParams(vmem_limit_bytes=4 * MIB),
    )(place, mask)


def queries_of(near, far, i):
    at = (i % 4) * ROWS
    return (near, far)[i // 4][at : at + BLK]


def grads_of(near, far, i):
    at = (i % 4) * ROWS + BLK
    return (near, far)[i // 4][at : at + D_ROWS]


def fill_quads(kvs, cols, buf):
    for quad in range(N_QUAD):
        for odd in range(2):
            at = slice((quad % 2) * WIDE, (quad % 2 + 1) * WIDE)
            buf[quad, odd * WIDE : (odd + 1) * WIDE] = kvs[2 * (quad // 2) + odd][at, cols]


def join(parts, axis=0):
    return parts[0] if len(parts) == 1 else jnp.concatenate(parts, axis=axis)


def heads(ref, i):
    return jnp.concatenate([ref[i, :BLK, h * HD : (h + 1) * HD] for h in range(HEADS)], axis=0)


E_SLOTS = 8


def scores_kernel(half, *refs):
    place, plan, q_in, kv0, kv1, kv2, kv3 = refs[:7]
    if half == 0:
        e_hbm, st, qs, ks, sc, ebuf, mx, lacc, count, e_sem = refs[7:]
    else:
        _, st_in, e_hbm, stats_hbm, qs, ks, sc, ebuf, mx, lacc, count, e_sem, st, st_sem = refs[7:]
        st[...] = st_in[...]
    count[0] = 0
    fill_quads((kv0, kv1, kv2, kv3), slice(0, HD), ks)
    for i in range(N_Q // 2):
        qs[i] = queries_of(q_in, q_in, i)
    diff = (
        lax.broadcasted_iota(jnp.int32, (BLK, WIDE), 1) % BLK
        - lax.broadcasted_iota(jnp.int32, (BLK, WIDE), 0)
    )

    def out_copy(slot, unit):
        return pltpu.make_async_copy(ebuf.at[slot], e_hbm.at[unit], e_sem.at[slot])

    def query_block(row, carry):
        i = half * (N_Q // 2) + row
        base = TABLE + i * T_ROW
        active = plan[base + T_COUNT]
        mx[...] = jnp.full(mx.shape, NEGATIVE, F32)
        lacc[...] = jnp.zeros(lacc.shape, F32)

        def score_quads(quads):
            limits = [plan[LIMITS + i * N_K + 4 * quad + a] for quad in quads for a in range(4)]
            joined = dot(join([ks[quad] for quad in quads]), heads(qs, row), NT)
            for hp in range(2):
                cols = slice(hp * WIDE, (hp + 1) * WIDE)
                best = mx[:, cols]
                for k, quad in enumerate(quads):
                    for a in range(4):
                        at = slice(a * BLK, (a + 1) * BLK)
                        s = joined[k * QUAD + a * BLK : k * QUAD + (a + 1) * BLK, cols]
                        part = jnp.where(diff >= limits[4 * k + a], s, NEGATIVE)
                        sc[quad, at, cols] = part
                        best = jnp.maximum(
                            best, jnp.max(part.reshape(BLK // 8, 8, WIDE), axis=0)
                        )
                mx[:, cols] = best

        def score_pair(n, carry):
            score_quads([plan[base + 2 * n], plan[base + 2 * n + 1]])
            return carry

        lax.fori_loop(0, active // 2, score_pair, 0)

        @pl.when(active % 2 == 1)
        def _():
            score_quads([plan[base + active - 1]])

        m = jnp.maximum(jnp.max(mx[...], axis=0, keepdims=True), FLOOR)

        def exp_quad(k, carry):
            quad = plan[base + k]
            n = count[0]
            slot = n % E_SLOTS

            @pl.when(n >= E_SLOTS)
            def _():
                out_copy(slot, 0).wait()

            for hp in range(2):
                cols = slice(hp * WIDE, (hp + 1) * WIDE)
                e = jnp.exp2((sc[quad, :, cols] - m[:, cols]) * EXP_SCALE)
                lacc[:, cols] += jnp.sum(e.reshape(QUAD // 8, 8, WIDE), axis=0)
                ebuf[slot, :, cols] = e.astype(BF16)
            out_copy(slot, quad * N_Q + i).start()
            count[0] = n + 1
            return carry

        lax.fori_loop(0, active, exp_quad, 0)
        g = place[AT_G + i]
        st[pl.ds(g, 1), :] = m
        st[pl.ds(N_Q + g, 1), :] = jnp.sum(lacc[...], axis=0, keepdims=True)
        return carry

    lax.fori_loop(0, N_Q // 2, query_block, 0)

    if half == 1:
        st_copies = copy_all([(st, stats_hbm.at[g]) for g in range(N_Q)], st_sem)
        for c in st_copies:
            c.start()
        for c in st_copies:
            c.wait()
    for slot_no in range(E_SLOTS):

        @pl.when(count[0] > slot_no)
        def _():
            out_copy(slot_no, 0).wait()


def run_scores(half, place, plan, queries, kvs, before=()):
    stats_shape = (2 * N_Q, COLS)
    return pl.pallas_call(
        functools.partial(scores_kernel, half),
        out_shape=[
            pltpu.HBM((N_QUAD * N_Q, QUAD, COLS), BF16),
            pltpu.HBM((N_Q, *stats_shape), F32) if half else struct(stats_shape, F32),
        ],
        in_specs=[SM, SM] + [VM] * 5 + ([HBM, VM] if half else []),
        out_specs=[HBM, HBM if half else VM],
        scratch_shapes=[
            pltpu.VMEM((N_Q // 2, BLK, COLS), BF16),
            pltpu.VMEM((N_QUAD, QUAD, HD), BF16),
            pltpu.VMEM((N_QUAD, QUAD, COLS), F32),
            pltpu.VMEM((E_SLOTS, QUAD, COLS), BF16),
            pltpu.VMEM((8, COLS), F32),
            pltpu.VMEM((8, COLS), F32),
            pltpu.SMEM((1,), jnp.int32),
            pltpu.SemaphoreType.DMA((E_SLOTS,)),
        ]
        + ([pltpu.VMEM(stats_shape, F32), pltpu.SemaphoreType.DMA((N_Q,))] if half else []),
        input_output_aliases={7: 0} if half else {},
        compiler_params=pltpu.CompilerParams(vmem_limit_bytes=20 * MIB),
    )(place, plan, queries, *kvs, *before)


DEPTH, AHEAD = 8, 6


def loop_units(plan, base, visit):
    pairs, total = plan[base], plan[base + 1]
    singles = total - 2 * pairs

    def pair(n, carry):
        visit([(2 * n, 2)])
        return carry

    def two_singles(n, carry):
        first = 2 * (pairs + n)
        visit([(first, 1), (first + 1, 1)])
        return carry

    lax.fori_loop(0, pairs, pair, 0)
    lax.fori_loop(0, singles // 2, two_singles, 0)

    @pl.when(singles % 2 == 1)
    def _():
        visit([(total - 1, 1)])


def prefetch(plan, base, copies, first, number):
    total = plan[base + 1]
    for k in range(number):

        @pl.when(first + k + AHEAD < total)
        def _():
            for c in copies(first + k + AHEAD):
                c.start()

    for k in range(number):
        for c in copies(first + k):
            c.wait()


def start_first(plan, base, copies):
    for n in range(AHEAD):

        @pl.when(n < plan[base + 1])
        def _():
            for c in copies(n):
                c.start()


def parts_kernel(
    place, plan, near, far, kv0, kv1, kv2, kv3, e_hbm,
    u_hbm, dq_hbm,
    ds, ks, vs, kts, ebuf, ubuf, dqs, dq_low, e_sem, u_sem, dq_sem,
):
    def in_copies(n):
        unit, at = plan[ALL + 2 + n], n % DEPTH
        return (pltpu.make_async_copy(e_hbm.at[unit], ebuf.at[at], e_sem.at[at]),)

    def out_copy(n, unit):
        at = n % DEPTH
        return pltpu.make_async_copy(ubuf.at[at], u_hbm.at[unit], u_sem.at[at])

    start_first(plan, ALL, in_copies)
    kvs = (kv0, kv1, kv2, kv3)
    fill_quads(kvs, slice(0, HD), ks)
    fill_quads(kvs, slice(HD, 2 * HD), vs)
    for i in range(N_Q):
        ds[i] = grads_of(near, far, i)
    dqs[...] = jnp.zeros(dqs.shape, F32)
    for quad in range(N_QUAD):
        kts[quad] = ks[quad].T

    def visit(groups):
        first, number = groups[0][0], sum(g[1] for g in groups)
        for k in range(number):

            @pl.when(first + k >= DEPTH)
            def _():
                out_copy(first + k, 0).wait()

        prefetch(plan, ALL, in_copies, first, number)
        done = []
        for start, size in groups:
            units = [plan[ALL + 2 + start + k] for k in range(size)]
            i, quads = units[0] % N_Q, [unit // N_Q for unit in units]
            extra = ds[i, BLK:, :].astype(F32)
            delta = extra[0:1] + extra[1:2] + extra[2:3]
            da = dot(join([vs[quad] for quad in quads]), heads(ds, i), NT)
            us = []
            for k in range(size):
                at = (start + k) % DEPTH
                u = (ebuf[at].astype(F32) * (da[k * QUAD : (k + 1) * QUAD] - delta)).astype(BF16)
                ubuf[at] = u
                us.append(u)
            done.append((i, dot(join([kts[quad] for quad in quads], axis=1), join(us), NN)))
            for k in range(size):
                out_copy(start + k, units[k]).start()
        for i, part in done:
            dqs[i] += part

    loop_units(plan, ALL, visit)
    dq_copies = copy_all([(dq_low.at[i], dq_hbm.at[place[AT_G + i]]) for i in range(N_Q)], dq_sem)
    for i in range(N_Q):
        dq_low[i] = dqs[i].astype(BF16)
        dq_copies[i].start()
    for c in dq_copies:
        c.wait()
    for n in range(DEPTH):

        @pl.when(n < plan[ALL + 1])
        def _():
            out_copy(n, 0).wait()


def run_parts(place, plan, near, far, kvs, e):
    dma = pltpu.SemaphoreType.DMA
    return pl.pallas_call(
        parts_kernel,
        out_shape=[
            pltpu.HBM((N_QUAD * N_Q, QUAD, COLS), BF16),
            pltpu.HBM((N_Q, HD, COLS), BF16),
        ],
        in_specs=[SM, SM] + [VM] * 6 + [HBM],
        out_specs=[HBM, HBM],
        scratch_shapes=[
            pltpu.VMEM((N_Q, D_ROWS, COLS), BF16),
            pltpu.VMEM((N_QUAD, QUAD, HD), BF16),
            pltpu.VMEM((N_QUAD, QUAD, HD), BF16),
            pltpu.VMEM((N_QUAD, HD, QUAD), BF16),
            pltpu.VMEM((DEPTH, QUAD, COLS), BF16),
            pltpu.VMEM((DEPTH, QUAD, COLS), BF16),
            pltpu.VMEM((N_Q, HD, COLS), F32),
            pltpu.VMEM((N_Q, HD, COLS), BF16),
            dma((DEPTH,)),
            dma((DEPTH,)),
            dma((N_Q,)),
        ],
        compiler_params=pltpu.CompilerParams(vmem_limit_bytes=28 * MIB),
    )(place, plan, near, far, *kvs, e)


def row_weights(place, stats, near, far, ws, wq, wdo):
    ms = [stats[j, :N_Q, :] for j in range(N_Q)]
    top = functools.reduce(jnp.maximum, ms)
    tot = sum(stats[j, N_Q:, :] * jnp.exp2((ms[j] - top) * EXP_SCALE) for j in range(N_Q))
    ws[...] = jnp.exp2((stats[place[AT_OWN], :N_Q, :] - top) * EXP_SCALE) / tot
    rows = []
    for i in range(N_Q):
        w = ws[pl.ds(place[AT_G + i], 1), :]
        rows += [w[:, h * BLK : (h + 1) * BLK] for h in range(HEADS)]
    rows.append(jnp.zeros((BLK - len(rows), BLK), F32))
    cols = jnp.concatenate(rows, axis=0).T
    for i in range(N_Q):
        q = queries_of(near, far, i)
        do = grads_of(near, far, i)
        for h in range(HEADS):
            w = cols[:, i * HEADS + h : i * HEADS + h + 1]
            at = slice(h * BLK, (h + 1) * BLK)
            c = slice(h * HD, (h + 1) * HD)
            wq[i, at, :] = (q[:, c].astype(F32) * w).astype(BF16)
            wdo[i, at, :] = (do[:BLK, c].astype(F32) * w).astype(BF16)


def sum_keys(plan, base, first_quad, rows, wq, wdo, e_hbm, u_hbm, acc, bufs):
    ebuf, ubuf, e_sem, u_sem = bufs
    size = acc.shape[1]

    def in_copies(n):
        unit, at = plan[base + 2 + n], n % DEPTH
        return [
            pltpu.make_async_copy(
                hbm.at[unit, pl.ds(rows, size)], buf.at[at, pl.ds(0, size)], sem.at[at]
            )
            for hbm, buf, sem in ((e_hbm, ebuf, e_sem), (u_hbm, ubuf, u_sem))
        ]

    start_first(plan, base, in_copies)
    acc[...] = jnp.zeros(acc.shape, F32)

    def visit(groups):
        prefetch(plan, base, in_copies, groups[0][0], sum(g[1] for g in groups))
        done = []
        for first, number in groups:
            unit = plan[base + 2 + first]
            i, quad = unit % N_Q, unit // N_Q - first_quad
            for buf, w, cols in ((ubuf, wq, slice(0, HD)), (ebuf, wdo, slice(HD, 2 * HD))):
                rows_of = [buf[(first + k) % DEPTH, :size] for k in range(number)]
                done.append((quad, number, cols, dot(join(rows_of), w[i], NN)))
        for quad, number, cols, part in done:
            for k in range(number):
                acc[quad + k, :, cols] += part[k * size : (k + 1) * size]

    return lambda: loop_units(plan, base, visit)


def far_kernel(
    place, plan, stats, near, far, e_hbm, u_hbm,
    out1, out2, out3, here1, here2, here3, wq_hbm, wdo_hbm,
    ws, wq, wdo, acc, acc_odd, w_sem, *bufs,
):
    w_copies = copy_all([(wq, wq_hbm), (wdo, wdo_hbm)], w_sem)

    sum_far = sum_keys(plan, FAR, 2, 0, wq, wdo, e_hbm, u_hbm, acc, bufs[:4])
    sum_odd = sum_keys(plan, NEAR, 0, WIDE, wq, wdo, e_hbm, u_hbm, acc_odd, bufs[4:])
    row_weights(place, stats, near, far, ws, wq, wdo)
    for c in w_copies:
        c.start()
    sum_far()
    sum_odd()
    for quad in range(2):
        parts = acc_odd[quad], acc[quad, :WIDE], acc[quad, WIDE:]
        for part, out, here in zip(parts, (out1, out2, out3), (here1, here2, here3)):
            part = part.astype(BF16)
            if quad == 0:
                here[...] = part[:BLK]
                out[:BLK, :] = part[BLK:]
            else:
                out[BLK:, :] = part
    for c in w_copies:
        c.wait()


def own_kernel(plan, wq_hbm, wdo_hbm, e_hbm, u_hbm, out, wq, wdo, acc, w_sem, *bufs):
    w_copies = copy_all([(wq_hbm, wq), (wdo_hbm, wdo)], w_sem)
    for c in w_copies:
        c.start()

    sum_own = sum_keys(plan, NEAR, 0, 0, wq, wdo, e_hbm, u_hbm, acc, bufs)
    for c in w_copies:
        c.wait()
    sum_own()
    for quad in range(2):
        out[quad * WIDE : (quad + 1) * WIDE, :] = acc[quad]


def keys_bufs(rows):
    return [
        pltpu.VMEM((DEPTH, rows, COLS), BF16),
        pltpu.VMEM((DEPTH, rows, COLS), BF16),
        pltpu.SemaphoreType.DMA((DEPTH,)),
        pltpu.SemaphoreType.DMA((DEPTH,)),
    ]


def run_far(place, plan, stats, near, far, e, u):
    return pl.pallas_call(
        far_kernel,
        out_shape=[struct((3 * BLK, 2 * HD), BF16)] * 3
        + [struct((BLK, 2 * HD), BF16)] * 3
        + [pltpu.HBM((N_Q, COLS, HD), BF16)] * 2,
        in_specs=[SM, SM] + [VM] * 3 + [HBM, HBM],
        out_specs=[VM] * 6 + [HBM] * 2,
        scratch_shapes=[
            pltpu.VMEM((N_Q, COLS), F32),
            pltpu.VMEM((N_Q, COLS, HD), BF16),
            pltpu.VMEM((N_Q, COLS, HD), BF16),
            pltpu.VMEM((2, QUAD, 2 * HD), F32),
            pltpu.VMEM((2, WIDE, 2 * HD), F32),
            pltpu.SemaphoreType.DMA((2,)),
        ]
        + keys_bufs(QUAD)
        + keys_bufs(WIDE),
        compiler_params=pltpu.CompilerParams(vmem_limit_bytes=24 * MIB),
    )(place, plan, stats, near, far, e, u)


def run_own(plan, wq, wdo, e, u):
    return pl.pallas_call(
        own_kernel,
        out_shape=struct((QUAD, 2 * HD), F32),
        in_specs=[SM] + [HBM] * 4,
        out_specs=VM,
        scratch_shapes=[
            pltpu.VMEM((N_Q, COLS, HD), BF16),
            pltpu.VMEM((N_Q, COLS, HD), BF16),
            pltpu.VMEM((2, WIDE, 2 * HD), F32),
            pltpu.SemaphoreType.DMA((2,)),
        ]
        + keys_bufs(WIDE),
        compiler_params=pltpu.CompilerParams(vmem_limit_bytes=14 * MIB),
    )(plan, wq, wdo, e, u)


def sum_kernel(own, a, b, c, *outs):
    for d, out in enumerate(outs):
        at = slice(d * BLK, (d + 1) * BLK)
        total = own[BLK + d * BLK : BLK + (d + 1) * BLK]
        for part in (a, b, c):
            total += part[at].astype(F32)
        out[...] = total.astype(BF16)


def run_sum(own, a, b, c):
    return pl.pallas_call(
        sum_kernel,
        out_shape=[struct((BLK, 2 * HD), BF16)] * 3,
        in_specs=[VM] * 4,
        out_specs=[VM] * 3,
        compiler_params=pltpu.CompilerParams(vmem_limit_bytes=6 * MIB),
    )(own, a, b, c)


def queries_kernel(place, parts, stats, out):
    own = place[AT_OWN]
    ms = [stats[j, pl.ds(own, 1), :] for j in range(N_Q)]
    ls = [stats[j, pl.ds(N_Q + own, 1), :] for j in range(N_Q)]
    top = functools.reduce(jnp.maximum, ms)
    es = [jnp.exp2((m - top) * EXP_SCALE) for m in ms]
    tot = sum(l * e for l, e in zip(ls, es))
    for h in range(HEADS):
        at = slice(h * HD, (h + 1) * HD)
        total = sum(parts[j, :, at].astype(F32) * es[j][:, at] for j in range(N_Q))
        out[:, at] = (total * (SCALING / tot[:, at])).T


def run_queries(place, parts, stats):
    return pl.pallas_call(
        queries_kernel,
        out_shape=struct((BLK, COLS), F32),
        in_specs=[SM, VM, VM],
        out_specs=VM,
        compiler_params=pltpu.CompilerParams(vmem_limit_bytes=6 * MIB),
    )(place, parts, stats)


def exchange(x, dx=0, dz=0, dy=0, dc=0):
    perm = []
    for b in range(16):
        for r in range(16):
            px = (b // 8) * 2 + (r // 2) % 2
            pz, py, pc = b % 8, r // 4, r % 2
            px, pz, py, pc = px ^ dx, pz ^ (2 * dz), py ^ dy, pc ^ dc
            other = (px // 2) * 8 + pz, py * 4 + (px % 2) * 2 + pc
            perm.append((b * 16 + r, other[0] * 16 + other[1]))
    return lax.ppermute(x, ("blk", "rows"), perm)


Q_GROUPS = [[r for r in range(16) if (r // 2) % 2 == lo] for lo in range(2)]


def to_group(x):
    return lax.all_to_all(x, "rows", 0, 0, axis_index_groups=Q_GROUPS, tiled=True)


def per_device(queries, keys, values, forward_out, grad_out, block_mask):
    b, r = lax.axis_index("blk"), lax.axis_index("rows")
    x = ((b >> 3) << 1) | ((r >> 1) & 1)
    zz, y, core = (b >> 1) & 3, r >> 2, r & 1
    slot_q = jnp.arange(N_Q)
    yq, cq = y ^ jnp.array((2, 0, 1, 3) * 2), core ^ (slot_q >> 2)
    q_blocks = ((b >> 1) << 4) + (yq << 2) + ((x & 1) << 1) + cq
    slot_k = jnp.arange(N_K)
    quad, a = slot_k >> 2, slot_k & 3
    xk = x ^ (((quad >> 1) << 1) | (a >> 1))
    zk = zz ^ (((quad & 1) << 1) | (a & 1))
    k_blocks = ((((xk >> 1) << 2) + zk) << 4) + (y << 2) + ((xk & 1) << 1) + core
    place = jnp.concatenate(
        [(b & 1)[None], q_blocks, k_blocks, (yq << 1) + cq, ((y << 1) + core)[None]]
    ).astype(jnp.int32)

    kv = pack_keys(keys, values)
    kv, queries = lax.optimization_barrier((kv, queries))
    qdo = pack_queries(queries, grad_out, forward_out)

    kv_z = jnp.concatenate([kv] + [exchange(kv, dz=d) for d in (1, 2, 3)], axis=0)
    kvs = [kv_z] + [exchange(kv_z, dx=d) for d in (1, 2, 3)]
    y1, y2, y3 = [exchange(qdo, dy=d) for d in (1, 2, 3)]
    near = jnp.concatenate([y2, qdo, y1, y3], axis=0)
    near, place = lax.optimization_barrier((near, place))
    plan = run_plan(place, pltpu.with_memory_space_constraint(block_mask, pltpu.HBM))
    near, k1, k3, k2, plan = lax.optimization_barrier((near, kvs[1], kvs[3], kvs[2], plan))
    kvs = [kv_z, k1, k2, k3]
    far = exchange(near, dc=1)

    e, totals = run_scores(0, place, plan, near, kvs)
    e = pltpu.with_memory_space_constraint(e, pltpu.HBM)
    e, stat = run_scores(1, place, plan, far, kvs, (e, totals))
    e = pltpu.with_memory_space_constraint(e, pltpu.HBM)
    stats = to_group(stat)
    u, dq = run_parts(place, plan, near, far, kvs, e)
    u = pltpu.with_memory_space_constraint(u, pltpu.HBM)
    dq_parts = to_group(dq)
    *remote, wq, wdo = run_far(place, plan, stats, near, far, e, u)
    wq, wdo = [pltpu.with_memory_space_constraint(w, pltpu.HBM) for w in (wq, wdo)]
    got = [exchange(remote[d - 1], dx=d) for d in (2, 1, 3)]
    wq, dq_parts, *here = lax.optimization_barrier((wq, dq_parts, *remote[3:]))
    here = [exchange(here[d - 1], dx=d) for d in (2, 1, 3)]
    own = run_own(plan, wq, wdo, e, u)
    rest = run_sum(own, *got)
    back = [exchange(rest[d - 1], dz=d) for d in (2, 1, 3)]
    grad_queries = run_queries(place, dq_parts, stats)
    total = own[:BLK] + sum(part.astype(F32) for part in (*back, *here))
    return grad_queries, total[:, :HD] * SCALING, total[:, HD:]


def solution(mesh):
    spec = P(("blk", "rows"), None)
    return jax.shard_map(
        per_device,
        mesh=mesh,
        in_specs=(spec, spec, spec, spec, spec, P()),
        out_specs=(spec, spec, spec),
        check_vma=False,
    )
```

```python
import functools
import math

import jax
import jax.numpy as jnp
from jax import lax
from jax.experimental import pallas as pl
from jax.experimental.pallas import tpu as pltpu
from jax.sharding import PartitionSpec as P

BLK = 128
HEADS = 4
HD = 128
COLS = HEADS * HD
N_Q = 8
N_K = 16
N_QUAD = N_K // 4
QUAD = 4 * BLK
WIDE = 2 * BLK
EXTRA = 16
Y_SLOTS = (2, 0, 1, 3)
D_ROWS = BLK + EXTRA
ROWS = BLK + D_ROWS
NEGATIVE = -1e30
FLOOR = -1e6
SCALING = 1.0 / math.sqrt(HD)
EXP_SCALE = SCALING * math.log2(math.e)
MIB = 1024 * 1024
F32 = jnp.float32
BF16 = jnp.bfloat16
ANY = pl.BlockSpec(memory_space=pl.ANY)
HBM = pl.BlockSpec(memory_space=pltpu.HBM)
VM = pl.BlockSpec(memory_space=pltpu.VMEM)
SM = pl.BlockSpec(memory_space=pltpu.SMEM)

NT = (((1,), (1,)), ((), ()))
NN = (((1,), (0,)), ((), ()))


def dot(a, b, dims):
    return lax.dot_general(a, b, dims, preferred_element_type=F32)


def struct(shape, dtype):
    return jax.ShapeDtypeStruct(shape, dtype)


def copy_all(pairs, sem):
    return [pltpu.make_async_copy(a, b, sem.at[n]) for n, (a, b) in enumerate(pairs)]


def pack_keys_kernel(k_ref, v_ref, kv_ref, sem):
    copies = copy_all(
        [(k_ref, kv_ref.at[:, pl.ds(0, HD)]), (v_ref, kv_ref.at[:, pl.ds(HD, HD)])], sem
    )
    for c in copies:
        c.start()
    for c in copies:
        c.wait()


def pack_queries_kernel(q_ref, do_ref, o_ref, qdo_ref, o_buf, sem):
    copies = copy_all(
        [
            (do_ref, qdo_ref.at[pl.ds(BLK, BLK)]),
            (o_ref, o_buf),
            (q_ref, qdo_ref.at[pl.ds(0, BLK)]),
        ],
        sem,
    )
    for c in copies:
        c.start()
    for c in copies[:2]:
        c.wait()
    prod = qdo_ref[BLK : 2 * BLK, :].astype(F32) * o_buf[...].astype(F32)
    delta = jnp.concatenate(
        [
            jnp.sum(prod[:, h * HD : (h + 1) * HD].T, axis=0, keepdims=True)
            for h in range(HEADS)
        ],
        axis=1,
    )
    high = delta.astype(BF16).astype(F32)
    rest = delta - high
    mid = rest.astype(BF16).astype(F32)
    low = rest - mid
    row = lax.broadcasted_iota(jnp.int32, (EXTRA, COLS), 0)
    extra = jnp.where(row == 0, high, jnp.where(row == 1, mid, jnp.where(row == 2, low, 0.0)))
    qdo_ref[2 * BLK :, :] = extra.astype(BF16)
    copies[2].wait()


def pack_keys(keys, values):
    return pl.pallas_call(
        pack_keys_kernel,
        out_shape=struct((BLK, 2 * HD), BF16),
        in_specs=[HBM] * 2,
        out_specs=VM,
        scratch_shapes=[pltpu.SemaphoreType.DMA((2,))],
        compiler_params=pltpu.CompilerParams(vmem_limit_bytes=4 * MIB),
    )(*[pltpu.with_memory_space_constraint(a, pltpu.HBM) for a in (keys, values)])


def pack_queries(queries, grad_out, forward_out):
    return pl.pallas_call(
        pack_queries_kernel,
        out_shape=struct((ROWS, COLS), BF16),
        in_specs=[HBM] * 3,
        out_specs=VM,
        scratch_shapes=[pltpu.VMEM((BLK, COLS), BF16), pltpu.SemaphoreType.DMA((3,))],
        compiler_params=pltpu.CompilerParams(vmem_limit_bytes=6 * MIB),
    )(*[pltpu.with_memory_space_constraint(a, pltpu.HBM) for a in (queries, grad_out, forward_out)])


LIMITS, TABLE, ALL, FAR, NEAR = 0, 128, 192, 256, 288
AT_Q, AT_K, AT_G, AT_OWN, PLAN = 320, 328, 344, 352, 384
T_ROW, T_COUNT = 8, 4


def plan_kernel(ids, mask_hbm, plan, mask_s, found, sem):
    b, r = ids[0], ids[1]
    copy = pltpu.make_async_copy(mask_hbm.at[b & 1], mask_s, sem)
    copy.start()
    x = ((b >> 3) << 1) | ((r >> 1) & 1)
    zz, y, core = (b >> 1) & 3, r >> 2, r & 1
    for i in range(N_Q):
        yq, cq = y ^ Y_SLOTS[i % 4], core ^ (i // 4)
        plan[AT_Q + i] = ((b >> 1) << 4) + (yq << 2) + ((x & 1) << 1) + cq
        plan[AT_G + i] = (yq << 1) + cq
    for s in range(N_K):
        quad, a = s // 4, s % 4
        xk = x ^ (quad // 2 * 2 + a // 2)
        zk = zz ^ (quad % 2 * 2 + a % 2)
        plan[AT_K + s] = ((((xk >> 1) << 2) + zk) << 4) + (y << 2) + ((xk & 1) << 1) + core
    plan[AT_OWN] = (y << 1) + core
    copy.wait()

    def row(i, carry):
        at = plan[AT_Q + i]
        active = jnp.int32(0)
        for quad in range(N_QUAD):
            seen = jnp.int32(0)
            for a in range(4):
                level = mask_s[at, plan[AT_K + 4 * quad + a]]
                plan[LIMITS + i * N_K + 4 * quad + a] = jnp.where(
                    level == 1, -BLK, jnp.where(level == 2, 0, BLK)
                )
                seen = seen | level
            plan[TABLE + i * T_ROW + active] = quad
            active += jnp.where(seen != 0, 1, 0)
        plan[TABLE + i * T_ROW + T_COUNT] = active
        return carry

    lax.fori_loop(0, N_Q, row, 0)

    n = jnp.int32(0)
    for i in range(N_Q):
        count = plan[TABLE + i * T_ROW + T_COUNT]
        for j in range(2):
            plan[ALL + 2 + n] = plan[TABLE + i * T_ROW + 2 * j] * N_Q + i
            plan[ALL + 3 + n] = plan[TABLE + i * T_ROW + 2 * j + 1] * N_Q + i
            n += jnp.where(count >= 2 * j + 2, 2, 0)
    plan[ALL] = n // 2
    for i in range(N_Q):
        count = plan[TABLE + i * T_ROW + T_COUNT]
        plan[ALL + 2 + n] = plan[TABLE + i * T_ROW + jnp.maximum(count - 1, 0)] * N_Q + i
        n += count % 2
    plan[ALL + 1] = n

    for base, quads in ((NEAR, (0, 1)), (FAR, (2, 3))):
        n = jnp.int32(0)
        for i in range(N_Q):
            has = [jnp.int32(0), jnp.int32(0)]
            for k in range(2):
                for a in range(N_QUAD):
                    here = (plan[TABLE + i * T_ROW + a] == quads[k]) & (
                        a < plan[TABLE + i * T_ROW + T_COUNT]
                    )
                    has[k] = has[k] | jnp.where(here, 1, 0)
            found[2 * i] = has[0]
            found[2 * i + 1] = has[1]
            plan[base + 2 + n] = quads[0] * N_Q + i
            plan[base + 3 + n] = quads[1] * N_Q + i
            n += 2 * (has[0] & has[1])
        plan[base] = n // 2
        for i in range(N_Q):
            plan[base + 2 + n] = (quads[0] + found[2 * i + 1]) * N_Q + i
            n += found[2 * i] ^ found[2 * i + 1]
        plan[base + 1] = n


def run_plan(ids, mask):
    return pl.pallas_call(
        plan_kernel,
        out_shape=struct((PLAN,), jnp.int32),
        in_specs=[SM, HBM],
        out_specs=SM,
        scratch_shapes=[
            pltpu.SMEM((BLK, BLK), jnp.int32),
            pltpu.SMEM((32,), jnp.int32),
            pltpu.SemaphoreType.DMA(()),
        ],
        compiler_params=pltpu.CompilerParams(vmem_limit_bytes=4 * MIB),
    )(ids, mask)


def queries_of(near, far, i):
    at = (i % 4) * ROWS
    return (near, far)[i // 4][at : at + BLK]


def grads_of(near, far, i):
    at = (i % 4) * ROWS + BLK
    return (near, far)[i // 4][at : at + D_ROWS]


def fill_quads(kvs, cols, buf):
    for quad in range(N_QUAD):
        for odd in range(2):
            at = slice((quad % 2) * WIDE, (quad % 2 + 1) * WIDE)
            buf[quad, odd * WIDE : (odd + 1) * WIDE] = kvs[2 * (quad // 2) + odd][at, cols]


def join(parts, axis=0):
    return parts[0] if len(parts) == 1 else jnp.concatenate(parts, axis=axis)


def heads(ref, i):
    return jnp.concatenate([ref[i, :BLK, h * HD : (h + 1) * HD] for h in range(HEADS)], axis=0)


E_SLOTS = 8


def scores_kernel(half, *refs):
    plan, q_in, kv0, kv1, kv2, kv3 = refs[:6]
    if half == 0:
        e_hbm, st, qs, ks, sc, ebuf, mx, lacc, count, e_sem = refs[6:]
    else:
        _, st_in, e_hbm, stats_hbm, qs, ks, sc, ebuf, mx, lacc, count, e_sem, st, st_sem = refs[6:]
        st[...] = st_in[...]
    count[0] = 0
    fill_quads((kv0, kv1, kv2, kv3), slice(0, HD), ks)
    for i in range(N_Q // 2):
        qs[i] = queries_of(q_in, q_in, i)
    diff = (
        lax.broadcasted_iota(jnp.int32, (BLK, WIDE), 1) % BLK
        - lax.broadcasted_iota(jnp.int32, (BLK, WIDE), 0)
    )

    def out_copy(slot, unit):
        return pltpu.make_async_copy(ebuf.at[slot], e_hbm.at[unit], e_sem.at[slot])

    def query_block(row, carry):
        i = half * (N_Q // 2) + row
        base = TABLE + i * T_ROW
        active = plan[base + T_COUNT]
        mx[...] = jnp.full(mx.shape, NEGATIVE, F32)
        lacc[...] = jnp.zeros(lacc.shape, F32)

        def score_quads(quads):
            limits = [plan[LIMITS + i * N_K + 4 * quad + a] for quad in quads for a in range(4)]
            joined = dot(join([ks[quad] for quad in quads]), heads(qs, row), NT)
            for hp in range(2):
                cols = slice(hp * WIDE, (hp + 1) * WIDE)
                best = mx[:, cols]
                for k, quad in enumerate(quads):
                    for a in range(4):
                        at = slice(a * BLK, (a + 1) * BLK)
                        s = joined[k * QUAD + a * BLK : k * QUAD + (a + 1) * BLK, cols]
                        part = jnp.where(diff >= limits[4 * k + a], s, NEGATIVE)
                        sc[quad, at, cols] = part
                        best = jnp.maximum(
                            best, jnp.max(part.reshape(BLK // 8, 8, WIDE), axis=0)
                        )
                mx[:, cols] = best

        def score_pair(n, carry):
            score_quads([plan[base + 2 * n], plan[base + 2 * n + 1]])
            return carry

        lax.fori_loop(0, active // 2, score_pair, 0)

        @pl.when(active % 2 == 1)
        def _():
            score_quads([plan[base + active - 1]])

        m = jnp.maximum(jnp.max(mx[...], axis=0, keepdims=True), FLOOR)

        def exp_quad(k, carry):
            quad = plan[base + k]
            n = count[0]
            slot = n % E_SLOTS

            @pl.when(n >= E_SLOTS)
            def _():
                out_copy(slot, 0).wait()

            for hp in range(2):
                cols = slice(hp * WIDE, (hp + 1) * WIDE)
                e = jnp.exp2((sc[quad, :, cols] - m[:, cols]) * EXP_SCALE)
                lacc[:, cols] += jnp.sum(e.reshape(QUAD // 8, 8, WIDE), axis=0)
                ebuf[slot, :, cols] = e.astype(BF16)
            out_copy(slot, quad * N_Q + i).start()
            count[0] = n + 1
            return carry

        lax.fori_loop(0, active, exp_quad, 0)
        g = plan[AT_G + i]
        st[pl.ds(g, 1), :] = m
        st[pl.ds(N_Q + g, 1), :] = jnp.sum(lacc[...], axis=0, keepdims=True)
        return carry

    lax.fori_loop(0, N_Q // 2, query_block, 0)

    if half == 1:
        st_copies = copy_all([(st, stats_hbm.at[g]) for g in range(N_Q)], st_sem)
        for c in st_copies:
            c.start()
        for c in st_copies:
            c.wait()
    for slot_no in range(E_SLOTS):

        @pl.when(count[0] > slot_no)
        def _():
            out_copy(slot_no, 0).wait()


def run_scores(half, plan, queries, kvs, before=()):
    stats_shape = (2 * N_Q, COLS)
    return pl.pallas_call(
        functools.partial(scores_kernel, half),
        out_shape=[
            pltpu.HBM((N_QUAD * N_Q, QUAD, COLS), BF16),
            pltpu.HBM((N_Q, *stats_shape), F32) if half else struct(stats_shape, F32),
        ],
        in_specs=[SM] + [VM] * 5 + ([HBM, VM] if half else []),
        out_specs=[HBM, HBM if half else VM],
        scratch_shapes=[
            pltpu.VMEM((N_Q // 2, BLK, COLS), BF16),
            pltpu.VMEM((N_QUAD, QUAD, HD), BF16),
            pltpu.VMEM((N_QUAD, QUAD, COLS), F32),
            pltpu.VMEM((E_SLOTS, QUAD, COLS), BF16),
            pltpu.VMEM((8, COLS), F32),
            pltpu.VMEM((8, COLS), F32),
            pltpu.SMEM((1,), jnp.int32),
            pltpu.SemaphoreType.DMA((E_SLOTS,)),
        ]
        + ([pltpu.VMEM(stats_shape, F32), pltpu.SemaphoreType.DMA((N_Q,))] if half else []),
        input_output_aliases={6: 0} if half else {},
        compiler_params=pltpu.CompilerParams(vmem_limit_bytes=20 * MIB),
    )(plan, queries, *kvs, *before)


DEPTH, AHEAD = 8, 6


def loop_units(plan, base, visit):
    pairs, total = plan[base], plan[base + 1]
    singles = total - 2 * pairs

    def pair(n, carry):
        visit([(2 * n, 2)])
        return carry

    def two_singles(n, carry):
        first = 2 * (pairs + n)
        visit([(first, 1), (first + 1, 1)])
        return carry

    lax.fori_loop(0, pairs, pair, 0)
    lax.fori_loop(0, singles // 2, two_singles, 0)

    @pl.when(singles % 2 == 1)
    def _():
        visit([(total - 1, 1)])


def prefetch(plan, base, copies, first, number):
    total = plan[base + 1]
    for k in range(number):

        @pl.when(first + k + AHEAD < total)
        def _():
            for c in copies(first + k + AHEAD):
                c.start()

    for k in range(number):
        for c in copies(first + k):
            c.wait()


def start_first(plan, base, copies):
    for n in range(AHEAD):

        @pl.when(n < plan[base + 1])
        def _():
            for c in copies(n):
                c.start()


def parts_kernel(
    plan, near, far, kv0, kv1, kv2, kv3, e_hbm,
    u_hbm, dq_hbm,
    ds, ks, vs, kts, ebuf, ubuf, dqs, dq_low, e_sem, u_sem, dq_sem,
):
    def in_copies(n):
        unit, at = plan[ALL + 2 + n], n % DEPTH
        return (pltpu.make_async_copy(e_hbm.at[unit], ebuf.at[at], e_sem.at[at]),)

    def out_copy(n, unit):
        at = n % DEPTH
        return pltpu.make_async_copy(ubuf.at[at], u_hbm.at[unit], u_sem.at[at])

    start_first(plan, ALL, in_copies)
    kvs = (kv0, kv1, kv2, kv3)
    fill_quads(kvs, slice(0, HD), ks)
    fill_quads(kvs, slice(HD, 2 * HD), vs)
    for i in range(N_Q):
        ds[i] = grads_of(near, far, i)
    dqs[...] = jnp.zeros(dqs.shape, F32)
    for quad in range(N_QUAD):
        kts[quad] = ks[quad].T

    def visit(groups):
        first, number = groups[0][0], sum(g[1] for g in groups)
        for k in range(number):

            @pl.when(first + k >= DEPTH)
            def _():
                out_copy(first + k, 0).wait()

        prefetch(plan, ALL, in_copies, first, number)
        done = []
        for start, size in groups:
            units = [plan[ALL + 2 + start + k] for k in range(size)]
            i, quads = units[0] % N_Q, [unit // N_Q for unit in units]
            extra = ds[i, BLK:, :].astype(F32)
            delta = extra[0:1] + extra[1:2] + extra[2:3]
            da = dot(join([vs[quad] for quad in quads]), heads(ds, i), NT)
            us = []
            for k in range(size):
                at = (start + k) % DEPTH
                u = (ebuf[at].astype(F32) * (da[k * QUAD : (k + 1) * QUAD] - delta)).astype(BF16)
                ubuf[at] = u
                us.append(u)
            done.append((i, dot(join([kts[quad] for quad in quads], axis=1), join(us), NN)))
            for k in range(size):
                out_copy(start + k, units[k]).start()
        for i, part in done:
            dqs[i] += part

    loop_units(plan, ALL, visit)
    dq_copies = copy_all([(dq_low.at[i], dq_hbm.at[plan[AT_G + i]]) for i in range(N_Q)], dq_sem)
    for i in range(N_Q):
        dq_low[i] = dqs[i].astype(BF16)
        dq_copies[i].start()
    for c in dq_copies:
        c.wait()
    for n in range(DEPTH):

        @pl.when(n < plan[ALL + 1])
        def _():
            out_copy(n, 0).wait()


def run_parts(plan, near, far, kvs, e):
    dma = pltpu.SemaphoreType.DMA
    return pl.pallas_call(
        parts_kernel,
        out_shape=[
            pltpu.HBM((N_QUAD * N_Q, QUAD, COLS), BF16),
            pltpu.HBM((N_Q, HD, COLS), BF16),
        ],
        in_specs=[SM] + [VM] * 6 + [HBM],
        out_specs=[HBM, HBM],
        scratch_shapes=[
            pltpu.VMEM((N_Q, D_ROWS, COLS), BF16),
            pltpu.VMEM((N_QUAD, QUAD, HD), BF16),
            pltpu.VMEM((N_QUAD, QUAD, HD), BF16),
            pltpu.VMEM((N_QUAD, HD, QUAD), BF16),
            pltpu.VMEM((DEPTH, QUAD, COLS), BF16),
            pltpu.VMEM((DEPTH, QUAD, COLS), BF16),
            pltpu.VMEM((N_Q, HD, COLS), F32),
            pltpu.VMEM((N_Q, HD, COLS), BF16),
            dma((DEPTH,)),
            dma((DEPTH,)),
            dma((N_Q,)),
        ],
        compiler_params=pltpu.CompilerParams(vmem_limit_bytes=28 * MIB),
    )(plan, near, far, *kvs, e)


def row_weights(plan, stats, near, far, ws, wq, wdo):
    ms = [stats[j, :N_Q, :] for j in range(N_Q)]
    top = functools.reduce(jnp.maximum, ms)
    tot = sum(stats[j, N_Q:, :] * jnp.exp2((ms[j] - top) * EXP_SCALE) for j in range(N_Q))
    ws[...] = jnp.exp2((stats[plan[AT_OWN], :N_Q, :] - top) * EXP_SCALE) / tot
    rows = []
    for i in range(N_Q):
        w = ws[pl.ds(plan[AT_G + i], 1), :]
        rows += [w[:, h * BLK : (h + 1) * BLK] for h in range(HEADS)]
    rows.append(jnp.zeros((BLK - len(rows), BLK), F32))
    cols = jnp.concatenate(rows, axis=0).T
    for i in range(N_Q):
        q = queries_of(near, far, i)
        do = grads_of(near, far, i)
        for h in range(HEADS):
            w = cols[:, i * HEADS + h : i * HEADS + h + 1]
            at = slice(h * BLK, (h + 1) * BLK)
            c = slice(h * HD, (h + 1) * HD)
            wq[i, at, :] = (q[:, c].astype(F32) * w).astype(BF16)
            wdo[i, at, :] = (do[:BLK, c].astype(F32) * w).astype(BF16)


def sum_keys(plan, base, first_quad, rows, wq, wdo, e_hbm, u_hbm, acc, bufs):
    ebuf, ubuf, e_sem, u_sem = bufs
    size = acc.shape[1]

    def in_copies(n):
        unit, at = plan[base + 2 + n], n % DEPTH
        return [
            pltpu.make_async_copy(
                hbm.at[unit, pl.ds(rows, size)], buf.at[at, pl.ds(0, size)], sem.at[at]
            )
            for hbm, buf, sem in ((e_hbm, ebuf, e_sem), (u_hbm, ubuf, u_sem))
        ]

    start_first(plan, base, in_copies)
    acc[...] = jnp.zeros(acc.shape, F32)

    def visit(groups):
        prefetch(plan, base, in_copies, groups[0][0], sum(g[1] for g in groups))
        done = []
        for first, number in groups:
            unit = plan[base + 2 + first]
            i, quad = unit % N_Q, unit // N_Q - first_quad
            for buf, w, cols in ((ubuf, wq, slice(0, HD)), (ebuf, wdo, slice(HD, 2 * HD))):
                rows_of = [buf[(first + k) % DEPTH, :size] for k in range(number)]
                done.append((quad, number, cols, dot(join(rows_of), w[i], NN)))
        for quad, number, cols, part in done:
            for k in range(number):
                acc[quad + k, :, cols] += part[k * size : (k + 1) * size]

    return lambda: loop_units(plan, base, visit)


def far_kernel(
    plan, stats, near, far, e_hbm, u_hbm,
    out1, out2, out3, wq_hbm, wdo_hbm,
    ws, wq, wdo, acc, acc_odd, w_sem, *bufs,
):
    w_copies = copy_all([(wq, wq_hbm), (wdo, wdo_hbm)], w_sem)

    sum_far = sum_keys(plan, FAR, 2, 0, wq, wdo, e_hbm, u_hbm, acc, bufs[:4])
    sum_odd = sum_keys(plan, NEAR, 0, WIDE, wq, wdo, e_hbm, u_hbm, acc_odd, bufs[4:])
    row_weights(plan, stats, near, far, ws, wq, wdo)
    for c in w_copies:
        c.start()
    sum_far()
    sum_odd()
    for quad in range(2):
        at = slice(quad * WIDE, (quad + 1) * WIDE)
        out1[at, :] = acc_odd[quad].astype(BF16)
        out2[at, :] = acc[quad, :WIDE].astype(BF16)
        out3[at, :] = acc[quad, WIDE:].astype(BF16)
    for c in w_copies:
        c.wait()


def own_kernel(plan, wq_hbm, wdo_hbm, e_hbm, u_hbm, out, wq, wdo, acc, w_sem, *bufs):
    w_copies = copy_all([(wq_hbm, wq), (wdo_hbm, wdo)], w_sem)
    for c in w_copies:
        c.start()

    sum_own = sum_keys(plan, NEAR, 0, 0, wq, wdo, e_hbm, u_hbm, acc, bufs)
    for c in w_copies:
        c.wait()
    sum_own()
    for quad in range(2):
        out[quad * WIDE : (quad + 1) * WIDE, :] = acc[quad]


def keys_bufs(rows):
    return [
        pltpu.VMEM((DEPTH, rows, COLS), BF16),
        pltpu.VMEM((DEPTH, rows, COLS), BF16),
        pltpu.SemaphoreType.DMA((DEPTH,)),
        pltpu.SemaphoreType.DMA((DEPTH,)),
    ]


def run_far(plan, stats, near, far, e, u):
    return pl.pallas_call(
        far_kernel,
        out_shape=[struct((QUAD, 2 * HD), BF16)] * 3 + [pltpu.HBM((N_Q, COLS, HD), BF16)] * 2,
        in_specs=[SM] + [VM] * 3 + [HBM, HBM],
        out_specs=[VM] * 3 + [HBM] * 2,
        scratch_shapes=[
            pltpu.VMEM((N_Q, COLS), F32),
            pltpu.VMEM((N_Q, COLS, HD), BF16),
            pltpu.VMEM((N_Q, COLS, HD), BF16),
            pltpu.VMEM((2, QUAD, 2 * HD), F32),
            pltpu.VMEM((2, WIDE, 2 * HD), F32),
            pltpu.SemaphoreType.DMA((2,)),
        ]
        + keys_bufs(QUAD)
        + keys_bufs(WIDE),
        compiler_params=pltpu.CompilerParams(vmem_limit_bytes=24 * MIB),
    )(plan, stats, near, far, e, u)


def run_own(plan, wq, wdo, e, u):
    return pl.pallas_call(
        own_kernel,
        out_shape=struct((QUAD, 2 * HD), F32),
        in_specs=[SM] + [HBM] * 4,
        out_specs=VM,
        scratch_shapes=[
            pltpu.VMEM((N_Q, COLS, HD), BF16),
            pltpu.VMEM((N_Q, COLS, HD), BF16),
            pltpu.VMEM((2, WIDE, 2 * HD), F32),
            pltpu.SemaphoreType.DMA((2,)),
        ]
        + keys_bufs(WIDE),
        compiler_params=pltpu.CompilerParams(vmem_limit_bytes=14 * MIB),
    )(plan, wq, wdo, e, u)


def sum_kernel(own, a, b, c, out0, out1, out2, out3):
    for d, out in enumerate((out0, out1, out2, out3)):
        at = slice(d * BLK, (d + 1) * BLK)
        total = own[at] + a[at].astype(F32) + b[at].astype(F32) + c[at].astype(F32)
        out[...] = total.astype(out.dtype)


def run_sum(own, a, b, c):
    return pl.pallas_call(
        sum_kernel,
        out_shape=[struct((BLK, 2 * HD), F32)] + [struct((BLK, 2 * HD), BF16)] * 3,
        in_specs=[VM] * 4,
        out_specs=[VM] * 4,
        compiler_params=pltpu.CompilerParams(vmem_limit_bytes=6 * MIB),
    )(own, a, b, c)


def queries_kernel(plan, parts, stats, out):
    own = plan[AT_OWN]
    ms = [stats[j, pl.ds(own, 1), :] for j in range(N_Q)]
    ls = [stats[j, pl.ds(N_Q + own, 1), :] for j in range(N_Q)]
    top = functools.reduce(jnp.maximum, ms)
    es = [jnp.exp2((m - top) * EXP_SCALE) for m in ms]
    tot = sum(l * e for l, e in zip(ls, es))
    for h in range(HEADS):
        at = slice(h * HD, (h + 1) * HD)
        total = sum(parts[j, :, at].astype(F32) * es[j][:, at] for j in range(N_Q))
        out[:, at] = (total * (SCALING / tot[:, at])).T


def run_queries(plan, parts, stats):
    return pl.pallas_call(
        queries_kernel,
        out_shape=struct((BLK, COLS), F32),
        in_specs=[SM, VM, VM],
        out_specs=VM,
        compiler_params=pltpu.CompilerParams(vmem_limit_bytes=6 * MIB),
    )(plan, parts, stats)


def exchange(x, dx=0, dz=0, dy=0, dc=0):
    perm = []
    for b in range(16):
        for r in range(16):
            px = (b // 8) * 2 + (r // 2) % 2
            pz, py, pc = b % 8, r // 4, r % 2
            px, pz, py, pc = px ^ dx, pz ^ (2 * dz), py ^ dy, pc ^ dc
            other = (px // 2) * 8 + pz, py * 4 + (px % 2) * 2 + pc
            perm.append((b * 16 + r, other[0] * 16 + other[1]))
    return lax.ppermute(x, ("blk", "rows"), perm)


Q_GROUPS = [[r for r in range(16) if (r // 2) % 2 == lo] for lo in range(2)]


def to_group(x):
    return lax.all_to_all(x, "rows", 0, 0, axis_index_groups=Q_GROUPS, tiled=True)


def per_device(queries, keys, values, forward_out, grad_out, block_mask):
    b, r = lax.axis_index("blk"), lax.axis_index("rows")
    ids = jnp.stack([b, r]).astype(jnp.int32)

    kv = pack_keys(keys, values)
    kv, queries = lax.optimization_barrier((kv, queries))
    qdo = pack_queries(queries, grad_out, forward_out)

    kv_z = jnp.concatenate([kv] + [exchange(kv, dz=d) for d in (1, 2, 3)], axis=0)
    kvs = [kv_z] + [exchange(kv_z, dx=d) for d in (1, 2, 3)]
    y1, y2, y3 = [exchange(qdo, dy=d) for d in (1, 2, 3)]
    near = jnp.concatenate([y2, qdo, y1, y3], axis=0)
    ids, _ = lax.optimization_barrier((ids, y3))
    plan = run_plan(ids, pltpu.with_memory_space_constraint(block_mask, pltpu.HBM))
    near, k1, k3, k2, plan = lax.optimization_barrier((near, kvs[1], kvs[3], kvs[2], plan))
    kvs = [kv_z, k1, k2, k3]
    far = exchange(near, dc=1)

    e, totals = run_scores(0, plan, near, kvs)
    e = pltpu.with_memory_space_constraint(e, pltpu.HBM)
    e, stat = run_scores(1, plan, far, kvs, (e, totals))
    e = pltpu.with_memory_space_constraint(e, pltpu.HBM)
    stats = to_group(stat)
    u, dq = run_parts(plan, near, far, kvs, e)
    u = pltpu.with_memory_space_constraint(u, pltpu.HBM)
    dq_parts = to_group(dq)
    *remote, wq, wdo = run_far(plan, stats, near, far, e, u)
    wq, wdo = [pltpu.with_memory_space_constraint(w, pltpu.HBM) for w in (wq, wdo)]
    got = [exchange(remote[d - 1], dx=d) for d in (2, 1, 3)]
    wq, dq_parts = lax.optimization_barrier((wq, dq_parts))
    own = run_own(plan, wq, wdo, e, u)
    mine, *rest = run_sum(own, *got)
    back = [exchange(rest[d - 1], dz=d) for d in (2, 1, 3)]
    grad_queries = run_queries(plan, dq_parts, stats)
    total = mine + sum(part.astype(F32) for part in back)
    return grad_queries, total[:, :HD] * SCALING, total[:, HD:]


def solution(mesh):
    spec = P(("blk", "rows"), None)
    return jax.shard_map(
        per_device,
        mesh=mesh,
        in_specs=(spec, spec, spec, spec, spec, P()),
        out_specs=(spec, spec, spec),
        check_vma=False,
    )
```

```python
import functools
import math

import jax
import jax.numpy as jnp
from jax import lax
from jax.experimental import pallas as pl
from jax.experimental.pallas import tpu as pltpu
from jax.sharding import PartitionSpec as P

BLK = 128
HEADS = 4
HD = 128
COLS = HEADS * HD
N_Q = 8
N_K = 16
N_QUAD = N_K // 4
QUAD = 4 * BLK
WIDE = 2 * BLK
EXTRA = 16
Y_SLOTS = (2, 0, 1, 3)
D_ROWS = BLK + EXTRA
ROWS = BLK + D_ROWS
NEGATIVE = -1e30
FLOOR = -1e6
SCALING = 1.0 / math.sqrt(HD)
EXP_SCALE = SCALING * math.log2(math.e)
MIB = 1024 * 1024
F32 = jnp.float32
BF16 = jnp.bfloat16
ANY = pl.BlockSpec(memory_space=pl.ANY)
HBM = pl.BlockSpec(memory_space=pltpu.HBM)
VM = pl.BlockSpec(memory_space=pltpu.VMEM)
SM = pl.BlockSpec(memory_space=pltpu.SMEM)

NT = (((1,), (1,)), ((), ()))
NN = (((1,), (0,)), ((), ()))


def dot(a, b, dims):
    return lax.dot_general(a, b, dims, preferred_element_type=F32)


def struct(shape, dtype):
    return jax.ShapeDtypeStruct(shape, dtype)


def copy_all(pairs, sem):
    return [pltpu.make_async_copy(a, b, sem.at[n]) for n, (a, b) in enumerate(pairs)]


def pack_keys_kernel(k_ref, v_ref, kv_ref, sem):
    copies = copy_all(
        [(k_ref, kv_ref.at[:, pl.ds(0, HD)]), (v_ref, kv_ref.at[:, pl.ds(HD, HD)])], sem
    )
    for c in copies:
        c.start()
    for c in copies:
        c.wait()


def pack_queries_kernel(q_ref, do_ref, o_ref, qdo_ref, o_buf, sem):
    copies = copy_all(
        [
            (do_ref, qdo_ref.at[pl.ds(BLK, BLK)]),
            (o_ref, o_buf),
            (q_ref, qdo_ref.at[pl.ds(0, BLK)]),
        ],
        sem,
    )
    for c in copies:
        c.start()
    for c in copies[:2]:
        c.wait()
    prod = qdo_ref[BLK : 2 * BLK, :].astype(F32) * o_buf[...].astype(F32)
    delta = jnp.concatenate(
        [
            jnp.sum(prod[:, h * HD : (h + 1) * HD].T, axis=0, keepdims=True)
            for h in range(HEADS)
        ],
        axis=1,
    )
    high = delta.astype(BF16).astype(F32)
    rest = delta - high
    mid = rest.astype(BF16).astype(F32)
    low = rest - mid
    row = lax.broadcasted_iota(jnp.int32, (EXTRA, COLS), 0)
    extra = jnp.where(row == 0, high, jnp.where(row == 1, mid, jnp.where(row == 2, low, 0.0)))
    qdo_ref[2 * BLK :, :] = extra.astype(BF16)
    copies[2].wait()


def pack_keys(keys, values):
    return pl.pallas_call(
        pack_keys_kernel,
        out_shape=struct((BLK, 2 * HD), BF16),
        in_specs=[HBM] * 2,
        out_specs=VM,
        scratch_shapes=[pltpu.SemaphoreType.DMA((2,))],
        compiler_params=pltpu.CompilerParams(vmem_limit_bytes=4 * MIB),
    )(*[pltpu.with_memory_space_constraint(a, pltpu.HBM) for a in (keys, values)])


def pack_queries(queries, grad_out, forward_out):
    return pl.pallas_call(
        pack_queries_kernel,
        out_shape=struct((ROWS, COLS), BF16),
        in_specs=[HBM] * 3,
        out_specs=VM,
        scratch_shapes=[pltpu.VMEM((BLK, COLS), BF16), pltpu.SemaphoreType.DMA((3,))],
        compiler_params=pltpu.CompilerParams(vmem_limit_bytes=6 * MIB),
    )(*[pltpu.with_memory_space_constraint(a, pltpu.HBM) for a in (queries, grad_out, forward_out)])


LIMITS, TABLE, ALL, FAR, NEAR = 0, 128, 192, 256, 288
AT_Q, AT_K, AT_G, AT_OWN, PLAN = 320, 328, 344, 352, 384
T_ROW, T_COUNT = 8, 4


def plan_kernel(ids, mask_hbm, plan, mask_s, found, sem):
    b, r = ids[0], ids[1]
    copy = pltpu.make_async_copy(mask_hbm.at[b & 1], mask_s, sem)
    copy.start()
    x = ((b >> 3) << 1) | ((r >> 1) & 1)
    zz, y, core = (b >> 1) & 3, r >> 2, r & 1
    for i in range(N_Q):
        yq, cq = y ^ Y_SLOTS[i % 4], core ^ (i // 4)
        plan[AT_Q + i] = ((b >> 1) << 4) + (yq << 2) + ((x & 1) << 1) + cq
        plan[AT_G + i] = (yq << 1) + cq
    for s in range(N_K):
        quad, a = s // 4, s % 4
        xk = x ^ (quad // 2 * 2 + a // 2)
        zk = zz ^ (quad % 2 * 2 + a % 2)
        plan[AT_K + s] = ((((xk >> 1) << 2) + zk) << 4) + (y << 2) + ((xk & 1) << 1) + core
    plan[AT_OWN] = (y << 1) + core
    copy.wait()

    def row(i, carry):
        at = plan[AT_Q + i]
        active = jnp.int32(0)
        for quad in range(N_QUAD):
            seen = jnp.int32(0)
            for a in range(4):
                level = mask_s[at, plan[AT_K + 4 * quad + a]]
                plan[LIMITS + i * N_K + 4 * quad + a] = jnp.where(
                    level == 1, -BLK, jnp.where(level == 2, 0, BLK)
                )
                seen = seen | level
            plan[TABLE + i * T_ROW + active] = quad
            active += jnp.where(seen != 0, 1, 0)
        plan[TABLE + i * T_ROW + T_COUNT] = active
        return carry

    lax.fori_loop(0, N_Q, row, 0)

    n = jnp.int32(0)
    for i in range(N_Q):
        count = plan[TABLE + i * T_ROW + T_COUNT]
        for j in range(2):
            plan[ALL + 2 + n] = plan[TABLE + i * T_ROW + 2 * j] * N_Q + i
            plan[ALL + 3 + n] = plan[TABLE + i * T_ROW + 2 * j + 1] * N_Q + i
            n += jnp.where(count >= 2 * j + 2, 2, 0)
    plan[ALL] = n // 2
    for i in range(N_Q):
        count = plan[TABLE + i * T_ROW + T_COUNT]
        plan[ALL + 2 + n] = plan[TABLE + i * T_ROW + jnp.maximum(count - 1, 0)] * N_Q + i
        n += count % 2
    plan[ALL + 1] = n

    for base, quads in ((NEAR, (0, 1)), (FAR, (2, 3))):
        n = jnp.int32(0)
        for i in range(N_Q):
            has = [jnp.int32(0), jnp.int32(0)]
            for k in range(2):
                for a in range(N_QUAD):
                    here = (plan[TABLE + i * T_ROW + a] == quads[k]) & (
                        a < plan[TABLE + i * T_ROW + T_COUNT]
                    )
                    has[k] = has[k] | jnp.where(here, 1, 0)
            found[2 * i] = has[0]
            found[2 * i + 1] = has[1]
            plan[base + 2 + n] = quads[0] * N_Q + i
            plan[base + 3 + n] = quads[1] * N_Q + i
            n += 2 * (has[0] & has[1])
        plan[base] = n // 2
        for i in range(N_Q):
            plan[base + 2 + n] = (quads[0] + found[2 * i + 1]) * N_Q + i
            n += found[2 * i] ^ found[2 * i + 1]
        plan[base + 1] = n


def run_plan(ids, mask):
    return pl.pallas_call(
        plan_kernel,
        out_shape=struct((PLAN,), jnp.int32),
        in_specs=[SM, HBM],
        out_specs=SM,
        scratch_shapes=[
            pltpu.SMEM((BLK, BLK), jnp.int32),
            pltpu.SMEM((32,), jnp.int32),
            pltpu.SemaphoreType.DMA(()),
        ],
        compiler_params=pltpu.CompilerParams(vmem_limit_bytes=4 * MIB),
    )(ids, mask)


def queries_of(near, far, i):
    at = (i % 4) * ROWS
    return (near, far)[i // 4][at : at + BLK]


def grads_of(near, far, i):
    at = (i % 4) * ROWS + BLK
    return (near, far)[i // 4][at : at + D_ROWS]


def fill_quads(kvs, cols, buf):
    for quad in range(N_QUAD):
        for odd in range(2):
            at = slice((quad % 2) * WIDE, (quad % 2 + 1) * WIDE)
            buf[quad, odd * WIDE : (odd + 1) * WIDE] = kvs[2 * (quad // 2) + odd][at, cols]


def join(parts, axis=0):
    return parts[0] if len(parts) == 1 else jnp.concatenate(parts, axis=axis)


def heads(ref, i):
    return jnp.concatenate([ref[i, :BLK, h * HD : (h + 1) * HD] for h in range(HEADS)], axis=0)


E_SLOTS = 8


def scores_kernel(half, *refs):
    plan, q_in, kv0, kv1, kv2, kv3 = refs[:6]
    if half == 0:
        e_hbm, st, qs, ks, sc, ebuf, mx, lacc, count, e_sem = refs[6:]
    else:
        _, st_in, e_hbm, stats_hbm, qs, ks, sc, ebuf, mx, lacc, count, e_sem, st, st_sem = refs[6:]
        st[...] = st_in[...]
    count[0] = 0
    fill_quads((kv0, kv1, kv2, kv3), slice(0, HD), ks)
    for i in range(N_Q // 2):
        qs[i] = queries_of(q_in, q_in, i)
    diff = (
        lax.broadcasted_iota(jnp.int32, (BLK, WIDE), 1) % BLK
        - lax.broadcasted_iota(jnp.int32, (BLK, WIDE), 0)
    )

    def out_copy(slot, unit):
        return pltpu.make_async_copy(ebuf.at[slot], e_hbm.at[unit], e_sem.at[slot])

    def query_block(row, carry):
        i = half * (N_Q // 2) + row
        base = TABLE + i * T_ROW
        active = plan[base + T_COUNT]
        mx[...] = jnp.full(mx.shape, NEGATIVE, F32)
        lacc[...] = jnp.zeros(lacc.shape, F32)

        def score_quads(quads):
            limits = [plan[LIMITS + i * N_K + 4 * quad + a] for quad in quads for a in range(4)]
            joined = dot(join([ks[quad] for quad in quads]), heads(qs, row), NT)
            for hp in range(2):
                cols = slice(hp * WIDE, (hp + 1) * WIDE)
                best = mx[:, cols]
                for k, quad in enumerate(quads):
                    for a in range(4):
                        at = slice(a * BLK, (a + 1) * BLK)
                        s = joined[k * QUAD + a * BLK : k * QUAD + (a + 1) * BLK, cols]
                        part = jnp.where(diff >= limits[4 * k + a], s, NEGATIVE)
                        sc[quad, at, cols] = part
                        best = jnp.maximum(
                            best, jnp.max(part.reshape(BLK // 8, 8, WIDE), axis=0)
                        )
                mx[:, cols] = best

        def score_pair(n, carry):
            score_quads([plan[base + 2 * n], plan[base + 2 * n + 1]])
            return carry

        lax.fori_loop(0, active // 2, score_pair, 0)

        @pl.when(active % 2 == 1)
        def _():
            score_quads([plan[base + active - 1]])

        m = jnp.maximum(jnp.max(mx[...], axis=0, keepdims=True), FLOOR)

        def exp_quad(k, carry):
            quad = plan[base + k]
            n = count[0]
            slot = n % E_SLOTS

            @pl.when(n >= E_SLOTS)
            def _():
                out_copy(slot, 0).wait()

            for hp in range(2):
                cols = slice(hp * WIDE, (hp + 1) * WIDE)
                e = jnp.exp2((sc[quad, :, cols] - m[:, cols]) * EXP_SCALE)
                lacc[:, cols] += jnp.sum(e.reshape(QUAD // 8, 8, WIDE), axis=0)
                ebuf[slot, :, cols] = e.astype(BF16)
            out_copy(slot, quad * N_Q + i).start()
            count[0] = n + 1
            return carry

        lax.fori_loop(0, active, exp_quad, 0)
        g = plan[AT_G + i]
        st[pl.ds(g, 1), :] = m
        st[pl.ds(N_Q + g, 1), :] = jnp.sum(lacc[...], axis=0, keepdims=True)
        return carry

    lax.fori_loop(0, N_Q // 2, query_block, 0)

    if half == 1:
        st_copies = copy_all([(st, stats_hbm.at[g]) for g in range(N_Q)], st_sem)
        for c in st_copies:
            c.start()
        for c in st_copies:
            c.wait()
    for slot_no in range(E_SLOTS):

        @pl.when(count[0] > slot_no)
        def _():
            out_copy(slot_no, 0).wait()


def run_scores(half, plan, queries, kvs, before=()):
    stats_shape = (2 * N_Q, COLS)
    return pl.pallas_call(
        functools.partial(scores_kernel, half),
        out_shape=[
            pltpu.HBM((N_QUAD * N_Q, QUAD, COLS), BF16),
            pltpu.HBM((N_Q, *stats_shape), F32) if half else struct(stats_shape, F32),
        ],
        in_specs=[SM] + [VM] * 5 + ([HBM, VM] if half else []),
        out_specs=[HBM, HBM if half else VM],
        scratch_shapes=[
            pltpu.VMEM((N_Q // 2, BLK, COLS), BF16),
            pltpu.VMEM((N_QUAD, QUAD, HD), BF16),
            pltpu.VMEM((N_QUAD, QUAD, COLS), F32),
            pltpu.VMEM((E_SLOTS, QUAD, COLS), BF16),
            pltpu.VMEM((8, COLS), F32),
            pltpu.VMEM((8, COLS), F32),
            pltpu.SMEM((1,), jnp.int32),
            pltpu.SemaphoreType.DMA((E_SLOTS,)),
        ]
        + ([pltpu.VMEM(stats_shape, F32), pltpu.SemaphoreType.DMA((N_Q,))] if half else []),
        input_output_aliases={6: 0} if half else {},
        compiler_params=pltpu.CompilerParams(vmem_limit_bytes=20 * MIB),
    )(plan, queries, *kvs, *before)


DEPTH, AHEAD = 8, 6


def loop_units(plan, base, visit):
    pairs, total = plan[base], plan[base + 1]
    singles = total - 2 * pairs

    def pair(n, carry):
        visit([(2 * n, 2)])
        return carry

    def two_singles(n, carry):
        first = 2 * (pairs + n)
        visit([(first, 1), (first + 1, 1)])
        return carry

    lax.fori_loop(0, pairs, pair, 0)
    lax.fori_loop(0, singles // 2, two_singles, 0)

    @pl.when(singles % 2 == 1)
    def _():
        visit([(total - 1, 1)])


def prefetch(plan, base, copies, first, number):
    total = plan[base + 1]
    for k in range(number):

        @pl.when(first + k + AHEAD < total)
        def _():
            for c in copies(first + k + AHEAD):
                c.start()

    for k in range(number):
        for c in copies(first + k):
            c.wait()


def start_first(plan, base, copies):
    for n in range(AHEAD):

        @pl.when(n < plan[base + 1])
        def _():
            for c in copies(n):
                c.start()


def parts_kernel(
    plan, near, far, kv0, kv1, kv2, kv3, e_hbm,
    u_hbm, dq_hbm,
    ds, ks, vs, kts, ebuf, ubuf, dqs, dq_low, e_sem, u_sem, dq_sem,
):
    def in_copies(n):
        unit, at = plan[ALL + 2 + n], n % DEPTH
        return (pltpu.make_async_copy(e_hbm.at[unit], ebuf.at[at], e_sem.at[at]),)

    def out_copy(n, unit):
        at = n % DEPTH
        return pltpu.make_async_copy(ubuf.at[at], u_hbm.at[unit], u_sem.at[at])

    start_first(plan, ALL, in_copies)
    kvs = (kv0, kv1, kv2, kv3)
    fill_quads(kvs, slice(0, HD), ks)
    fill_quads(kvs, slice(HD, 2 * HD), vs)
    for i in range(N_Q):
        ds[i] = grads_of(near, far, i)
    dqs[...] = jnp.zeros(dqs.shape, F32)
    for quad in range(N_QUAD):
        kts[quad] = ks[quad].T

    def visit(groups):
        first, number = groups[0][0], sum(g[1] for g in groups)
        for k in range(number):

            @pl.when(first + k >= DEPTH)
            def _():
                out_copy(first + k, 0).wait()

        prefetch(plan, ALL, in_copies, first, number)
        done = []
        for start, size in groups:
            units = [plan[ALL + 2 + start + k] for k in range(size)]
            i, quads = units[0] % N_Q, [unit // N_Q for unit in units]
            extra = ds[i, BLK:, :].astype(F32)
            delta = extra[0:1] + extra[1:2] + extra[2:3]
            da = dot(join([vs[quad] for quad in quads]), heads(ds, i), NT)
            us = []
            for k in range(size):
                at = (start + k) % DEPTH
                u = (ebuf[at].astype(F32) * (da[k * QUAD : (k + 1) * QUAD] - delta)).astype(BF16)
                ubuf[at] = u
                us.append(u)
            done.append((i, dot(join([kts[quad] for quad in quads], axis=1), join(us), NN)))
            for k in range(size):
                out_copy(start + k, units[k]).start()
        for i, part in done:
            dqs[i] += part

    loop_units(plan, ALL, visit)
    dq_copies = copy_all([(dq_low.at[i], dq_hbm.at[plan[AT_G + i]]) for i in range(N_Q)], dq_sem)
    for i in range(N_Q):
        dq_low[i] = dqs[i].astype(BF16)
        dq_copies[i].start()
    for c in dq_copies:
        c.wait()
    for n in range(DEPTH):

        @pl.when(n < plan[ALL + 1])
        def _():
            out_copy(n, 0).wait()


def run_parts(plan, near, far, kvs, e):
    dma = pltpu.SemaphoreType.DMA
    return pl.pallas_call(
        parts_kernel,
        out_shape=[
            pltpu.HBM((N_QUAD * N_Q, QUAD, COLS), BF16),
            pltpu.HBM((N_Q, HD, COLS), BF16),
        ],
        in_specs=[SM] + [VM] * 6 + [HBM],
        out_specs=[HBM, HBM],
        scratch_shapes=[
            pltpu.VMEM((N_Q, D_ROWS, COLS), BF16),
            pltpu.VMEM((N_QUAD, QUAD, HD), BF16),
            pltpu.VMEM((N_QUAD, QUAD, HD), BF16),
            pltpu.VMEM((N_QUAD, HD, QUAD), BF16),
            pltpu.VMEM((DEPTH, QUAD, COLS), BF16),
            pltpu.VMEM((DEPTH, QUAD, COLS), BF16),
            pltpu.VMEM((N_Q, HD, COLS), F32),
            pltpu.VMEM((N_Q, HD, COLS), BF16),
            dma((DEPTH,)),
            dma((DEPTH,)),
            dma((N_Q,)),
        ],
        compiler_params=pltpu.CompilerParams(vmem_limit_bytes=28 * MIB),
    )(plan, near, far, *kvs, e)


def row_weights(plan, stats, near, far, ws, wq, wdo):
    ms = [stats[j, :N_Q, :] for j in range(N_Q)]
    top = functools.reduce(jnp.maximum, ms)
    tot = sum(stats[j, N_Q:, :] * jnp.exp2((ms[j] - top) * EXP_SCALE) for j in range(N_Q))
    ws[...] = jnp.exp2((stats[plan[AT_OWN], :N_Q, :] - top) * EXP_SCALE) / tot
    rows = []
    for i in range(N_Q):
        w = ws[pl.ds(plan[AT_G + i], 1), :]
        rows += [w[:, h * BLK : (h + 1) * BLK] for h in range(HEADS)]
    rows.append(jnp.zeros((BLK - len(rows), BLK), F32))
    cols = jnp.concatenate(rows, axis=0).T
    for i in range(N_Q):
        q = queries_of(near, far, i)
        do = grads_of(near, far, i)
        for h in range(HEADS):
            w = cols[:, i * HEADS + h : i * HEADS + h + 1]
            at = slice(h * BLK, (h + 1) * BLK)
            c = slice(h * HD, (h + 1) * HD)
            wq[i, at, :] = (q[:, c].astype(F32) * w).astype(BF16)
            wdo[i, at, :] = (do[:BLK, c].astype(F32) * w).astype(BF16)


def sum_keys(plan, base, first_quad, rows, wq, wdo, e_hbm, u_hbm, acc, bufs):
    ebuf, ubuf, e_sem, u_sem = bufs
    size = acc.shape[1]

    def in_copies(n):
        unit, at = plan[base + 2 + n], n % DEPTH
        return [
            pltpu.make_async_copy(
                hbm.at[unit, pl.ds(rows, size)], buf.at[at, pl.ds(0, size)], sem.at[at]
            )
            for hbm, buf, sem in ((e_hbm, ebuf, e_sem), (u_hbm, ubuf, u_sem))
        ]

    start_first(plan, base, in_copies)
    acc[...] = jnp.zeros(acc.shape, F32)

    def visit(groups):
        prefetch(plan, base, in_copies, groups[0][0], sum(g[1] for g in groups))
        done = []
        for first, number in groups:
            unit = plan[base + 2 + first]
            i, quad = unit % N_Q, unit // N_Q - first_quad
            for buf, w, cols in ((ubuf, wq, slice(0, HD)), (ebuf, wdo, slice(HD, 2 * HD))):
                rows_of = [buf[(first + k) % DEPTH, :size] for k in range(number)]
                done.append((quad, number, cols, dot(join(rows_of), w[i], NN)))
        for quad, number, cols, part in done:
            for k in range(number):
                acc[quad + k, :, cols] += part[k * size : (k + 1) * size]

    return lambda: loop_units(plan, base, visit)


def far_kernel(
    plan, stats, near, far, e_hbm, u_hbm,
    out1, out2, out3, wq_hbm, wdo_hbm,
    ws, wq, wdo, acc, acc_odd, w_sem, *bufs,
):
    w_copies = copy_all([(wq, wq_hbm), (wdo, wdo_hbm)], w_sem)

    sum_far = sum_keys(plan, FAR, 2, 0, wq, wdo, e_hbm, u_hbm, acc, bufs[:4])
    sum_odd = sum_keys(plan, NEAR, 0, WIDE, wq, wdo, e_hbm, u_hbm, acc_odd, bufs[4:])
    row_weights(plan, stats, near, far, ws, wq, wdo)
    for c in w_copies:
        c.start()
    sum_far()
    sum_odd()
    for quad in range(2):
        at = slice(quad * WIDE, (quad + 1) * WIDE)
        out1[at, :] = acc_odd[quad].astype(BF16)
        out2[at, :] = acc[quad, :WIDE].astype(BF16)
        out3[at, :] = acc[quad, WIDE:].astype(BF16)
    for c in w_copies:
        c.wait()


def own_kernel(plan, wq_hbm, wdo_hbm, e_hbm, u_hbm, out, wq, wdo, acc, w_sem, *bufs):
    w_copies = copy_all([(wq_hbm, wq), (wdo_hbm, wdo)], w_sem)
    for c in w_copies:
        c.start()

    sum_own = sum_keys(plan, NEAR, 0, 0, wq, wdo, e_hbm, u_hbm, acc, bufs)
    for c in w_copies:
        c.wait()
    sum_own()
    for quad in range(2):
        out[quad * WIDE : (quad + 1) * WIDE, :] = acc[quad]


def keys_bufs(rows):
    return [
        pltpu.VMEM((DEPTH, rows, COLS), BF16),
        pltpu.VMEM((DEPTH, rows, COLS), BF16),
        pltpu.SemaphoreType.DMA((DEPTH,)),
        pltpu.SemaphoreType.DMA((DEPTH,)),
    ]


def run_far(plan, stats, near, far, e, u):
    return pl.pallas_call(
        far_kernel,
        out_shape=[struct((QUAD, 2 * HD), BF16)] * 3 + [pltpu.HBM((N_Q, COLS, HD), BF16)] * 2,
        in_specs=[SM] + [VM] * 3 + [HBM, HBM],
        out_specs=[VM] * 3 + [HBM] * 2,
        scratch_shapes=[
            pltpu.VMEM((N_Q, COLS), F32),
            pltpu.VMEM((N_Q, COLS, HD), BF16),
            pltpu.VMEM((N_Q, COLS, HD), BF16),
            pltpu.VMEM((2, QUAD, 2 * HD), F32),
            pltpu.VMEM((2, WIDE, 2 * HD), F32),
            pltpu.SemaphoreType.DMA((2,)),
        ]
        + keys_bufs(QUAD)
        + keys_bufs(WIDE),
        compiler_params=pltpu.CompilerParams(vmem_limit_bytes=24 * MIB),
    )(plan, stats, near, far, e, u)


def run_own(plan, wq, wdo, e, u):
    return pl.pallas_call(
        own_kernel,
        out_shape=struct((QUAD, 2 * HD), F32),
        in_specs=[SM] + [HBM] * 4,
        out_specs=VM,
        scratch_shapes=[
            pltpu.VMEM((N_Q, COLS, HD), BF16),
            pltpu.VMEM((N_Q, COLS, HD), BF16),
            pltpu.VMEM((2, WIDE, 2 * HD), F32),
            pltpu.SemaphoreType.DMA((2,)),
        ]
        + keys_bufs(WIDE),
        compiler_params=pltpu.CompilerParams(vmem_limit_bytes=14 * MIB),
    )(plan, wq, wdo, e, u)


def sum_kernel(own, a, b, c, out0, out1, out2, out3):
    for d, out in enumerate((out0, out1, out2, out3)):
        at = slice(d * BLK, (d + 1) * BLK)
        total = own[at] + a[at].astype(F32) + b[at].astype(F32) + c[at].astype(F32)
        out[...] = total.astype(out.dtype)


def run_sum(own, a, b, c):
    return pl.pallas_call(
        sum_kernel,
        out_shape=[struct((BLK, 2 * HD), F32)] + [struct((BLK, 2 * HD), BF16)] * 3,
        in_specs=[VM] * 4,
        out_specs=[VM] * 4,
        compiler_params=pltpu.CompilerParams(vmem_limit_bytes=6 * MIB),
    )(own, a, b, c)


def queries_kernel(plan, parts, stats, out):
    own = plan[AT_OWN]
    ms = [stats[j, pl.ds(own, 1), :] for j in range(N_Q)]
    ls = [stats[j, pl.ds(N_Q + own, 1), :] for j in range(N_Q)]
    top = functools.reduce(jnp.maximum, ms)
    es = [jnp.exp2((m - top) * EXP_SCALE) for m in ms]
    tot = sum(l * e for l, e in zip(ls, es))
    for h in range(HEADS):
        at = slice(h * HD, (h + 1) * HD)
        total = sum(parts[j, :, at].astype(F32) * es[j][:, at] for j in range(N_Q))
        out[:, at] = (total * (SCALING / tot[:, at])).T


def run_queries(plan, parts, stats):
    return pl.pallas_call(
        queries_kernel,
        out_shape=struct((BLK, COLS), F32),
        in_specs=[SM, VM, VM],
        out_specs=VM,
        compiler_params=pltpu.CompilerParams(vmem_limit_bytes=6 * MIB),
    )(plan, parts, stats)


def exchange(x, dx=0, dz=0, dy=0, dc=0):
    perm = []
    for b in range(16):
        for r in range(16):
            px = (b // 8) * 2 + (r // 2) % 2
            pz, py, pc = b % 8, r // 4, r % 2
            px, pz, py, pc = px ^ dx, pz ^ (2 * dz), py ^ dy, pc ^ dc
            other = (px // 2) * 8 + pz, py * 4 + (px % 2) * 2 + pc
            perm.append((b * 16 + r, other[0] * 16 + other[1]))
    return lax.ppermute(x, ("blk", "rows"), perm)


Q_GROUPS = [[r for r in range(16) if (r // 2) % 2 == lo] for lo in range(2)]


def to_group(x):
    return lax.all_to_all(x, "rows", 0, 0, axis_index_groups=Q_GROUPS, tiled=True)


def per_device(queries, keys, values, forward_out, grad_out, block_mask):
    b, r = lax.axis_index("blk"), lax.axis_index("rows")
    ids = jnp.stack([b, r]).astype(jnp.int32)

    kv = pack_keys(keys, values)
    kv, queries = lax.optimization_barrier((kv, queries))
    qdo = pack_queries(queries, grad_out, forward_out)

    kv_z = jnp.concatenate([kv] + [exchange(kv, dz=d) for d in (1, 2, 3)], axis=0)
    kvs = [kv_z] + [exchange(kv_z, dx=d) for d in (1, 2, 3)]
    y1, y2, y3 = [exchange(qdo, dy=d) for d in (1, 2, 3)]
    near = jnp.concatenate([y2, qdo, y1, y3], axis=0)
    ids, _ = lax.optimization_barrier((ids, y3))
    plan = run_plan(ids, pltpu.with_memory_space_constraint(block_mask, pltpu.HBM))
    near, k1, k3, k2, plan = lax.optimization_barrier((near, kvs[1], kvs[3], kvs[2], plan))
    kvs = [kv_z, k1, k2, k3]
    far = exchange(near, dc=1)

    e, totals = run_scores(0, plan, near, kvs)
    e = pltpu.with_memory_space_constraint(e, pltpu.HBM)
    e, stat = run_scores(1, plan, far, kvs, (e, totals))
    e = pltpu.with_memory_space_constraint(e, pltpu.HBM)
    stats = to_group(stat)
    u, dq = run_parts(plan, near, far, kvs, e)
    u = pltpu.with_memory_space_constraint(u, pltpu.HBM)
    *remote, wq, wdo = run_far(plan, stats, near, far, e, u)
    wq, wdo = [pltpu.with_memory_space_constraint(w, pltpu.HBM) for w in (wq, wdo)]
    got = [exchange(remote[d - 1], dx=d) for d in (2, 1, 3)]
    dq, _ = lax.optimization_barrier((dq, remote[0]))
    dq_parts = to_group(dq)
    own = run_own(plan, wq, wdo, e, u)
    mine, *rest = run_sum(own, *got)
    back = [exchange(rest[d - 1], dz=d) for d in (2, 1, 3)]
    grad_queries = run_queries(plan, dq_parts, stats)
    total = mine + sum(part.astype(F32) for part in back)
    return grad_queries, total[:, :HD] * SCALING, total[:, HD:]


def solution(mesh):
    spec = P(("blk", "rows"), None)
    return jax.shard_map(
        per_device,
        mesh=mesh,
        in_specs=(spec, spec, spec, spec, spec, P()),
        out_specs=(spec, spec, spec),
        check_vma=False,
    )
```
